32 devices in a mesh: rows: 8 (over y, x, core), batch: 4 (over z).
Axes of the slice: x: 2, y: 2, z: 4, core: 2. Of those that a mesh axis runs over, the one named last changes fastest.
Arguments:
- section_four: bfloat16 [8, 64, 128, 1024], P('batch', 'rows'), may hold values from -6 to 6
- section_five: bfloat16 [8, 32, 64, 2048], P('batch', 'rows'), may hold values from -6 to 6
- target_four: float32 [8, 64, 128, 12], P('batch', 'rows'), may hold values from -6 to 6
- target_five: float32 [8, 32, 64, 12], P('batch', 'rows'), may hold values from -6 to 6
- target_six: float32 [8, 16, 32, 12], P('batch', 'rows'), may hold values from -6 to 6
- anchor_four: int32 [8, 64, 128, 3], P('batch', 'rows'), may hold values from 0 to 1, as said below
- anchor_five: int32 [8, 32, 64, 3], P('batch', 'rows'), may hold values from 0 to 1, as said below
- anchor_six: int32 [8, 16, 32, 3], P('batch', 'rows'), may hold values from 0 to 1, as said below
- lateral_four: float32 [1024, 256], P(('rows', 'batch')), may hold values from -0.1875 to 0.1875
- lateral_five: float32 [2048, 256], P(('rows', 'batch')), may hold values from -0.125 to 0.125
- output_conv: float32 [2, 2304, 256], P(None, ('rows', 'batch')), may hold values from -0.125 to 0.125
- delta_head: float32 [2304, 12], P(('rows', 'batch')), may hold values from -0.125 to 0.125
- mean_four: float32 [1024, 256], P(('rows', 'batch')), may hold values from -0.00390625 to 0.00390625
- mean_five: float32 [2048, 256], P(('rows', 'batch')), may hold values from -0.00390625 to 0.00390625
- mean_conv: float32 [2, 2304, 256], P(None, ('rows', 'batch')), may hold values from -0.00390625 to 0.00390625
- mean_head: float32 [2304, 12], P(('rows', 'batch')), may hold values from -0.02734375 to 0.02734375
- square_four: float32 [1024, 256], P(('rows', 'batch')), may hold values from 7.6293944e-08 to 3.0517577e-07
- square_five: float32 [2048, 256], P(('rows', 'batch')), may hold values from 7.6293944e-08 to 3.0517577e-07
- square_conv: float32 [2, 2304, 256], P(None, ('rows', 'batch')), may hold values from 7.6293944e-08 to 3.0517577e-07
- square_head: float32 [2304, 12], P(('rows', 'batch')), may hold values from 3.0517579e-06 to 1.2207031e-05
Outputs:
- loss_sum: float32 [], replicated
- positives: float32 [], replicated
- first_four: float32 [1024, 256], P(('rows', 'batch'))
- first_five: float32 [2048, 256], P(('rows', 'batch'))
- first_conv: float32 [2, 2304, 256], P(None, ('rows', 'batch'))
- first_head: float32 [2304, 12], P(('rows', 'batch'))
- second_four: float32 [1024, 256], P(('rows', 'batch'))
- second_five: float32 [2048, 256], P(('rows', 'batch'))
- second_conv: float32 [2, 2304, 256], P(None, ('rows', 'batch'))
- second_head: float32 [2304, 12], P(('rows', 'batch'))
- weight_four: float32 [1024, 256], P(('rows', 'batch'))
- weight_five: float32 [2048, 256], P(('rows', 'batch'))
- weight_conv: float32 [2, 2304, 256], P(None, ('rows', 'batch'))
- weight_head: float32 [2304, 12], P(('rows', 'batch'))
The draws below stay inside these ranges and needn't reach their ends.
Inputs may be any that keep to these rules, and one draw needn't show every extreme that they name: `anchor_four`: 1 marks a positive anchor. `anchor_five`: 1 marks a positive anchor. `anchor_six`: 1 marks a positive anchor.
All inputs are finite; a program needn't handle non-finite values.
Results may differ from the reference program's by a relative error of at most 0.012.
The reference program's roundings to bfloat16 on the way count: a program that leaves them out, or rounds other values in their place, can miss the bound.
Values may be sent and summed in bfloat16 or wider, within the bound.
No kernel may reach another device: no remote copies, remote signals or barrier semaphores. Data moves between devices by JAX's collectives and lax.ppermute only.
A program may use at most 128 MiB of HBM per device.

```python
import jax
import jax.numpy as jnp
from jax import lax

F = 256
C4 = 1024
C5 = 2048
A4 = 12
STEP = 5
CROP_DEV = 2
W5 = 64
W4 = 128
W6 = 32
CROPS = 8
H4 = 64
H5 = 32
H6 = 16
N_BATCH = 4


def anchor_draw(key, height, extent):
    row_index = jnp.arange(height, dtype=jnp.int32)[None, :, None, None]
    crop_index = jnp.arange(CROPS, dtype=jnp.int32)[:, None, None, None]
    floor_share = 10 + 20 * row_index // height
    limit_share = floor_share + floor_share * crop_index // CROPS
    rolled = jax.random.randint(key, (CROPS, height, extent, 3), 0, 100)
    return (rolled < limit_share).astype(jnp.int32)


def draw_anchor_four(key, part):
    key = jax.random.fold_in(key, 11)
    return anchor_draw(key, H4, W4)


def draw_anchor_five(key, part):
    key = jax.random.fold_in(key, 12)
    return anchor_draw(key, H5, W5)


def draw_anchor_six(key, part):
    key = jax.random.fold_in(key, 13)
    return anchor_draw(key, H6, W6)


def level_of(key, dims, cuts, smallest, top_value):
    level = 1.0
    for position, parts in cuts:
        steps = jax.random.uniform(jax.random.fold_in(jax.random.fold_in(key, 6), position), (parts,), jnp.float32, smallest / len(cuts), top_value / len(cuts))
        level = level * jnp.repeat(jnp.exp(steps), dims[position] // parts).reshape((-1,) + (1,) * (len(dims) - 1 - position))
    return level


def centred(stream_key, shape, width, limit, cuts=(), held_as=jnp.bfloat16):
    array = jax.random.normal(stream_key, shape, jnp.float32) * width
    if len(cuts) > 0:
        array = level_of(stream_key, shape, cuts, -0.22, 0.18) * array
    return jnp.clip(array, min=-limit, max=limit).astype(held_as)


def setup_inputs(seed: int = 0) -> dict:
    splits = jax.random.split(jax.random.key(seed), 21)
    section_four = centred(splits[0], (CROPS, H4, W4, C4), 1.0, 6.0, ((0, 4), (1, 8)))
    section_five = centred(splits[1], (CROPS, H5, W5, C5), 1.0, 6.0, ((0, 4), (1, 8)))
    target_four = centred(splits[2], (CROPS, H4, W4, A4), 1.0, 6.0, ((0, 4), (1, 8)), jnp.float32)
    target_five = centred(splits[3], (CROPS, H5, W5, A4), 1.0, 6.0, ((0, 4), (1, 8)), jnp.float32)
    target_six = centred(splits[4], (CROPS, H6, W6, A4), 1.0, 6.0, ((0, 4), (1, 8)), jnp.float32)
    anchor_four = draw_anchor_four(jax.random.fold_in(splits[20], 71), 0)
    anchor_five = draw_anchor_five(jax.random.fold_in(splits[20], 71), 0)
    anchor_six = draw_anchor_six(jax.random.fold_in(splits[20], 71), 0)
    lateral_four = centred(splits[8], (C4, F), C4 ** -0.5, 0.1875, ((0, 32),), jnp.float32)
    lateral_five = centred(splits[9], (C5, F), C5 ** -0.5, 0.125, ((0, 32),), jnp.float32)
    output_conv = centred(splits[10], (2, 9 * F, F), (9 * F) ** -0.5, 0.125, ((1, 32),), jnp.float32)
    delta_head = centred(splits[11], (9 * F, A4), (9 * F) ** -0.5, 0.125, ((0, 32),), jnp.float32)
    mean_four = centred(splits[12], (C4, F), (0.07 * (CROPS * H4 * W4) ** -0.5), 0.00390625, ((0, 32),), jnp.float32)
    mean_five = centred(splits[13], (C5, F), (0.07 * (CROPS * H4 * W4) ** -0.5), 0.00390625, ((0, 32),), jnp.float32)
    mean_conv = centred(splits[14], (2, 9 * F, F), (0.07 * (CROPS * H4 * W4) ** -0.5), 0.00390625, ((1, 32),), jnp.float32)
    mean_head = centred(splits[15], (9 * F, A4), (0.45 * (CROPS * H4 * W4) ** -0.5), 0.02734375, ((0, 32),), jnp.float32)
    square_four = jnp.clip(7.629394360719743e-08 + 2.288818308215923e-07 * jax.random.uniform(splits[16], (C4, F), jnp.float32) ** level_of(splits[16], (C4, F), ((0, 32),), -0.2, 0.2), 7.629394360719743e-08, 3.0517577442878974e-07)
    square_five = jnp.clip(7.629394360719743e-08 + 2.288818308215923e-07 * jax.random.uniform(splits[17], (C5, F), jnp.float32) ** level_of(splits[17], (C5, F), ((0, 32),), -0.2, 0.2), 7.629394360719743e-08, 3.0517577442878974e-07)
    square_conv = jnp.clip(7.629394360719743e-08 + 2.288818308215923e-07 * jax.random.uniform(splits[18], (2, 9 * F, F), jnp.float32) ** level_of(splits[18], (2, 9 * F, F), ((1, 32),), -0.2, 0.2), 7.629394360719743e-08, 3.0517577442878974e-07)
    square_head = jnp.clip(3.051757857974735e-06 + 9.155273573924205e-06 * jax.random.uniform(splits[19], (9 * F, A4), jnp.float32) ** level_of(splits[19], (9 * F, A4), ((0, 32),), -0.2, 0.2), 3.051757857974735e-06, 1.220703143189894e-05)
    return {"section_four": section_four, "section_five": section_five, "target_four": target_four, "target_five": target_five, "target_six": target_six, "anchor_four": anchor_four, "anchor_five": anchor_five, "anchor_six": anchor_six, "lateral_four": lateral_four, "lateral_five": lateral_five, "output_conv": output_conv, "delta_head": delta_head, "mean_four": mean_four, "mean_five": mean_five, "mean_conv": mean_conv, "mean_head": mean_head, "square_four": square_four, "square_five": square_five, "square_conv": square_conv, "square_head": square_head}


@jax.custom_vjp
def low(v):
    return lax.optimization_barrier(v.astype(jnp.bfloat16)).astype(jnp.float32)

@jax.custom_vjp
def low_back(v):
    return v

def low_keep(v):
    return (low(v), None)

def low_pass(kept, grad):
    return (grad,)

def back_keep(v):
    return (v, None)

def back_low(kept, grad):
    return (low(grad),)
low.defvjp(low_keep, low_pass)
low_back.defvjp(back_keep, back_low)
box_beta = 1.0 / 9.0
beta_one = 0.5
beta_two = 0.5
learn_rate = 0.02
weight_decay = 0.01
epsilon = 1e-08

def conv_three(field, kernel):
    shaped = kernel.reshape(3, 3, field.shape[-1], kernel.shape[-1])
    return lax.conv_general_dilated(field, shaped, (1, 1), ((1, 1), (1, 1)), dimension_numbers=('NHWC', 'HWIO', 'NHWC'), precision=lax.Precision.HIGHEST)

def spread_up(field):
    return jnp.repeat(jnp.repeat(field, 2, axis=1), 2, axis=2)

def pooled(field):
    count_b, height, extent, channels = field.shape
    return lax.optimization_barrier(jnp.mean(field.reshape(count_b, height // 2, 2, extent // 2, 2, channels), axis=(2, 4)))

def smooth_box(mismatch):
    magnitude = jnp.abs(mismatch)
    return jnp.where(magnitude < box_beta, 0.5 * mismatch * mismatch / box_beta, magnitude - 0.5 * box_beta)

def group_loss(params, section_four, section_five, target_four, target_five, target_six, mask_four, mask_five, mask_six):
    copy_four, copy_five, copy_conv, copy_head = [low(weight) for weight in params]
    lat_five = low_back(jnp.einsum('bhwc,co->bhwo', section_five, copy_five, precision=lax.Precision.HIGHEST))
    lat_four = low_back(jnp.einsum('bhwc,co->bhwo', section_four, copy_four, precision=lax.Precision.HIGHEST))
    input_four = low(lat_four + spread_up(lat_five))
    input_five = low(lat_five)
    level_four = low_back(conv_three(input_four, copy_conv[0]))
    level_five = low_back(conv_three(input_five, copy_conv[1]))
    level_six = pooled(level_five)
    summed = jnp.zeros((), jnp.float32)
    for level, target, mask in ((level_four, target_four, mask_four), (level_five, target_five, mask_five), (level_six, target_six, mask_six)):
        delta = low_back(conv_three(low(level), copy_head))
        summed = summed + jnp.sum(jnp.repeat(mask, 4, axis=3) * smooth_box(delta - target))
    return summed

def reference(section_four, section_five, target_four, target_five, target_six, anchor_four, anchor_five, anchor_six, lateral_four, lateral_five, output_conv, delta_head, mean_four, mean_five, mean_conv, mean_head, square_four, square_five, square_conv, square_head):
    masks = [anchor.astype(jnp.float32) for anchor in (anchor_four, anchor_five, anchor_six)]
    positives = jnp.sum(masks[0]) + jnp.sum(masks[1]) + jnp.sum(masks[2])
    inverse = 1.0 / jnp.maximum(positives, 1.0)
    params = (lateral_four, lateral_five, output_conv, delta_head)

    def split(field):
        return field.reshape((N_BATCH, CROP_DEV) + field.shape[1:])
    stacked = tuple((split(field) for field in (section_four.astype(jnp.float32), section_five.astype(jnp.float32), target_four, target_five, target_six, masks[0], masks[1], masks[2])))

    def one_group(carried, batch_part):
        loss_now, gradients = carried
        result, pullback = jax.vjp(lambda weights: group_loss(weights, *batch_part), params)
        more, = pullback(inverse)
        return ((loss_now + result, tuple((old + new for old, new in zip(gradients, more)))), None)
    start = (jnp.zeros((), jnp.float32), tuple((jnp.zeros_like(weight) for weight in params)))
    (loss_sum, gradients), _ = lax.scan(one_group, start, stacked)
    firsts, seconds, weights = ([], [], [])
    for weight, gradient, mean, square in zip(params, gradients, (mean_four, mean_five, mean_conv, mean_head), (square_four, square_five, square_conv, square_head)):
        first = beta_one * mean + (1.0 - beta_one) * gradient
        second = beta_two * square + (1.0 - beta_two) * gradient * gradient
        corrected_first = first / (1.0 - beta_one ** STEP)
        corrected_second = second / (1.0 - beta_two ** STEP)
        firsts.append(first)
        seconds.append(second)
        weights.append(weight - learn_rate * (corrected_first / (jnp.sqrt(corrected_second) + epsilon) + weight_decay * weight))
    return (loss_sum, positives, firsts[0], firsts[1], firsts[2], firsts[3], seconds[0], seconds[1], seconds[2], seconds[3], weights[0], weights[1], weights[2], weights[3])
```

```python
import jax
import jax.numpy as jnp
from jax import lax
from jax.sharding import PartitionSpec as P

STEP = 5


box_beta = 1.0 / 9.0
beta_one = 0.5
beta_two = 0.5
learn_rate = 0.02
weight_decay = 0.01
epsilon = 1e-08


def with_halo(value, sides, width):
    for axis, dim in sides:
        count, length = (lax.axis_size(axis), value.shape[dim])
        up = [(i, (i + 1) % count) for i in range(count - 1)]
        down = [(j, i) for i, j in up]
        last = lax.slice_in_dim(value, length - width, length, axis=dim)
        first = lax.slice_in_dim(value, 0, width, axis=dim)
        before = lax.ppermute(last, axis, up)
        after = lax.ppermute(first, axis, down)
        value = jnp.concatenate([before, value, after], axis=dim)
    return value


def widened(field):
    return jnp.pad(field, ((0, 0), (0, 0), (1, 1), (0, 0)))


def conv_taps(padded, kernel):
    height = padded.shape[1] - 2
    extent = padded.shape[2]
    channels = padded.shape[3]
    spread = widened(padded)
    summed = jnp.zeros((padded.shape[0], height, extent, kernel.shape[1]), jnp.float32)
    for offset in range(9):
        row_step, col_step = divmod(offset, 3)
        window = spread[:, row_step : row_step + height, col_step : col_step + extent]
        summed = summed + jnp.dot(
            window,
            kernel[offset * channels : (offset + 1) * channels],
            preferred_element_type=jnp.float32,
        )
    return summed


def conv_back(padded_grad, kernel):
    height = padded_grad.shape[1] - 2
    extent = padded_grad.shape[2]
    channels = kernel.shape[0] // 9
    spread = widened(padded_grad)
    summed = jnp.zeros((padded_grad.shape[0], height, extent, channels), jnp.float32)
    for offset in range(9):
        row_step, col_step = divmod(offset, 3)
        window = spread[
            :, 2 - row_step : 2 - row_step + height, 2 - col_step : 2 - col_step + extent
        ]
        summed = summed + jnp.dot(
            window,
            kernel[offset * channels : (offset + 1) * channels].T,
            preferred_element_type=jnp.float32,
        )
    return summed


def weight_grad(padded, gradient):
    height = gradient.shape[1]
    extent = gradient.shape[2]
    spread = widened(padded)
    pieces = []
    for offset in range(9):
        row_step, col_step = divmod(offset, 3)
        window = spread[:, row_step : row_step + height, col_step : col_step + extent]
        pieces.append(
            jnp.einsum("bhwc,bhwo->co", window, gradient, preferred_element_type=jnp.float32)
        )
    return jnp.concatenate(pieces, axis=0)


def rim_forward(field):
    return with_halo(field, (("rows", 1),), 1)


def rim_backward(field):
    return with_halo(field, (("rows", 1),), 1)


def spread_up(field):
    return jnp.repeat(jnp.repeat(field, 2, axis=1), 2, axis=2)


def pooled(field):
    count_b, height, extent, channels = field.shape
    return jnp.mean(field.reshape(count_b, height // 2, 2, extent // 2, 2, channels), axis=(2, 4))


def folded(field):
    count_b, height, extent, channels = field.shape
    return jnp.sum(field.reshape(count_b, height // 2, 2, extent // 2, 2, channels), axis=(2, 4))


def smooth_box(mismatch):
    magnitude = jnp.abs(mismatch)
    return jnp.where(
        magnitude < box_beta, 0.5 * mismatch * mismatch / box_beta, magnitude - 0.5 * box_beta
    )


def adamw_update(weight, gradient, mean, square):
    first = beta_one * mean + (1.0 - beta_one) * gradient
    second = beta_two * square + (1.0 - beta_two) * gradient * gradient
    corrected_first = first / (1.0 - beta_one**STEP)
    corrected_second = second / (1.0 - beta_two**STEP)
    return (
        first,
        second,
        weight
        - learn_rate
        * (corrected_first / (jnp.sqrt(corrected_second) + epsilon) + weight_decay * weight),
    )


def gathered_batch(piece):
    count, me = lax.axis_size("batch"), lax.axis_index("batch")
    held = [piece] + [
        lax.ppermute(piece, "batch", [(i, i ^ k) for i in range(count)]) for k in range(1, count)
    ]
    stacked = jnp.stack(held)
    return [lax.dynamic_index_in_dim(stacked, t ^ me, 0, keepdims=False) for t in range(count)]


def row_groups():
    count = lax.axis_size("rows")
    low = max(count // 4, 1)
    return count, low, count // low


def gathered_rows(piece):
    count, low, high = row_groups()
    held = [piece] + [
        lax.ppermute(piece, "rows", [(i, i ^ (j * low)) for i in range(count)])
        for j in range(1, high)
    ]
    result = [None] * count
    for j in range(high):
        result[j * low] = held[j]
        for k in range(1, low):
            result[j * low + k] = lax.ppermute(
                held[j], "rows", [(i, i ^ k) for i in range(count)]
            )
    return result


def summed_rows(blocks):
    count, low, high = row_groups()
    partial = []
    for j in range(high):
        total = blocks[j * low]
        for k in range(1, low):
            total = total + lax.ppermute(
                blocks[j * low + k].astype(jnp.bfloat16), "rows", [(i, i ^ k) for i in range(count)]
            ).astype(jnp.float32)
        partial.append(total)
    total = partial[0]
    for j in range(1, high):
        total = total + lax.ppermute(
            partial[j].astype(jnp.bfloat16), "rows", [(i, i ^ (j * low)) for i in range(count)]
        ).astype(jnp.float32)
    return total


def summed_batch(blocks):
    count, me = lax.axis_size("batch"), lax.axis_index("batch")
    total = lax.dynamic_index_in_dim(blocks, me, 0, keepdims=False)
    for k in range(1, count):
        sent = lax.dynamic_index_in_dim(blocks, me ^ k, 0, keepdims=False).astype(jnp.bfloat16)
        total = total + lax.ppermute(
            sent, "batch", [(i, i ^ k) for i in range(count)]
        ).astype(jnp.float32)
    return total


def thirds(value):
    high = lax.reduce_precision(value, 8, 7)
    middle = lax.reduce_precision(value - high, 8, 7)
    return high, middle, value - high - middle


def on_device(
    section_four,
    section_five,
    target_four,
    target_five,
    target_six,
    anchor_four,
    anchor_five,
    anchor_six,
    lateral_four,
    lateral_five,
    output_conv,
    delta_head,
    mean_four,
    mean_five,
    mean_conv,
    mean_head,
    square_four,
    square_five,
    square_conv,
    square_head,
):
    n_rows, n_batch = lax.axis_size("rows"), lax.axis_size("batch")
    row_me, batch_me = lax.axis_index("rows"), lax.axis_index("batch")
    anchors = [anchor.astype(jnp.float32) for anchor in (anchor_four, anchor_five, anchor_six)]
    local_count = sum((jnp.sum(anchor) for anchor in anchors))
    four_n, five_n, conv_n = lateral_four.shape[0], lateral_five.shape[0], output_conv.shape[1]
    width, deltas = lateral_four.shape[1], delta_head.shape[1]
    lateral = jnp.concatenate([lateral_four, lateral_five]).astype(jnp.bfloat16)
    parts = gathered_batch(lateral)
    lateral = jnp.concatenate([p[:four_n] for p in parts] + [p[four_n:] for p in parts])
    order = jnp.arange(n_rows) ^ row_me
    laterals = jnp.stack(gathered_rows(lateral))[order]
    full_four = laterals[:, : n_batch * four_n].reshape(-1, width)
    full_five = laterals[:, n_batch * four_n :].reshape(-1, width)
    lane = lax.broadcasted_iota(jnp.int32, (conv_n, 128), 1)
    line = lax.broadcasted_iota(jnp.int32, (conv_n, 128), 0)
    spare = jnp.pad(delta_head, ((0, 0), (0, 128 - deltas)))
    for k, piece in enumerate(thirds(local_count)):
        spare = jnp.where((line == 0) & (lane == deltas + k), piece, spare)
    conv = jnp.concatenate([output_conv[0], output_conv[1], spare], axis=1).astype(jnp.bfloat16)
    conv = jnp.concatenate(gathered_batch(conv))
    convs = jnp.stack(gathered_rows(conv))[order].reshape(-1, 2 * width + 128)
    full_conv = (convs[:, :width], convs[:, width : 2 * width])
    full_head = convs[:, 2 * width : 2 * width + deltas]
    positives = jnp.sum(convs[:, 2 * width + deltas : 2 * width + deltas + 3].astype(jnp.float32))
    lat_five = jnp.dot(section_five, full_five, preferred_element_type=jnp.float32)
    merged = jnp.dot(section_four, full_four, preferred_element_type=jnp.float32) + spread_up(
        lat_five
    )
    input_four = rim_forward(merged.astype(jnp.bfloat16))
    input_five = rim_forward(lat_five.astype(jnp.bfloat16))
    level_four = conv_taps(input_four, full_conv[0])
    level_five = conv_taps(input_five, full_conv[1])
    level_six = pooled(level_five)
    head_inputs = [
        rim_forward(level.astype(jnp.bfloat16)) for level in (level_four, level_five, level_six)
    ]
    masks = [jnp.repeat(anchor, 4, axis=3) for anchor in anchors]
    mismatches = [
        conv_taps(head_in, full_head) - target
        for head_in, target in zip(head_inputs, (target_four, target_five, target_six))
    ]
    local_loss = sum(
        (jnp.sum(mask * smooth_box(mismatch)) for mask, mismatch in zip(masks, mismatches))
    )
    inverse = 1.0 / jnp.maximum(positives, 1.0)
    delta_grads = [
        (mask * jnp.clip(mismatch / box_beta, -1.0, 1.0) * inverse).astype(jnp.bfloat16)
        for mask, mismatch in zip(masks, mismatches)
    ]
    head_grad = jnp.zeros(full_head.shape, jnp.float32)
    for head_in, delta_grad in zip(head_inputs, delta_grads):
        head_grad = head_grad + weight_grad(head_in, delta_grad)
    delta_padded = [rim_backward(delta_grad) for delta_grad in delta_grads]
    level_backs = [conv_back(padded, full_head) for padded in delta_padded]
    grad_four = level_backs[0].astype(jnp.bfloat16)
    grad_five = (level_backs[1] + 0.25 * spread_up(level_backs[2])).astype(jnp.bfloat16)
    conv_grad = [weight_grad(input_four, grad_four), weight_grad(input_five, grad_five)]
    number = row_me * n_batch + batch_me
    line = lax.broadcasted_iota(jnp.int32, (conv_n, 128), 0)
    lane = lax.broadcasted_iota(jnp.int32, (conv_n, 128), 1)
    place = jnp.zeros((conv_n, 128), jnp.float32)
    for k, piece in enumerate(thirds(local_loss)):
        spot = (line == number % conv_n) & (lane == deltas + 3 * (number // conv_n) + k)
        place = jnp.where(spot, piece, place)
    spare = jnp.pad(head_grad, ((0, 0), (0, 128 - deltas))).reshape(-1, conv_n, 128) + place
    conv_all = jnp.concatenate(conv_grad + [spare.reshape(-1, 128)], axis=1)
    conv_all = conv_all.reshape(n_rows, n_batch * conv_n, -1)[order]
    conv_all = summed_rows([conv_all[k] for k in range(n_rows)])
    conv_all = summed_batch(conv_all.reshape(n_batch, conv_n, -1))
    conv_part = jnp.stack([conv_all[:, :width], conv_all[:, width : 2 * width]])
    head_part = conv_all[:, 2 * width : 2 * width + deltas]
    loss_sum = jnp.sum(conv_all[:, 2 * width + deltas :])
    padded_four = rim_backward(grad_four)
    padded_five = rim_backward(grad_five)
    back_merged = conv_back(padded_four, full_conv[0])
    back_five = conv_back(padded_five, full_conv[1])
    grad_lat_four = back_merged.astype(jnp.bfloat16)
    grad_lat_five = (back_five + folded(back_merged)).astype(jnp.bfloat16)
    four_grad = jnp.einsum(
        "bhwc,bhwo->co", section_four, grad_lat_four, preferred_element_type=jnp.float32
    )
    five_grad = jnp.einsum(
        "bhwc,bhwo->co", section_five, grad_lat_five, preferred_element_type=jnp.float32
    )
    lateral_all = jnp.concatenate(
        [
            four_grad.reshape(n_rows, n_batch, four_n, width),
            five_grad.reshape(n_rows, n_batch, five_n, width),
        ],
        axis=2,
    )[order]
    lateral_all = summed_batch(summed_rows([lateral_all[k] for k in range(n_rows)]))
    four_part, five_part = lateral_all[:four_n], lateral_all[four_n:]
    first_four, second_four, weight_four = adamw_update(
        lateral_four, four_part, mean_four, square_four
    )
    first_five, second_five, weight_five = adamw_update(
        lateral_five, five_part, mean_five, square_five
    )
    first_conv, second_conv, weight_conv = adamw_update(
        output_conv, conv_part, mean_conv, square_conv
    )
    first_head, second_head, weight_head = adamw_update(
        delta_head, head_part, mean_head, square_head
    )
    return (
        loss_sum,
        positives,
        first_four,
        first_five,
        first_conv,
        first_head,
        second_four,
        second_five,
        second_conv,
        second_head,
        weight_four,
        weight_five,
        weight_conv,
        weight_head,
    )


def solution(mesh):
    return jax.shard_map(
        on_device,
        mesh=mesh,
        in_specs=(
            P("batch", "rows", None, None),
            P("batch", "rows", None, None),
            P("batch", "rows", None, None),
            P("batch", "rows", None, None),
            P("batch", "rows", None, None),
            P("batch", "rows", None, None),
            P("batch", "rows", None, None),
            P("batch", "rows", None, None),
            P(("rows", "batch"), None),
            P(("rows", "batch"), None),
            P(None, ("rows", "batch"), None),
            P(("rows", "batch"), None),
            P(("rows", "batch"), None),
            P(("rows", "batch"), None),
            P(None, ("rows", "batch"), None),
            P(("rows", "batch"), None),
            P(("rows", "batch"), None),
            P(("rows", "batch"), None),
            P(None, ("rows", "batch"), None),
            P(("rows", "batch"), None),
        ),
        out_specs=(
            P(),
            P(),
            P(("rows", "batch"), None),
            P(("rows", "batch"), None),
            P(None, ("rows", "batch"), None),
            P(("rows", "batch"), None),
            P(("rows", "batch"), None),
            P(("rows", "batch"), None),
            P(None, ("rows", "batch"), None),
            P(("rows", "batch"), None),
            P(("rows", "batch"), None),
            P(("rows", "batch"), None),
            P(None, ("rows", "batch"), None),
            P(("rows", "batch"), None),
        ),
        check_vma=False,
    )
```

```python
import functools

import jax
import jax.numpy as jnp
from jax import lax
from jax.experimental import pallas as pl
from jax.experimental.pallas import tpu as pltpu
from jax.sharding import PartitionSpec as P

STEP = 5

LANES = 128
DELTA_ROWS = 16
VMEM_BYTES = 56 * 1024 * 1024

box_beta = 1.0 / 9.0
beta_one = 0.5
beta_two = 0.5
learn_rate = 0.02
weight_decay = 0.01
epsilon = 1e-08

bf16 = jnp.bfloat16
f32 = jnp.float32


def adamw_update(weight, gradient, mean, square):
    first = beta_one * mean + (1.0 - beta_one) * gradient
    second = beta_two * square + (1.0 - beta_two) * gradient * gradient
    corrected_first = first / (1.0 - beta_one**STEP)
    corrected_second = second / (1.0 - beta_two**STEP)
    return (
        first,
        second,
        weight
        - learn_rate
        * (corrected_first / (jnp.sqrt(corrected_second) + epsilon) + weight_decay * weight),
    )


def sent(value, axis, mask):
    count = lax.axis_size(axis)
    return lax.ppermute(value, axis, [(i, i ^ mask) for i in range(count)])


def gathered_batch(piece):
    count, me = lax.axis_size("batch"), lax.axis_index("batch")
    stacked = jnp.stack([piece] + [sent(piece, "batch", k) for k in range(1, count)])
    return [lax.dynamic_index_in_dim(stacked, t ^ me, 0, keepdims=False) for t in range(count)]


def row_groups():
    count = lax.axis_size("rows")
    low = max(count // 4, 1)
    return count, low, count // low


def gathered_high(piece):
    _, low, high = row_groups()
    return [piece] + [sent(piece, "rows", j * low) for j in range(1, high)]


def gathered_low(held):
    count, low, high = row_groups()
    result = [None] * count
    for j in range(high):
        result[j * low] = held[j]
        for k in range(1, low):
            result[j * low + k] = sent(held[j], "rows", k)
    return result


def summed_low(blocks):
    _, low, high = row_groups()
    came = [sent(blocks[k], "rows", k) for k in range(1, low)]
    return [
        sum((c[j].astype(f32) for c in came), blocks[0][j].astype(f32)) for j in range(high)
    ]


def summed_high(partial):
    _, low, high = row_groups()
    return sum(
        (sent(partial[j].astype(bf16), "rows", j * low).astype(f32) for j in range(1, high)),
        partial[0],
    )


def summed_batch(blocks):
    count, me = lax.axis_size("batch"), lax.axis_index("batch")
    total = lax.dynamic_index_in_dim(blocks, me, 0, keepdims=False)
    for k in range(1, count):
        block = lax.dynamic_index_in_dim(blocks, me ^ k, 0, keepdims=False).astype(bf16)
        total = total + sent(block, "batch", k).astype(f32)
    return total


def from_neighbours(first, last):
    count = lax.axis_size("rows")
    above = lax.ppermute(last, "rows", [(i, i + 1) for i in range(count - 1)])
    below = lax.ppermute(first, "rows", [(i + 1, i) for i in range(count - 1)])
    return above, below


def thirds(value):
    high = lax.reduce_precision(value, 8, 7)
    middle = lax.reduce_precision(value - high, 8, 7)
    return high, middle, value - high - middle


def call(kernel, name, args, outs, scratch=(), flops=0, scalars=0, scalar_outs=0):
    vmem, smem = pl.BlockSpec(memory_space=pltpu.VMEM), pl.BlockSpec(memory_space=pltpu.SMEM)
    size = sum(a.size * a.dtype.itemsize for a in (*args, *outs))
    return pl.pallas_call(
        kernel,
        out_shape=list(outs),
        in_specs=[vmem] * (len(args) - scalars) + [smem] * scalars,
        out_specs=[vmem] * (len(outs) - scalar_outs) + [smem] * scalar_outs,
        scratch_shapes=list(scratch),
        compiler_params=pltpu.CompilerParams(vmem_limit_bytes=VMEM_BYTES),
        cost_estimate=pl.CostEstimate(flops=flops, bytes_accessed=size, transcendentals=0),
        name=name,
    )(*args)


def dot(left, right, dims=((1,), (0,))):
    return lax.dot_general(left, right, (dims, ((), ())), preferred_element_type=f32)


def turned(value, step, axis, width):
    size = value.shape[axis]
    column = lax.broadcasted_iota(jnp.int32, value.shape, axis) % width
    rolled = pltpu.roll(value, step % size, axis)
    return jnp.where(column == (0 if step == 1 else width - 1), 0.0, rolled)


def doubled_columns(ref, row):
    count = row.shape[0]
    for h in range(ref.shape[0]):
        part = row[:, h * LANES : (h + 1) * LANES]
        ref[h, pl.ds(0, count, stride=2), :] = part
        ref[h, pl.ds(1, count, stride=2), :] = part
    return jnp.concatenate([ref[h] for h in range(ref.shape[0])], axis=1)


def lateral_kernel(n_rows, four, five, *refs):
    pieces, (input_four, input_five, first, last, kernel_four, kernel_five, wide) = (
        refs[:n_rows],
        refs[n_rows:],
    )
    crops, height, width, depth = four.shape
    low_height, low_width = five.shape[1:3]
    me = lax.axis_index("rows")
    part_four, part_five = depth // n_rows, five.shape[3] // n_rows
    for k in range(n_rows):
        owner = me ^ k
        at_four = pl.multiple_of(owner * part_four, part_four)
        at_five = pl.multiple_of(owner * part_five, part_five)
        kernel_four[pl.ds(at_four, part_four), :] = pieces[k][:part_four]
        kernel_five[pl.ds(at_five, part_five), :] = pieces[k][part_four:]
    for b in range(crops):
        low = dot(five[b].reshape(low_height * low_width, -1), kernel_five[...])
        low_rounded = low.astype(bf16).reshape(low_height, low_width, -1)
        input_five[b] = low_rounded
        first[b, width:] = low_rounded[0]
        last[b, width:] = low_rounded[low_height - 1]
        for q in range(low_height):
            up = doubled_columns(wide, low[q * low_width : (q + 1) * low_width])
            rows = four[b, 2 * q : 2 * q + 2].reshape(2 * width, depth)
            merged = dot(rows, kernel_four[...]).reshape(2, width, -1) + up[None]
            rounded = merged.astype(bf16)
            input_four[b, 2 * q : 2 * q + 2] = rounded
            if q == 0:
                first[b, :width] = rounded[0]
            if q == low_height - 1:
                last[b, :width] = rounded[1]


def three_taps(source, b, start, rows, weights, step):
    width, channels = source.shape[2:]
    parts = []
    for j in range(3):
        taps = range(3) if step == 1 else (2, 1, 0)
        left = jnp.concatenate(
            [
                source[b, start + i : start + i + rows].reshape(rows * width, channels)
                for i in range(3)
            ],
            axis=1,
        )
        blocks = [weights[(3 * i + j) * channels : (3 * i + j + 1) * channels] for i in taps]
        if step == 1:
            parts.append(dot(left, jnp.concatenate(blocks, axis=0)))
        else:
            parts.append(dot(left, jnp.concatenate(blocks, axis=1), ((1,), (1,))))
    return parts[1] + turned(parts[0], step, 0, width) + turned(parts[2], -step, 0, width)


def fill_padded(padded, own, above, below, start):
    height, width = own.shape[1:3]
    for b in range(own.shape[0]):
        padded[b, 0] = above[b, start : start + width]
        padded[b, 1 : height + 1] = own[b]
        padded[b, height + 1] = below[b, start : start + width]


def output_kernel(n_rows, deltas, input_four, input_five, above, below, *refs):
    pieces, (levels, first, last, kernel_four, kernel_five, head, count, spread_four, spread_five, wide) = (
        refs[:n_rows],
        refs[n_rows:],
    )
    crops, height, width, channels = input_four.shape
    low_height, low_width = input_five.shape[1:3]
    me = lax.axis_index("rows")
    part = 9 * channels // n_rows
    positives = jnp.zeros((), f32)
    spare = wide.at[:]
    for k in range(n_rows):
        at = pl.multiple_of((me ^ k) * part, part)
        kernel_four[pl.ds(at, part), :] = pieces[k][:, :channels]
        kernel_five[pl.ds(at, part), :] = pieces[k][:, channels : 2 * channels]
        spare[pl.ds(at, part), :] = pieces[k][:, 2 * channels :].astype(f32)
    lane = lax.broadcasted_iota(jnp.int32, (channels, LANES), 1)
    line = lax.broadcasted_iota(jnp.int32, (DELTA_ROWS, channels), 0)
    for t in range(9):
        block = spare[t * channels : (t + 1) * channels, :]
        positives = positives + jnp.sum(
            jnp.where((lane >= deltas) & (lane < deltas + 3), block, 0.0)
        )
        turned_block = jnp.where(line < deltas, block.T[:DELTA_ROWS], 0.0)
        head[t * DELTA_ROWS : (t + 1) * DELTA_ROWS, :] = turned_block.astype(bf16)
    count[0, 0] = positives
    fill_padded(spread_four, input_four, above, below, 0)
    fill_padded(spread_five, input_five, above, below, width)
    low_start, top_start = height, height + low_height
    half = width // 2
    levels[:, low_start:, half:, :] = jnp.zeros(
        (crops, levels.shape[1] - low_start, width - half, channels), bf16
    )
    quarter = low_width // 2
    levels[:, top_start:, quarter:, :] = jnp.zeros(
        (crops, levels.shape[1] - top_start, width - quarter, channels), bf16
    )
    rows = 4
    for b in range(crops):
        low = three_taps(spread_five, b, 0, low_height, kernel_five, 1)
        low_rounded = low.astype(bf16).reshape(low_height, low_width, channels)
        levels[b, low_start:top_start, :low_width, :] = low_rounded
        first[b, width : width + low_width] = low_rounded[0]
        last[b, width : width + low_width] = low_rounded[low_height - 1]
        for h in range(0, channels, LANES):
            spare[: low_height * low_width, :] = low[:, h : h + LANES]
            for q in range(low_height // 2):
                total = jnp.zeros((quarter, LANES), f32)
                for at in (2 * q * low_width, (2 * q + 1) * low_width):
                    for side in range(2):
                        total = total + spare[pl.ds(at + side, quarter, stride=2), :]
                pooled = (0.25 * total).astype(bf16)
                levels[b, top_start + q, :quarter, h : h + LANES] = pooled
                if q == 0:
                    first[b, width + low_width :, h : h + LANES] = pooled
                if q == low_height // 2 - 1:
                    last[b, width + low_width :, h : h + LANES] = pooled
        for r in range(0, height, rows):
            sums = three_taps(spread_four, b, r, rows, kernel_four, 1)
            rounded = sums.astype(bf16).reshape(rows, width, channels)
            levels[b, r : r + rows] = rounded
            if r == 0:
                first[b, :width] = rounded[0]
            if r == height - rows:
                last[b, :width] = rounded[rows - 1]


def level_rows(height):
    result, padded, own = [], 0, 0
    for count in (height, height // 2, height // 4):
        result.append((padded, own, count))
        padded, own = padded + count + 2, own + count
    return result


def head_kernel(height, levels, above, below, head, target, mask, count, grads, first, last, loss, spread):
    crops, _, width, channels = levels.shape
    inverse = 1.0 / jnp.maximum(count[0, 0], 1.0)
    plan = level_rows(height)
    summed = jnp.zeros((DELTA_ROWS, LANES), f32)
    for b in range(crops):
        edge = 0
        for index, (padded, own, lines) in enumerate(plan):
            extent = width >> index
            for at, rim in ((padded, above), (padded + lines + 1, below)):
                spread[at, :extent] = rim[b, edge : edge + extent]
                if extent < width:
                    spread[at, extent:] = jnp.zeros((width - extent, channels), bf16)
            spread[padded + 1 : padded + 1 + lines] = levels[b, own : own + lines]
            edge += extent
        total_rows = spread.shape[0]
        products = dot(
            head[...], spread[...].reshape(total_rows * width, channels), ((1,), (1,))
        )
        columns = []
        for j in range(3):
            pieces = []
            for padded, own, lines in plan:
                total = jnp.zeros((DELTA_ROWS, lines * width), f32)
                for i in range(3):
                    tap = (3 * i + j) * DELTA_ROWS
                    total = total + products[
                        tap : tap + DELTA_ROWS, (padded + i) * width : (padded + i + lines) * width
                    ]
                pieces.append(total)
            columns.append(jnp.concatenate(pieces, axis=1))
        values = columns[1] + turned(columns[0], 1, 1, width) + turned(columns[2], -1, 1, width)
        mismatch = values - target[b]
        weight = mask[b]
        magnitude = jnp.abs(mismatch)
        losses = weight * jnp.where(
            magnitude < box_beta, 0.5 * mismatch * mismatch / box_beta, magnitude - 0.5 * box_beta
        )
        for at in range(0, losses.shape[1], LANES):
            summed = summed + losses[:, at : at + LANES]
        gradient = (weight * jnp.clip(mismatch / box_beta, -1.0, 1.0) * inverse).astype(bf16)
        grads[b] = gradient
        for index, (padded, own, lines) in enumerate(plan):
            at = slice(index * width, (index + 1) * width)
            first[b, :, at] = gradient[:, own * width : (own + 1) * width]
            last[b, :, at] = gradient[:, (own + lines - 1) * width : (own + lines) * width]
    loss[0, 0] = jnp.sum(summed)


def back_kernel(height, levels, head, grads, above, below, head_grad, grad_four, grad_five, first, last, taps, wide):
    crops, _, width, channels = levels.shape
    plan = level_rows(height)
    total = jnp.zeros((9 * DELTA_ROWS, channels), f32)
    for b in range(crops):
        pieces = []
        for index, (padded, own, lines) in enumerate(plan):
            at = slice(index * width, (index + 1) * width)
            pieces += [
                above[b, :, at],
                grads[b, :, own * width : (own + lines) * width],
                below[b, :, at],
            ]
        middle = jnp.concatenate(pieces, axis=1).astype(f32)
        shifted = [turned(middle, -1, 1, width), middle, turned(middle, 1, 1, width)]
        for i in range(3):
            for j in range(3):
                for padded, own, lines in plan:
                    at = (padded + 2 - i) * width
                    taps[
                        (3 * i + j) * DELTA_ROWS : (3 * i + j + 1) * DELTA_ROWS,
                        own * width : (own + lines) * width,
                    ] = shifted[j][:, at : at + lines * width].astype(bf16)
        spread = taps[...]
        lines_all = levels.shape[1]
        total = total + dot(spread, levels[b].reshape(lines_all * width, channels))
        back = dot(spread, head[...], ((0,), (0,))).reshape(lines_all, width, channels)
        rounded = back[:height].astype(bf16)
        grad_four[b] = rounded
        first[b, :width] = rounded[0]
        last[b, :width] = rounded[height - 1]
        low_height, low_width = height // 2, width // 2
        for q in range(low_height // 2):
            up = doubled_columns(wide, back[height + low_height + q, : low_width // 2])
            for row in (2 * q, 2 * q + 1):
                low = (back[height + row, :low_width] + 0.25 * up).astype(bf16)
                grad_five[b, row] = low
                if row == 0:
                    first[b, width:] = low
                if row == low_height - 1:
                    last[b, width:] = low
    head_grad[...] = total


def conv_grad_kernel(n_rows, input_four, input_five, above, below, grad_four, grad_five, head_grad, place, kept, turned_rows, sums_four, sums_five, spare):
    crops, height, width, channels = input_four.shape
    low_height, low_width = input_five.shape[1:3]
    padding = jnp.zeros((width - low_width, channels), bf16)
    for own, grad, edge, sums in (
        (input_four, grad_four, 0, sums_four),
        (input_five, grad_five, width, sums_five),
    ):
        lines, extent = own.shape[1:3]

        def widened(row):
            if extent == width:
                return row
            return jnp.concatenate([row, padding], axis=0)

        for b in range(crops):
            for r in range(lines + 2):
                if r == 0:
                    row = above[b, edge : edge + extent]
                elif r == lines + 1:
                    row = below[b, edge : edge + extent]
                else:
                    row = own[b, r - 1]
                turned_rows[:, r * width : (r + 1) * width] = widened(row).T
            left = jnp.concatenate(
                [turned_rows[:, i * width : (i + lines) * width] for i in range(3)], axis=0
            )
            middle = jnp.concatenate([widened(grad[b, r]) for r in range(lines)], axis=0)
            wide = middle.astype(f32)
            right = jnp.concatenate(
                [
                    turned(wide, -1, 0, width).astype(bf16),
                    middle,
                    turned(wide, 1, 0, width).astype(bf16),
                ],
                axis=1,
            )
            product = dot(left, right)
            if b == 0:
                sums[...] = product
            else:
                sums[...] += product
    for t in range(9):
        block = head_grad[t * DELTA_ROWS : (t + 1) * DELTA_ROWS, :]
        block = jnp.concatenate(
            [block, jnp.zeros((LANES - DELTA_ROWS, channels), f32)], axis=0
        )
        spare[t * channels : (t + 1) * channels, :] = block.T
    me = lax.axis_index("rows")
    part = 9 * channels // n_rows
    for owner in range(n_rows):
        index = owner ^ me
        for start in range(0, part, 16):
            line = owner * part + start
            i, rest = divmod(line, 3 * channels)
            j, channel = divmod(rest, channels)
            lines = jnp.concatenate(
                [
                    sums_four[pl.ds(i * channels + channel, 16), j * channels : (j + 1) * channels],
                    sums_five[pl.ds(i * channels + channel, 16), j * channels : (j + 1) * channels],
                    spare[pl.ds(line, 16), :] + place[pl.ds(start, 16), :],
                ],
                axis=1,
            ).astype(bf16)
            kept[index, start : start + 16, :] = lines


def merged_grad_kernel(grad_four, grad_five, above, below, kernel_four, kernel_five, lat_four, lat_five, spread_four, spread_five, fold):
    crops, height, width, channels = grad_four.shape
    low_height, low_width = grad_five.shape[1:3]
    fill_padded(spread_four, grad_four, above, below, 0)
    fill_padded(spread_five, grad_five, above, below, width)
    rows = 4
    for b in range(crops):
        low = three_taps(spread_five, b, 0, low_height, kernel_five, -1)
        low = low.reshape(low_height, low_width, channels)
        for r in range(0, height, rows):
            back = three_taps(spread_four, b, r, rows, kernel_four, -1)
            at = (b * height + r) * width
            lat_four[at : at + rows * width, :] = back.astype(bf16)
            for h in range(0, channels, LANES):
                fold[...] = back[:, h : h + LANES]
                for q in range(rows // 2):
                    total = low[r // 2 + q, :, h : h + LANES]
                    folded = jnp.zeros_like(total)
                    for line in (2 * q * width, (2 * q + 1) * width):
                        for side in range(2):
                            folded = folded + fold[pl.ds(line + side, low_width, stride=2), :]
                    at_low = (b * low_height + r // 2 + q) * low_width
                    lat_five[at_low : at_low + low_width, h : h + LANES] = (total + folded).astype(bf16)


def section_grad_kernel(n_rows, four, five, lat_four, lat_five, kept):
    crops, height, width, depth = four.shape
    low_height, low_width, low_depth = five.shape[1:]
    me = lax.axis_index("rows")
    part_four, part_five = depth // n_rows, low_depth // n_rows
    positions = crops * height * width
    low_positions = crops * low_height * low_width
    turned_four = lat_four[...].T
    turned_five = lat_five[...].T
    for owner in range(n_rows):
        index = owner ^ me
        at = slice(owner * part_four, (owner + 1) * part_four)
        block = dot(turned_four, four[:, :, :, at].reshape(positions, part_four))
        kept[index, :part_four, :] = block.T.astype(bf16)
        at = slice(owner * part_five, (owner + 1) * part_five)
        block = dot(turned_five, five[:, :, :, at].reshape(low_positions, part_five))
        kept[index, part_four:, :] = block.T.astype(bf16)


def planes(field, rows):
    crops, height, width, depth = field.shape
    field = jnp.transpose(field, (0, 3, 1, 2))
    field = jnp.pad(field, ((0, 0), (0, rows - depth), (0, 0), (0, LANES - width)))
    return field.reshape(crops, rows, height * LANES)


def on_device(
    section_four,
    section_five,
    target_four,
    target_five,
    target_six,
    anchor_four,
    anchor_five,
    anchor_six,
    lateral_four,
    lateral_five,
    output_conv,
    delta_head,
    mean_four,
    mean_five,
    mean_conv,
    mean_head,
    square_four,
    square_five,
    square_conv,
    square_head,
):
    n_rows, n_batch = lax.axis_size("rows"), lax.axis_size("batch")
    number = lax.axis_index("rows") * n_batch + lax.axis_index("batch")
    _, low_group, high_group = row_groups()
    crops, height, width, depth = section_four.shape
    low_height, low_width, low_depth = section_five.shape[1:]
    top_width = target_six.shape[2]
    four_n, five_n, conv_n = lateral_four.shape[0], lateral_five.shape[0], output_conv.shape[1]
    channels, deltas = delta_head.shape[0] * n_rows * n_batch // 9, delta_head.shape[1]
    shape = jax.ShapeDtypeStruct

    lateral = jnp.concatenate([lateral_four, lateral_five]).astype(bf16)
    parts = gathered_batch(lateral)
    lateral = jnp.concatenate([p[:four_n] for p in parts] + [p[four_n:] for p in parts])
    laterals = gathered_high(lateral)

    anchors = [a.astype(f32) for a in (anchor_four, anchor_five, anchor_six)]
    mask = jnp.concatenate(
        [planes(jnp.repeat(a, deltas // a.shape[3], axis=3), DELTA_ROWS) for a in anchors], axis=2
    )
    target = jnp.concatenate(
        [planes(t, DELTA_ROWS) for t in (target_four, target_five, target_six)], axis=2
    )
    local_count = sum(jnp.sum(a) for a in anchors)

    lane = lax.broadcasted_iota(jnp.int32, (conv_n, LANES), 1)
    line = lax.broadcasted_iota(jnp.int32, (conv_n, LANES), 0)
    spare = jnp.pad(delta_head, ((0, 0), (0, LANES - deltas)))
    for k, piece in enumerate(thirds(local_count)):
        spare = jnp.where((line == 0) & (lane == deltas + k), piece, spare)
    conv = jnp.concatenate([output_conv[0], output_conv[1], spare], axis=1).astype(bf16)
    conv, _ = lax.optimization_barrier((conv, lateral))
    conv = jnp.concatenate(gathered_batch(conv))
    conv, laterals = lax.optimization_barrier((conv, laterals))
    laterals = gathered_low(laterals)
    convs = gathered_high(conv)

    edge = width + low_width
    input_four, input_five, first, last = call(
        functools.partial(lateral_kernel, n_rows),
        "laterals",
        [section_four, section_five, *laterals],
        [
            shape((crops, height, width, channels), bf16),
            shape((crops, low_height, low_width, channels), bf16),
            shape((crops, edge, channels), bf16),
            shape((crops, edge, channels), bf16),
        ],
        [
            pltpu.VMEM((depth, channels), bf16),
            pltpu.VMEM((low_depth, channels), bf16),
            pltpu.VMEM((channels // LANES, width, LANES), f32),
        ],
        flops=2 * crops * channels * (height * width * depth + low_height * low_width * low_depth),
    )
    above_in, below_in = from_neighbours(first, last)
    convs, _ = lax.optimization_barrier((convs, input_four))
    convs = gathered_low(convs)

    lines = height + low_height + low_height // 2
    conv_flops = 18 * crops * channels * channels * (height * width + low_height * low_width)
    levels, first, last, kernel_four, kernel_five, head, count = call(
        functools.partial(output_kernel, n_rows, deltas),
        "outputs",
        [input_four, input_five, above_in, below_in, *convs],
        [
            shape((crops, lines, width, channels), bf16),
            shape((crops, edge + top_width, channels), bf16),
            shape((crops, edge + top_width, channels), bf16),
            shape((9 * channels, channels), bf16),
            shape((9 * channels, channels), bf16),
            shape((9 * DELTA_ROWS, channels), bf16),
            shape((1, 1), f32),
        ],
        [
            pltpu.VMEM((crops, height + 2, width, channels), bf16),
            pltpu.VMEM((crops, low_height + 2, low_width, channels), bf16),
            pltpu.VMEM((9 * channels, LANES), f32),
        ],
        flops=conv_flops,
        scalar_outs=1,
    )
    above, below = from_neighbours(first, last)

    head_flops = 18 * DELTA_ROWS * crops * lines * width * channels
    grads, first, last, loss = call(
        functools.partial(head_kernel, height),
        "deltas",
        [levels, above, below, head, target, mask, count],
        [
            shape((crops, DELTA_ROWS, lines * width), bf16),
            shape((crops, DELTA_ROWS, 3 * width), bf16),
            shape((crops, DELTA_ROWS, 3 * width), bf16),
            shape((1, 1), f32),
        ],
        [pltpu.VMEM((lines + 6, width, channels), bf16)],
        flops=head_flops,
        scalars=1,
        scalar_outs=1,
    )
    above, below = from_neighbours(first, last)

    head_grad, grad_four, grad_five, first, last = call(
        functools.partial(back_kernel, height),
        "level_grads",
        [levels, head, grads, above, below],
        [
            shape((9 * DELTA_ROWS, channels), f32),
            shape((crops, height, width, channels), bf16),
            shape((crops, low_height, low_width, channels), bf16),
            shape((crops, edge, channels), bf16),
            shape((crops, edge, channels), bf16),
        ],
        [
            pltpu.VMEM((9 * DELTA_ROWS, lines * width), bf16),
            pltpu.VMEM((channels // LANES, low_width, LANES), f32),
        ],
        flops=2 * head_flops,
    )
    above, below = from_neighbours(first, last)

    place = jnp.zeros((conv_n, LANES), f32)
    for k, piece in enumerate(thirds(loss[0, 0])):
        spot = (line == number % conv_n) & (lane == deltas + 3 * (number // conv_n) + k)
        place = jnp.where(spot, piece, place)
    place = jnp.concatenate([place] * n_batch)
    conv_width = 2 * channels + LANES
    (conv_blocks,) = call(
        functools.partial(conv_grad_kernel, n_rows),
        "conv_grads",
        [input_four, input_five, above_in, below_in, grad_four, grad_five, head_grad, place],
        [shape((n_rows, n_batch * conv_n, conv_width), bf16)],
        [
            pltpu.VMEM((channels, (height + 2) * width), bf16),
            pltpu.VMEM((3 * channels, 3 * channels), f32),
            pltpu.VMEM((3 * channels, 3 * channels), f32),
            pltpu.VMEM((9 * channels, LANES), f32),
        ],
        flops=conv_flops,
    )
    conv_blocks = conv_blocks.reshape(high_group, low_group, n_batch * conv_n, conv_width)
    positions, low_positions = crops * height * width, crops * low_height * low_width
    lat_four, lat_five = call(
        merged_grad_kernel,
        "merged_grads",
        [grad_four, grad_five, above, below, kernel_four, kernel_five],
        [shape((positions, channels), bf16), shape((low_positions, channels), bf16)],
        [
            pltpu.VMEM((crops, height + 2, width, channels), bf16),
            pltpu.VMEM((crops, low_height + 2, low_width, channels), bf16),
            pltpu.VMEM((4 * width, LANES), f32),
        ],
        flops=conv_flops,
    )
    conv_partial = summed_low([conv_blocks[:, k] for k in range(low_group)])
    lat_four, conv_partial = lax.optimization_barrier((lat_four, conv_partial))
    conv_sum = summed_high(conv_partial)

    (lateral_blocks,) = call(
        functools.partial(section_grad_kernel, n_rows),
        "lateral_grads",
        [section_four, section_five, lat_four, lat_five],
        [shape((n_rows, n_batch * (four_n + five_n), channels), bf16)],
        flops=2 * channels * (positions * depth + low_positions * low_depth),
    )
    lateral_blocks = lateral_blocks.reshape(
        high_group, low_group, n_batch * (four_n + five_n), channels
    )
    lateral_partial = summed_low([lateral_blocks[:, k] for k in range(low_group)])
    lateral_partial, conv_sum = lax.optimization_barrier((lateral_partial, conv_sum))
    lateral_sum = summed_high(lateral_partial)
    conv_sum = summed_batch(conv_sum.reshape(n_batch, conv_n, conv_width))
    lateral_sum = summed_batch(
        jnp.concatenate(
            [
                lateral_sum[: n_batch * four_n].reshape(n_batch, four_n, channels),
                lateral_sum[n_batch * four_n :].reshape(n_batch, five_n, channels),
            ],
            axis=1,
        )
    )

    conv_part = jnp.stack([conv_sum[:, :channels], conv_sum[:, channels : 2 * channels]])
    head_part = conv_sum[:, 2 * channels : 2 * channels + deltas]
    loss_sum = jnp.sum(conv_sum[:, 2 * channels + deltas :])
    first_four, second_four, weight_four = adamw_update(
        lateral_four, lateral_sum[:four_n], mean_four, square_four
    )
    first_five, second_five, weight_five = adamw_update(
        lateral_five, lateral_sum[four_n:], mean_five, square_five
    )
    first_conv, second_conv, weight_conv = adamw_update(
        output_conv, conv_part, mean_conv, square_conv
    )
    first_head, second_head, weight_head = adamw_update(
        delta_head, head_part, mean_head, square_head
    )
    return (
        loss_sum,
        count[0, 0],
        first_four,
        first_five,
        first_conv,
        first_head,
        second_four,
        second_five,
        second_conv,
        second_head,
        weight_four,
        weight_five,
        weight_conv,
        weight_head,
    )


def solution(mesh):
    split = P("batch", "rows", None, None)
    whole, pair = P(("rows", "batch"), None), P(None, ("rows", "batch"), None)
    weights = (whole, whole, pair, whole)
    return jax.shard_map(
        on_device,
        mesh=mesh,
        in_specs=(split,) * 8 + weights * 3,
        out_specs=(P(), P()) + weights * 3,
        check_vma=False,
    )
```

```python
import functools

import jax
import jax.numpy as jnp
from jax import lax
from jax.experimental import pallas as pl
from jax.experimental.pallas import tpu as pltpu
from jax.sharding import PartitionSpec as P

STEP = 5

LANES = 128
DELTA_ROWS = 16
VMEM_BYTES = 56 * 1024 * 1024

box_beta = 1.0 / 9.0
beta_one = 0.5
beta_two = 0.5
learn_rate = 0.02
weight_decay = 0.01
epsilon = 1e-08

bf16 = jnp.bfloat16
f32 = jnp.float32


def adamw_update(weight, gradient, mean, square):
    first = beta_one * mean + (1.0 - beta_one) * gradient
    second = beta_two * square + (1.0 - beta_two) * gradient * gradient
    corrected_first = first / (1.0 - beta_one**STEP)
    corrected_second = second / (1.0 - beta_two**STEP)
    return (
        first,
        second,
        weight
        - learn_rate
        * (corrected_first / (jnp.sqrt(corrected_second) + epsilon) + weight_decay * weight),
    )


def sent(value, axis, mask):
    count = lax.axis_size(axis)
    return lax.ppermute(value, axis, [(i, i ^ mask) for i in range(count)])


def gathered_batch(piece):
    count, me = lax.axis_size("batch"), lax.axis_index("batch")
    stacked = jnp.stack([piece] + [sent(piece, "batch", k) for k in range(1, count)])
    return [lax.dynamic_index_in_dim(stacked, t ^ me, 0, keepdims=False) for t in range(count)]


def row_groups():
    count = lax.axis_size("rows")
    low = max(count // 4, 1)
    return count, low, count // low


def gathered_high(piece):
    _, low, high = row_groups()
    return [piece] + [sent(piece, "rows", j * low) for j in range(1, high)]


def gathered_low(held):
    count, low, high = row_groups()
    result = [None] * count
    for j in range(high):
        result[j * low] = held[j]
        for k in range(1, low):
            result[j * low + k] = sent(held[j], "rows", k)
    return result


def summed_low(blocks):
    _, low, high = row_groups()
    came = []
    for k in range(1, low):
        whole = isinstance(blocks[k], jax.Array)
        came.append(
            sent(blocks[k], "rows", k) if whole else [sent(block, "rows", k) for block in blocks[k]]
        )
    return [
        sum((c[j].astype(f32) for c in came), blocks[0][j].astype(f32)) for j in range(high)
    ]


def summed_high(partial):
    _, low, high = row_groups()
    return sum(
        (sent(partial[j].astype(bf16), "rows", j * low).astype(f32) for j in range(1, high)),
        partial[0],
    )


def shared_batch(blocks):
    count, me = lax.axis_size("batch"), lax.axis_index("batch")
    own = lax.dynamic_index_in_dim(blocks, me, 0, keepdims=False)
    came = []
    for k in range(1, count):
        block = lax.dynamic_index_in_dim(blocks, me ^ k, 0, keepdims=False).astype(bf16)
        came.append(sent(block, "batch", k))
    return [own, *came]


def from_neighbours(first, last):
    count = lax.axis_size("rows")
    above = lax.ppermute(last, "rows", [(i, i + 1) for i in range(count - 1)])
    below = lax.ppermute(first, "rows", [(i + 1, i) for i in range(count - 1)])
    return above, below


def call(kernel, name, args, outs, scratch=(), flops=0, scalars=0, scalar_outs=0):
    vmem, smem = pl.BlockSpec(memory_space=pltpu.VMEM), pl.BlockSpec(memory_space=pltpu.SMEM)
    size = sum(a.size * a.dtype.itemsize for a in (*args, *outs))
    return pl.pallas_call(
        kernel,
        out_shape=list(outs),
        in_specs=[vmem] * (len(args) - scalars) + [smem] * scalars,
        out_specs=[vmem] * (len(outs) - scalar_outs) + [smem] * scalar_outs,
        scratch_shapes=list(scratch),
        compiler_params=pltpu.CompilerParams(vmem_limit_bytes=VMEM_BYTES),
        cost_estimate=pl.CostEstimate(flops=flops, bytes_accessed=size, transcendentals=0),
        name=name,
    )(*args)


def dot(left, right, dims=((1,), (0,))):
    return lax.dot_general(left, right, (dims, ((), ())), preferred_element_type=f32)


def turned(value, step, axis, width):
    size = value.shape[axis]
    column = lax.broadcasted_iota(jnp.int32, value.shape, axis) % width
    rolled = pltpu.roll(value, step % size, axis)
    return jnp.where(column == (0 if step == 1 else width - 1), 0.0, rolled)


def doubled_columns(ref, row):
    count = row.shape[0]
    for h in range(ref.shape[0]):
        part = row[:, h * LANES : (h + 1) * LANES]
        ref[h, pl.ds(0, count, stride=2), :] = part
        ref[h, pl.ds(1, count, stride=2), :] = part
    return jnp.concatenate([ref[h] for h in range(ref.shape[0])], axis=1)


def pieces_of(value):
    high = value.astype(bf16).astype(f32)
    middle = (value - high).astype(bf16).astype(f32)
    return high, middle, value - high - middle


def pack_lateral_kernel(four, five, packed):
    packed[: four.shape[0]] = four[...].astype(bf16)
    packed[four.shape[0] :] = five[...].astype(bf16)


def pack_conv_kernel(conv, head, anchor_four, anchor_five, anchor_six, packed, square):
    lines, channels = conv.shape[1:]
    deltas = head.shape[0]
    total = jnp.zeros((1, 1), f32)
    for anchor in (anchor_four, anchor_five, anchor_six):
        total = total + jnp.sum(anchor[...].astype(f32), keepdims=True).reshape(1, 1)
    square[...] = jnp.zeros_like(square)
    square[:deltas, :lines] = head[...]
    spare = square[...].T[:lines]
    line = lax.broadcasted_iota(jnp.int32, spare.shape, 0)
    lane = lax.broadcasted_iota(jnp.int32, spare.shape, 1)
    for k, piece in enumerate(pieces_of(jnp.broadcast_to(total, spare.shape))):
        spare = jnp.where((line == 0) & (lane == deltas + k), piece, spare)
    packed[:, :channels] = conv[0].astype(bf16)
    packed[:, channels : 2 * channels] = conv[1].astype(bf16)
    packed[:, 2 * channels :] = spare.astype(bf16)


def lateral_kernel(n_rows, four, five, *refs):
    pieces, (input_four, input_five, first, last, kernel_four, kernel_five, wide) = (
        refs[:n_rows],
        refs[n_rows:],
    )
    crops, height, width, depth = four.shape
    low_height, low_width = five.shape[1:3]
    me = lax.axis_index("rows")
    part_four, part_five = depth // n_rows, five.shape[3] // n_rows
    for k in range(n_rows):
        owner = me ^ k
        at_four = pl.multiple_of(owner * part_four, part_four)
        at_five = pl.multiple_of(owner * part_five, part_five)
        kernel_four[pl.ds(at_four, part_four), :] = pieces[k][:part_four]
        kernel_five[pl.ds(at_five, part_five), :] = pieces[k][part_four:]
    for b in range(crops):
        low = dot(five[b].reshape(low_height * low_width, -1), kernel_five[...])
        low_rounded = low.astype(bf16).reshape(low_height, low_width, -1)
        input_five[b] = low_rounded
        first[b, width:] = low_rounded[0]
        last[b, width:] = low_rounded[low_height - 1]
        for q in range(low_height):
            up = doubled_columns(wide, low[q * low_width : (q + 1) * low_width])
            rows = four[b, 2 * q : 2 * q + 2].reshape(2 * width, depth)
            merged = dot(rows, kernel_four[...]).reshape(2, width, -1) + up[None]
            rounded = merged.astype(bf16)
            input_four[b, 2 * q : 2 * q + 2] = rounded
            if q == 0:
                first[b, :width] = rounded[0]
            if q == low_height - 1:
                last[b, :width] = rounded[1]


def three_taps(source, b, start, rows, weights, step):
    width, channels = source.shape[2:]
    parts = []
    for j in range(3):
        taps = range(3) if step == 1 else (2, 1, 0)
        left = jnp.concatenate(
            [
                source[b, start + i : start + i + rows].reshape(rows * width, channels)
                for i in range(3)
            ],
            axis=1,
        )
        blocks = [weights[(3 * i + j) * channels : (3 * i + j + 1) * channels] for i in taps]
        if step == 1:
            parts.append(dot(left, jnp.concatenate(blocks, axis=0)))
        else:
            parts.append(dot(left, jnp.concatenate(blocks, axis=1), ((1,), (1,))))
    return parts[1] + turned(parts[0], step, 0, width) + turned(parts[2], -step, 0, width)


def fill_padded(padded, own, above, below, start):
    height, width = own.shape[1:3]
    for b in range(own.shape[0]):
        padded[b, 0] = above[b, start : start + width]
        padded[b, 1 : height + 1] = own[b]
        padded[b, height + 1] = below[b, start : start + width]


def output_kernel(n_rows, deltas, input_four, input_five, above, below, target, mask, *refs):
    pieces, (levels, values, first, last, kernel_four, kernel_five, head, count, spread_four, spread_five, wide) = (
        refs[:n_rows],
        refs[n_rows:],
    )
    crops, height, width, channels = input_four.shape
    low_height, low_width = input_five.shape[1:3]
    me = lax.axis_index("rows")
    part = 9 * channels // n_rows
    positives = jnp.zeros((), f32)
    spare = wide.at[:]
    for k in range(n_rows):
        at = pl.multiple_of((me ^ k) * part, part)
        kernel_four[pl.ds(at, part), :] = pieces[k][:, :channels]
        kernel_five[pl.ds(at, part), :] = pieces[k][:, channels : 2 * channels]
        spare[pl.ds(at, part), :] = pieces[k][:, 2 * channels :].astype(f32)
    lane = lax.broadcasted_iota(jnp.int32, (channels, LANES), 1)
    line = lax.broadcasted_iota(jnp.int32, (DELTA_ROWS, channels), 0)
    for t in range(9):
        block = spare[t * channels : (t + 1) * channels, :]
        positives = positives + jnp.sum(
            jnp.where((lane >= deltas) & (lane < deltas + 3), block, 0.0)
        )
        turned_block = jnp.where(line < deltas, block.T[:DELTA_ROWS], 0.0)
        head[t * DELTA_ROWS : (t + 1) * DELTA_ROWS, :] = turned_block.astype(bf16)
    count[0, 0] = positives
    fill_padded(spread_four, input_four, above, below, 0)
    fill_padded(spread_five, input_five, above, below, width)
    low_start, top_start = height, height + low_height
    half = width // 2
    levels[:, low_start:, half:, :] = jnp.zeros(
        (crops, levels.shape[1] - low_start, width - half, channels), bf16
    )
    quarter = low_width // 2
    levels[:, top_start:, quarter:, :] = jnp.zeros(
        (crops, levels.shape[1] - top_start, width - quarter, channels), bf16
    )
    rows = 4
    for b in range(crops):
        low = three_taps(spread_five, b, 0, low_height, kernel_five, 1)
        low_rounded = low.astype(bf16).reshape(low_height, low_width, channels)
        levels[b, low_start:top_start, :low_width, :] = low_rounded
        for h in range(0, channels, LANES):
            spare[: low_height * low_width, :] = low[:, h : h + LANES]
            for q in range(low_height // 2):
                total = jnp.zeros((quarter, LANES), f32)
                for at in (2 * q * low_width, (2 * q + 1) * low_width):
                    for side in range(2):
                        total = total + spare[pl.ds(at + side, quarter, stride=2), :]
                pooled = (0.25 * total).astype(bf16)
                levels[b, top_start + q, :quarter, h : h + LANES] = pooled
        for r in range(0, height, rows):
            sums = three_taps(spread_four, b, r, rows, kernel_four, 1)
            rounded = sums.astype(bf16).reshape(rows, width, channels)
            levels[b, r : r + rows] = rounded
        lines_all = levels.shape[1]
        products = dot(
            head[...], levels[b].reshape(lines_all * width, channels), ((1,), (1,))
        )
        none = jnp.zeros((products.shape[0], 2 * width), f32)
        columns = []
        for j in range(3):
            pieces = []
            for _, own, count_lines in level_rows(height, 1):
                padded = jnp.concatenate(
                    [none, products[:, own * width : (own + count_lines) * width], none], axis=1
                )
                total = jnp.zeros((DELTA_ROWS, (count_lines + 2) * width), f32)
                for i in range(3):
                    tap = (3 * i + j) * DELTA_ROWS
                    at = slice(i * width, (i + count_lines + 2) * width)
                    total = total + padded[tap : tap + DELTA_ROWS, at]
                pieces.append(total)
            columns.append(jnp.concatenate(pieces, axis=1))
        sums = columns[1] + turned(columns[0], 1, 1, width) + turned(columns[2], -1, 1, width)
        for index, (padded, own, count_lines) in enumerate(level_rows(height, 1)):
            own_at = slice(own * width, (own + count_lines) * width)
            start, end = padded * width, (padded + count_lines + 2) * width
            partial = sums[:, start + width : end - width] - target[b, :, own_at]
            values[b, :, start : start + width] = sums[:, start : start + width]
            values[b, :, start + width : end - width] = partial
            values[b, :, end - width : end] = sums[:, end - width : end]
            at = slice(index * width, (index + 1) * width)
            first[b, 0, :, at] = partial[:, :width]
            last[b, 0, :, at] = partial[:, (count_lines - 1) * width :]
            first[b, 1, :, at] = sums[:, start : start + width]
            last[b, 1, :, at] = sums[:, end - width : end]
            first[b, 2, :, at] = mask[b, :, own * width : (own + 1) * width]
            last[b, 2, :, at] = mask[b, :, (own + count_lines - 1) * width : (own + count_lines) * width]


def level_rows(height, rim):
    result, padded, own = [], 0, 0
    for count in (height, height // 2, height // 4):
        result.append((padded, own, count))
        padded, own = padded + count + 2 * rim, own + count
    return result


def head_kernel(height, levels, above, below, head, values, mask, count, head_grad, grad_four, grad_five, first, last, loss, taps, wide):
    crops, _, width, channels = levels.shape
    inverse = 1.0 / jnp.maximum(count[0, 0], 1.0)
    plan = level_rows(height, 1)
    summed = jnp.zeros((DELTA_ROWS, LANES), f32)
    total_grad = jnp.zeros((9 * DELTA_ROWS, channels), f32)
    low_height, low_width = height // 2, width // 2
    for b in range(crops):
        partial, weights = [], []
        for index, (padded, own, lines) in enumerate(plan):
            at = slice(index * width, (index + 1) * width)
            rows = [
                values[b, :, line * width : (line + 1) * width]
                for line in range(padded, padded + lines + 2)
            ]
            rows[0] = rows[0] + above[b, 0, :, at]
            rows[1] = rows[1] + above[b, 1, :, at]
            rows[lines] = rows[lines] + below[b, 1, :, at]
            rows[lines + 1] = rows[lines + 1] + below[b, 0, :, at]
            partial += rows
            weights += [
                above[b, 2, :, at],
                mask[b, :, own * width : (own + lines) * width],
                below[b, 2, :, at],
            ]
        mismatch = jnp.concatenate(partial, axis=1)
        weight = jnp.concatenate(weights, axis=1)
        magnitude = jnp.abs(mismatch)
        losses = weight * jnp.where(
            magnitude < box_beta, 0.5 * mismatch * mismatch / box_beta, magnitude - 0.5 * box_beta
        )
        for padded, own, lines in plan:
            for line in range(padded + 1, padded + 1 + lines):
                summed = summed + losses[:, line * width : (line + 1) * width]
        middle = weight * jnp.clip(mismatch / box_beta, -1.0, 1.0) * inverse
        middle = middle.astype(bf16).astype(f32)
        shifted = [turned(middle, -1, 1, width), middle, turned(middle, 1, 1, width)]
        for i in range(3):
            for j in range(3):
                for padded, own, lines in plan:
                    at = (padded + 2 - i) * width
                    taps[
                        (3 * i + j) * DELTA_ROWS : (3 * i + j + 1) * DELTA_ROWS,
                        own * width : (own + lines) * width,
                    ] = shifted[j][:, at : at + lines * width].astype(bf16)
        around = taps[...]
        lines_all = levels.shape[1]
        total_grad = total_grad + dot(around, levels[b].reshape(lines_all * width, channels))
        back = dot(around, head[...], ((0,), (0,))).reshape(lines_all, width, channels)
        rounded = back[:height].astype(bf16)
        grad_four[b] = rounded
        first[b, :width] = rounded[0]
        last[b, :width] = rounded[height - 1]
        for q in range(low_height // 2):
            up = doubled_columns(wide, back[height + low_height + q, : low_width // 2])
            for row in (2 * q, 2 * q + 1):
                low = (back[height + row, :low_width] + 0.25 * up).astype(bf16)
                grad_five[b, row] = low
                if row == 0:
                    first[b, width:] = low
                if row == low_height - 1:
                    last[b, width:] = low
    head_grad[...] = total_grad
    loss[0, 0] = jnp.sum(summed)


def conv_grad_kernel(n_rows, n_batch, deltas, input_four, input_five, above, below, grad_four, grad_five, head_grad, loss, *refs):
    outs, (turned_rows, sums_four, sums_five, spare) = refs[:-4], refs[-4:]
    crops, height, width, channels = input_four.shape
    low_height, low_width = input_five.shape[1:3]
    padding = jnp.zeros((width - low_width, channels), bf16)
    for own, grad, edge, sums in (
        (input_four, grad_four, 0, sums_four),
        (input_five, grad_five, width, sums_five),
    ):
        lines, extent = own.shape[1:3]

        def widened(row):
            if extent == width:
                return row
            return jnp.concatenate([row, padding], axis=0)

        for b in range(crops):
            for r in range(lines + 2):
                if r == 0:
                    row = above[b, edge : edge + extent]
                elif r == lines + 1:
                    row = below[b, edge : edge + extent]
                else:
                    row = own[b, r - 1]
                turned_rows[:, r * width : (r + 1) * width] = widened(row).T
            left = jnp.concatenate(
                [turned_rows[:, i * width : (i + lines) * width] for i in range(3)], axis=0
            )
            middle = jnp.concatenate([widened(grad[b, r]) for r in range(lines)], axis=0)
            wide = middle.astype(f32)
            right = jnp.concatenate(
                [
                    turned(wide, -1, 0, width).astype(bf16),
                    middle,
                    turned(wide, 1, 0, width).astype(bf16),
                ],
                axis=1,
            )
            for i in range(3):
                product = dot(left[i * channels : (i + 1) * channels], right)
                for j in range(3):
                    at = slice((3 * i + j) * channels, (3 * i + j + 1) * channels)
                    block = product[:, j * channels : (j + 1) * channels]
                    if b == 0:
                        sums[at, :] = block
                    else:
                        sums[at, :] += block
    for t in range(9):
        block = head_grad[t * DELTA_ROWS : (t + 1) * DELTA_ROWS, :]
        block = jnp.concatenate(
            [block, jnp.zeros((LANES - DELTA_ROWS, channels), f32)], axis=0
        )
        spare[t * channels : (t + 1) * channels, :] = block.T
    me = lax.axis_index("rows")
    number = me * n_batch + lax.axis_index("batch")
    part = 9 * channels // n_rows
    own = part // n_batch
    place = jnp.zeros((part, LANES), f32)
    line = lax.broadcasted_iota(jnp.int32, place.shape, 0) % own
    lane = lax.broadcasted_iota(jnp.int32, place.shape, 1) - deltas - 3 * (number // own)
    for piece, value in enumerate(pieces_of(jnp.full(place.shape, loss[0, 0], f32))):
        place = jnp.where((line == number % own) & (lane == piece), value, place)
    low = len(outs)
    for index in range(n_rows):
        at = pl.ds(pl.multiple_of((index ^ me) * part, part), part)
        out, j = outs[index % low], index // low
        out[j, :, :channels] = sums_four[at, :].astype(bf16)
        out[j, :, channels : 2 * channels] = sums_five[at, :].astype(bf16)
        out[j, :, 2 * channels :] = (spare[at, :] + place).astype(bf16)


def merged_grad_kernel(grad_four, grad_five, above, below, kernel_four, kernel_five, lat_four, lat_five, spread_four, spread_five, fold):
    crops, height, width, channels = grad_four.shape
    low_height, low_width = grad_five.shape[1:3]
    fill_padded(spread_four, grad_four, above, below, 0)
    fill_padded(spread_five, grad_five, above, below, width)
    rows = 4
    for b in range(crops):
        low = three_taps(spread_five, b, 0, low_height, kernel_five, -1)
        low = low.reshape(low_height, low_width, channels)
        for r in range(0, height, rows):
            back = three_taps(spread_four, b, r, rows, kernel_four, -1)
            at = (b * height + r) * width
            lat_four[at : at + rows * width, :] = back.astype(bf16)
            for h in range(0, channels, LANES):
                fold[...] = back[:, h : h + LANES]
                for q in range(rows // 2):
                    total = low[r // 2 + q, :, h : h + LANES]
                    folded = jnp.zeros_like(total)
                    for line in (2 * q * width, (2 * q + 1) * width):
                        for side in range(2):
                            folded = folded + fold[pl.ds(line + side, low_width, stride=2), :]
                    at_low = (b * low_height + r // 2 + q) * low_width
                    lat_five[at_low : at_low + low_width, h : h + LANES] = (total + folded).astype(bf16)


def section_grad_kernel(n_rows, four, five, lat_four, lat_five, kept, *refs):
    outs, (sums_four, sums_five) = refs[:-2], refs[-2:]
    crops, height, width, depth = four.shape
    low_height, low_width, low_depth = five.shape[1:]
    me = lax.axis_index("rows")
    part_four, part_five = depth // n_rows, low_depth // n_rows
    positions = crops * height * width
    low_positions = crops * low_height * low_width
    turned_four = lat_four[...].T
    turned_five = lat_five[...].T
    step = 256
    for at in range(0, depth, step):
        block = four[:, :, :, at : at + step].reshape(positions, step)
        sums_four[at : at + step, :] = dot(turned_four, block).T
    for at in range(0, low_depth, step):
        block = five[:, :, :, at : at + step].reshape(low_positions, step)
        sums_five[at : at + step, :] = dot(turned_five, block).T
    high = kept.shape[0]
    low = n_rows // high
    for index in range(n_rows):
        k, j = index % low, index // low
        out = kept.at[j] if k == 0 else outs[k - 1].at[j]
        owner = index ^ me
        at = pl.ds(pl.multiple_of(owner * part_four, part_four), part_four)
        out[:part_four, :] = sums_four[at, :].astype(bf16)
        at = pl.ds(pl.multiple_of(owner * part_five, part_five), part_five)
        out[part_four:, :] = sums_five[at, :].astype(bf16)


def adamw_into(outs, weight, gradient, mean, square):
    for out, value in zip(outs, adamw_update(weight, gradient, mean, square)):
        out[...] = value


def conv_step_kernel(count, deltas, own, *refs):
    came, (weight, mean, square, first, second, new, head, loss) = refs[:count], refs[count:]
    channels = weight.shape[2]
    total = own[...]
    for piece in came:
        total = total + piece[...].astype(f32)
    for k in range(2):
        adamw_into(
            (first.at[k], second.at[k], new.at[k]),
            weight[k],
            total[:, k * channels : (k + 1) * channels],
            mean[k],
            square[k],
        )
    spare = total[:, 2 * channels :]
    head[...] = spare
    lane = lax.broadcasted_iota(jnp.int32, spare.shape, 1)
    loss[0, 0] = jnp.sum(jnp.where(lane >= deltas, spare, 0.0))


def lateral_step_kernel(count, own, *refs):
    came, rest = refs[:count], refs[count:]
    inputs, outs = rest[:6], rest[6:]
    total = own[...]
    for piece in came:
        total = total + piece[...].astype(f32)
    lines = inputs[0].shape[0]
    for k, gradient in enumerate((total[:lines], total[lines:])):
        weight, mean, square = (ref[...] for ref in inputs[3 * k : 3 * k + 3])
        adamw_into(outs[3 * k : 3 * k + 3], weight, gradient, mean, square)


def planes(field, rows):
    crops, height, width, depth = field.shape
    field = jnp.transpose(field, (0, 3, 1, 2))
    field = jnp.pad(field, ((0, 0), (0, rows - depth), (0, 0), (0, LANES - width)))
    return field.reshape(crops, rows, height * LANES)


def on_device(
    section_four,
    section_five,
    target_four,
    target_five,
    target_six,
    anchor_four,
    anchor_five,
    anchor_six,
    lateral_four,
    lateral_five,
    output_conv,
    delta_head,
    mean_four,
    mean_five,
    mean_conv,
    mean_head,
    square_four,
    square_five,
    square_conv,
    square_head,
):
    n_rows, n_batch = lax.axis_size("rows"), lax.axis_size("batch")
    _, low_group, high_group = row_groups()
    crops, height, width, depth = section_four.shape
    low_height, low_width, low_depth = section_five.shape[1:]
    four_n, five_n, conv_n = lateral_four.shape[0], lateral_five.shape[0], output_conv.shape[1]
    channels, deltas = delta_head.shape[0] * n_rows * n_batch // 9, delta_head.shape[1]
    shape = jax.ShapeDtypeStruct

    (lateral,) = call(
        pack_lateral_kernel,
        "pack_laterals",
        [lateral_four, lateral_five],
        [shape((four_n + five_n, channels), bf16)],
    )
    parts = gathered_batch(lateral)
    lateral = jnp.concatenate([p[:four_n] for p in parts] + [p[four_n:] for p in parts])
    laterals = gathered_high(lateral)

    flat = [jnp.transpose(a, (0, 3, 1, 2)) for a in (anchor_four, anchor_five, anchor_six)]
    (conv,) = call(
        pack_conv_kernel,
        "pack_convs",
        [output_conv, delta_head.T, *flat],
        [shape((conv_n, 2 * channels + LANES), bf16)],
        [pltpu.VMEM((LANES, LANES), f32)],
    )
    conv, _ = lax.optimization_barrier((conv, lateral))
    conv = jnp.concatenate(gathered_batch(conv))
    anchors, targets, _ = lax.optimization_barrier(
        (
            (anchor_four, anchor_five, anchor_six),
            (target_four, target_five, target_six),
            conv,
        )
    )
    mask = jnp.concatenate(
        [
            planes(jnp.repeat(a.astype(f32), deltas // a.shape[3], axis=3), DELTA_ROWS)
            for a in anchors
        ],
        axis=2,
    )
    target = jnp.concatenate([planes(t, DELTA_ROWS) for t in targets], axis=2)
    conv, laterals = lax.optimization_barrier((conv, laterals))
    laterals = gathered_low(laterals)
    convs = gathered_high(conv)

    edge = width + low_width
    input_four, input_five, first, last = call(
        functools.partial(lateral_kernel, n_rows),
        "laterals",
        [section_four, section_five, *laterals],
        [
            shape((crops, height, width, channels), bf16),
            shape((crops, low_height, low_width, channels), bf16),
            shape((crops, edge, channels), bf16),
            shape((crops, edge, channels), bf16),
        ],
        [
            pltpu.VMEM((depth, channels), bf16),
            pltpu.VMEM((low_depth, channels), bf16),
            pltpu.VMEM((channels // LANES, width, LANES), f32),
        ],
        flops=2 * crops * channels * (height * width * depth + low_height * low_width * low_depth),
    )
    above_in, below_in = from_neighbours(first, last)
    convs, above_in, below_in = lax.optimization_barrier((convs, above_in, below_in))
    convs = gathered_low(convs)

    lines = height + low_height + low_height // 2
    conv_flops = 18 * crops * channels * channels * (height * width + low_height * low_width)
    levels, values, first, last, kernel_four, kernel_five, head, count = call(
        functools.partial(output_kernel, n_rows, deltas),
        "outputs",
        [input_four, input_five, above_in, below_in, target, mask, *convs],
        [
            shape((crops, lines, width, channels), bf16),
            shape((crops, DELTA_ROWS, (lines + 6) * width), f32),
            shape((crops, 3, DELTA_ROWS, 3 * width), f32),
            shape((crops, 3, DELTA_ROWS, 3 * width), f32),
            shape((9 * channels, channels), bf16),
            shape((9 * channels, channels), bf16),
            shape((9 * DELTA_ROWS, channels), bf16),
            shape((1, 1), f32),
        ],
        [
            pltpu.VMEM((crops, height + 2, width, channels), bf16),
            pltpu.VMEM((crops, low_height + 2, low_width, channels), bf16),
            pltpu.VMEM((9 * channels, LANES), f32),
        ],
        flops=conv_flops,
        scalar_outs=1,
    )
    above, below = from_neighbours(first, last)

    head_flops = 18 * DELTA_ROWS * crops * lines * width * channels
    head_grad, grad_four, grad_five, first, last, loss = call(
        functools.partial(head_kernel, height),
        "heads",
        [levels, above, below, head, values, mask, count],
        [
            shape((9 * DELTA_ROWS, channels), f32),
            shape((crops, height, width, channels), bf16),
            shape((crops, low_height, low_width, channels), bf16),
            shape((crops, edge, channels), bf16),
            shape((crops, edge, channels), bf16),
            shape((1, 1), f32),
        ],
        [
            pltpu.VMEM((9 * DELTA_ROWS, lines * width), bf16),
            pltpu.VMEM((channels // LANES, low_width, LANES), f32),
        ],
        flops=3 * head_flops,
        scalars=1,
        scalar_outs=1,
    )
    above, below = from_neighbours(first, last)

    conv_width = 2 * channels + LANES
    conv_blocks = call(
        functools.partial(conv_grad_kernel, n_rows, n_batch, deltas),
        "conv_grads",
        [input_four, input_five, above_in, below_in, grad_four, grad_five, head_grad, loss],
        [shape((high_group, n_batch * conv_n, conv_width), bf16)] * low_group,
        [
            pltpu.VMEM((channels, (height + 2) * width), bf16),
            pltpu.VMEM((9 * channels, channels), f32),
            pltpu.VMEM((9 * channels, channels), f32),
            pltpu.VMEM((9 * channels, LANES), f32),
        ],
        flops=conv_flops,
        scalars=1,
    )

    positions, low_positions = crops * height * width, crops * low_height * low_width
    conv_partial = summed_low(conv_blocks)
    above, below, conv_partial = lax.optimization_barrier((above, below, conv_partial))
    lat_four, lat_five = call(
        merged_grad_kernel,
        "merged_grads",
        [grad_four, grad_five, above, below, kernel_four, kernel_five],
        [shape((positions, channels), bf16), shape((low_positions, channels), bf16)],
        [
            pltpu.VMEM((crops, height + 2, width, channels), bf16),
            pltpu.VMEM((crops, low_height + 2, low_width, channels), bf16),
            pltpu.VMEM((4 * width, LANES), f32),
        ],
        flops=conv_flops,
    )
    conv_sum = summed_high(conv_partial)

    lateral_n = four_n + five_n
    lateral_kept, *lateral_moved = call(
        functools.partial(section_grad_kernel, n_rows),
        "lateral_grads",
        [section_four, section_five, lat_four, lat_five],
        [shape((high_group, n_batch * lateral_n, channels), bf16)] * low_group,
        [pltpu.VMEM((depth, channels), f32), pltpu.VMEM((low_depth, channels), f32)],
        flops=1,
    )
    lateral_moved, conv_sum = lax.optimization_barrier((lateral_moved, conv_sum))
    lateral_partial = summed_low([lateral_kept, *lateral_moved])
    lateral_sum = summed_high(lateral_partial)
    conv_shares = shared_batch(conv_sum.reshape(n_batch, conv_n, conv_width))
    conv_shares, lateral_sum = lax.optimization_barrier((conv_shares, lateral_sum))
    first_conv, second_conv, weight_conv, head_part, loss_sum = call(
        functools.partial(conv_step_kernel, n_batch - 1, deltas),
        "conv_step",
        [*conv_shares, output_conv, mean_conv, square_conv],
        [shape(output_conv.shape, f32)] * 3 + [shape((conv_n, LANES), f32), shape((1, 1), f32)],
        scalar_outs=1,
    )
    lateral_sum = jnp.concatenate(
        [
            lateral_sum[: n_batch * four_n].reshape(n_batch, four_n, channels),
            lateral_sum[n_batch * four_n :].reshape(n_batch, five_n, channels),
        ],
        axis=1,
    )
    first_four, second_four, weight_four, first_five, second_five, weight_five = call(
        functools.partial(lateral_step_kernel, n_batch - 1),
        "lateral_step",
        [
            *shared_batch(lateral_sum),
            lateral_four,
            mean_four,
            square_four,
            lateral_five,
            mean_five,
            square_five,
        ],
        [shape(lateral_four.shape, f32)] * 3 + [shape(lateral_five.shape, f32)] * 3,
    )
    head_part = head_part[:, :deltas]
    first_head, second_head, weight_head = adamw_update(
        delta_head, head_part, mean_head, square_head
    )
    return (
        loss_sum[0, 0],
        count[0, 0],
        first_four,
        first_five,
        first_conv,
        first_head,
        second_four,
        second_five,
        second_conv,
        second_head,
        weight_four,
        weight_five,
        weight_conv,
        weight_head,
    )


def solution(mesh):
    split = P("batch", "rows", None, None)
    whole, pair = P(("rows", "batch"), None), P(None, ("rows", "batch"), None)
    weights = (whole, whole, pair, whole)
    return jax.shard_map(
        on_device,
        mesh=mesh,
        in_specs=(split,) * 8 + weights * 3,
        out_specs=(P(), P()) + weights * 3,
        check_vma=False,
    )
```

```python
import functools
import math

import jax
import jax.numpy as jnp
from jax import lax
from jax.experimental import pallas as pl
from jax.experimental.pallas import tpu as pltpu
from jax.sharding import PartitionSpec as P

STEP = 5

LANES = 128
DELTA_ROWS = 16
SPARE_BYTES = 12 * 1024 * 1024
ALL_BYTES = 60 * 1024 * 1024

box_beta = 1.0 / 9.0
beta_one = 0.5
beta_two = 0.5
learn_rate = 0.02
weight_decay = 0.01
epsilon = 1e-08

bf16 = jnp.bfloat16
f32 = jnp.float32


def adamw_update(weight, gradient, mean, square):
    first = beta_one * mean + (1.0 - beta_one) * gradient
    second = beta_two * square + (1.0 - beta_two) * gradient * gradient
    corrected_first = first / (1.0 - beta_one**STEP)
    corrected_second = second / (1.0 - beta_two**STEP)
    return (
        first,
        second,
        weight
        - learn_rate
        * (corrected_first / (jnp.sqrt(corrected_second) + epsilon) + weight_decay * weight),
    )


def sent(value, axis, mask):
    count = lax.axis_size(axis)
    return lax.ppermute(value, axis, [(i, i ^ mask) for i in range(count)])


def gathered_batch(piece):
    count, me = lax.axis_size("batch"), lax.axis_index("batch")
    stacked = jnp.stack([piece] + [sent(piece, "batch", k) for k in range(1, count)])
    return [lax.dynamic_index_in_dim(stacked, t ^ me, 0, keepdims=False) for t in range(count)]


def row_groups():
    count = lax.axis_size("rows")
    low = max(count // 4, 1)
    return count, low, count // low


def gathered_high(piece):
    _, low, high = row_groups()
    return [piece] + [sent(piece, "rows", j * low) for j in range(1, high)]


def gathered_low(held):
    count, low, high = row_groups()
    result = [None] * count
    for j in range(high):
        result[j * low] = held[j]
        for k in range(1, low):
            result[j * low + k] = sent(held[j], "rows", k)
    return result


def summed_low(blocks):
    _, low, high = row_groups()
    came = []
    for k in range(1, low):
        whole = isinstance(blocks[k], jax.Array)
        came.append(
            sent(blocks[k], "rows", k) if whole else [sent(block, "rows", k) for block in blocks[k]]
        )
    return [
        sum((c[j].astype(f32) for c in came), blocks[0][j].astype(f32)) for j in range(high)
    ]


def summed_high(partial):
    _, low, high = row_groups()
    return sum(
        (sent(partial[j].astype(bf16), "rows", j * low).astype(f32) for j in range(1, high)),
        partial[0],
    )


def shared_batch(blocks):
    count, me = lax.axis_size("batch"), lax.axis_index("batch")
    own = lax.dynamic_index_in_dim(blocks, me, 0, keepdims=False)
    came = []
    for k in range(1, count):
        block = lax.dynamic_index_in_dim(blocks, me ^ k, 0, keepdims=False).astype(bf16)
        came.append(sent(block, "batch", k))
    return [own, *came]


def from_neighbours(pair, other):
    count = lax.axis_size("rows")
    links = [(i, i + 1) for i in range(1, count - 1, 2)]
    return sent(pair, "rows", 1), lax.ppermute(other, "rows", links + [(j, i) for i, j in links])


def call(kernel, name, args, outs, scratch=(), flops=0, scalars=0, scalar_outs=0, apart=0):
    vmem, smem = pl.BlockSpec(memory_space=pltpu.VMEM), pl.BlockSpec(memory_space=pltpu.SMEM)
    hbm = pl.BlockSpec(memory_space=pltpu.HBM)
    size = sum(a.size * a.dtype.itemsize for a in (*args, *outs))
    held = sum(
        math.prod(ref.shape) * jnp.dtype(ref.dtype).itemsize
        for ref in scratch
        if ref.memory_space == pltpu.VMEM
    )
    return pl.pallas_call(
        kernel,
        out_shape=list(outs),
        in_specs=[hbm] * apart + [vmem] * (len(args) - scalars - apart) + [smem] * scalars,
        out_specs=[vmem] * (len(outs) - scalar_outs) + [smem] * scalar_outs,
        scratch_shapes=list(scratch),
        compiler_params=pltpu.CompilerParams(vmem_limit_bytes=ALL_BYTES if apart else held + SPARE_BYTES),
        cost_estimate=pl.CostEstimate(flops=flops, bytes_accessed=size, transcendentals=0),
        name=name,
    )(*args)


def swapped(upper, lower, pair, other, outward):
    odd = lax.axis_index("rows") % 2 == 1

    def move(one, two):
        for ref, side in ((one, pair), (two, other)):
            if outward:
                side[...] = ref[...]
            else:
                ref[...] = side[...]

    pl.when(odd)(lambda: move(upper, lower))
    pl.when(jnp.logical_not(odd))(lambda: move(lower, upper))


def dot(left, right, dims=((1,), (0,))):
    return lax.dot_general(left, right, (dims, ((), ())), preferred_element_type=f32)


def turned(value, step, axis, width):
    size = value.shape[axis]
    column = lax.broadcasted_iota(jnp.int32, value.shape, axis) % width
    rolled = pltpu.roll(value, step % size, axis)
    return jnp.where(column == (0 if step == 1 else width - 1), 0.0, rolled)


def doubled_columns(ref, row):
    count = row.shape[0]
    for h in range(ref.shape[0]):
        part = row[:, h * LANES : (h + 1) * LANES]
        ref[h, pl.ds(0, count, stride=2), :] = part
        ref[h, pl.ds(1, count, stride=2), :] = part
    return jnp.concatenate([ref[h] for h in range(ref.shape[0])], axis=1)


def pieces_of(value):
    high = value.astype(bf16).astype(f32)
    middle = (value - high).astype(bf16).astype(f32)
    return high, middle, value - high - middle


def pack_kernel(*refs):
    sources, packed, square, held, arrived = refs[:6], refs[6], refs[7], refs[8:14], refs[14]
    copies = [
        pltpu.make_async_copy(source, target, arrived.at[k])
        for k, (source, target) in enumerate(zip(sources, held))
    ]
    for copy in copies:
        copy.start()
    for copy in copies:
        copy.wait()
    four, five, head, anchor_four, anchor_five, anchor_six = held
    lines = four.shape[0] + five.shape[0]
    packed[: four.shape[0]] = four[...].astype(bf16)
    packed[four.shape[0] : lines] = five[...].astype(bf16)
    total = jnp.zeros((1, 1), f32)
    for anchor in (anchor_four, anchor_five, anchor_six):
        total = total + jnp.sum(anchor[...].astype(f32), keepdims=True).reshape(1, 1)
    square[...] = jnp.zeros_like(square)
    square[: head.shape[0], : head.shape[1]] = head[...]
    spare = square[...]
    line = lax.broadcasted_iota(jnp.int32, spare.shape, 0)
    lane = lax.broadcasted_iota(jnp.int32, spare.shape, 1)
    for k, piece in enumerate(pieces_of(jnp.broadcast_to(total, spare.shape))):
        spare = jnp.where((line == head.shape[0]) & (lane == k), piece, spare)
    packed[lines:] = joined(spare).astype(bf16)


def joined(square):
    return jnp.concatenate([square[:8], square[8:]], axis=1)


def parted(lines):
    return jnp.concatenate([lines[:, :LANES], lines[:, LANES:]], axis=0)


def head_weights_kernel(n_rows, n_batch, deltas, own, *refs):
    pieces, (head, count, flat) = refs[:n_rows], refs[n_rows:]
    channels = head.shape[1]
    me = lax.axis_index("rows")
    flat[...] = jnp.zeros_like(flat)
    line = lax.broadcasted_iota(jnp.int32, (DELTA_ROWS, LANES), 0)
    total = jnp.zeros((DELTA_ROWS, LANES), f32)
    for k in range(n_rows):
        lines = pieces[k][pieces[k].shape[0] - 8 * n_batch :].astype(f32)
        for z in range(n_batch):
            square = parted(lines[8 * z : 8 * z + 8])
            total = total + jnp.where(line >= deltas, square, 0.0)
            square = jnp.where(line < deltas, square, 0.0)
            place = ((me ^ k) * n_batch + z) * own
            wide = jnp.concatenate([square, jnp.zeros_like(square)], axis=1)
            wide = pltpu.roll(wide, place % LANES, 1)
            at = pl.ds(pl.multiple_of(place // LANES * LANES, LANES), 2 * LANES)
            flat[:, at] += wide
    for t in range(9):
        block = flat[:, t * channels : (t + 1) * channels].astype(bf16)
        head[t * DELTA_ROWS : (t + 1) * DELTA_ROWS, :] = block
    count[0, 0] = jnp.sum(total)


def planes_kernel(*refs):
    targets, anchors, (target, mask) = refs[:3], refs[3:6], refs[-2:]
    crops, deltas = targets[0].shape[:2]
    own = 0
    target[:, deltas:, :] = jnp.zeros((crops, target.shape[1] - deltas, target.shape[2]), f32)
    mask[:, deltas:, :] = jnp.zeros((crops, mask.shape[1] - deltas, mask.shape[2]), f32)
    for target_ref, anchor_ref in zip(targets, anchors):
        _, count, lines, width = anchor_ref.shape
        share = deltas // count
        for b in range(crops):
            for r in range(lines):
                at, rest = own + r * LANES, LANES - width
                target[b, :deltas, at : at + width] = target_ref[b, :, r, :]
                if rest:
                    target[b, :deltas, at + width : at + LANES] = jnp.zeros((deltas, rest), f32)
                    mask[b, :deltas, at + width : at + LANES] = jnp.zeros((deltas, rest), f32)
                for a in range(count):
                    row = anchor_ref[b, a, r : r + 1, :].astype(f32)
                    mask[b, a * share : (a + 1) * share, at : at + width] = jnp.broadcast_to(
                        row, (share, width)
                    )
        own += lines * LANES


def lateral_kernel(n_rows, four, five, *refs):
    pieces, rest = refs[:n_rows], refs[n_rows:]
    input_four, input_five, pair, other, kernel_four, kernel_five, wide, first, last = rest
    crops, height, width, depth = four.shape
    low_height, low_width = five.shape[1:3]
    me = lax.axis_index("rows")
    part_four, part_five = depth // n_rows, five.shape[3] // n_rows
    for k in range(n_rows):
        owner = me ^ k
        at_four = pl.multiple_of(owner * part_four, part_four)
        at_five = pl.multiple_of(owner * part_five, part_five)
        kernel_four[pl.ds(at_four, part_four), :] = pieces[k][:part_four]
        kernel_five[pl.ds(at_five, part_five), :] = pieces[k][part_four : part_four + part_five]
    for b in range(crops):
        low = dot(five[b].reshape(low_height * low_width, -1), kernel_five[...])
        low_rounded = low.astype(bf16).reshape(low_height, low_width, -1)
        input_five[b] = low_rounded
        first[b, width:] = low_rounded[0]
        last[b, width:] = low_rounded[low_height - 1]
        for q in range(low_height):
            up = doubled_columns(wide, low[q * low_width : (q + 1) * low_width])
            rows = four[b, 2 * q : 2 * q + 2].reshape(2 * width, depth)
            merged = dot(rows, kernel_four[...]).reshape(2, width, -1) + up[None]
            rounded = merged.astype(bf16)
            input_four[b, 2 * q : 2 * q + 2] = rounded
            if q == 0:
                first[b, :width] = rounded[0]
            if q == low_height - 1:
                last[b, :width] = rounded[1]
    swapped(first, last, pair, other, True)


def three_taps(source, b, start, rows, weights, step):
    width, channels = source.shape[2:]
    parts = []
    for j in range(3):
        taps = range(3) if step == 1 else (2, 1, 0)
        left = jnp.concatenate(
            [
                source[b, start + i : start + i + rows].reshape(rows * width, channels)
                for i in range(3)
            ],
            axis=1,
        )
        blocks = [weights[(3 * i + j) * channels : (3 * i + j + 1) * channels] for i in taps]
        if step == 1:
            parts.append(dot(left, jnp.concatenate(blocks, axis=0)))
        else:
            parts.append(dot(left, jnp.concatenate(blocks, axis=1), ((1,), (1,))))
    return parts[1] + turned(parts[0], step, 0, width) + turned(parts[2], -step, 0, width)


def fill_padded(padded, own, above, below, start):
    height, width = own.shape[1:3]
    for b in range(own.shape[0]):
        padded[b, 0] = above[b, start : start + width]
        padded[b, 1 : height + 1] = own[b]
        padded[b, height + 1] = below[b, start : start + width]


def output_kernel(n_rows, input_four, input_five, pair_in, other_in, head, target, mask, *refs):
    pieces, rest = refs[:n_rows], refs[n_rows:]
    levels, values, pair, other, kernel_four, kernel_five = rest[:6]
    spread_four, spread_five, spare, above, below, first, last = rest[6:]
    swapped(above, below, pair_in, other_in, False)
    crops, height, width, channels = input_four.shape
    low_height, low_width = input_five.shape[1:3]
    me = lax.axis_index("rows")
    part = 9 * channels // n_rows
    for k in range(n_rows):
        at = pl.multiple_of((me ^ k) * part, part)
        kernel_four[pl.ds(at, part), :] = pieces[k][:, :channels]
        kernel_five[pl.ds(at, part), :] = pieces[k][:, channels:]
    fill_padded(spread_four, input_four, above, below, 0)
    fill_padded(spread_five, input_five, above, below, width)
    low_start, top_start = height, height + low_height
    half = width // 2
    levels[:, low_start:, half:, :] = jnp.zeros(
        (crops, levels.shape[1] - low_start, width - half, channels), bf16
    )
    quarter = low_width // 2
    levels[:, top_start:, quarter:, :] = jnp.zeros(
        (crops, levels.shape[1] - top_start, width - quarter, channels), bf16
    )
    rows = 4
    for b in range(crops):
        low = three_taps(spread_five, b, 0, low_height, kernel_five, 1)
        low_rounded = low.astype(bf16).reshape(low_height, low_width, channels)
        levels[b, low_start:top_start, :low_width, :] = low_rounded
        for h in range(0, channels, LANES):
            spare[: low_height * low_width, :] = low[:, h : h + LANES]
            for q in range(low_height // 2):
                total = jnp.zeros((quarter, LANES), f32)
                for at in (2 * q * low_width, (2 * q + 1) * low_width):
                    for side in range(2):
                        total = total + spare[pl.ds(at + side, quarter, stride=2), :]
                pooled = (0.25 * total).astype(bf16)
                levels[b, top_start + q, :quarter, h : h + LANES] = pooled
        for r in range(0, height, rows):
            sums = three_taps(spread_four, b, r, rows, kernel_four, 1)
            rounded = sums.astype(bf16).reshape(rows, width, channels)
            levels[b, r : r + rows] = rounded
        lines_all = levels.shape[1]
        products = dot(
            head[...], levels[b].reshape(lines_all * width, channels), ((1,), (1,))
        )
        none = jnp.zeros((products.shape[0], 2 * width), f32)
        columns = []
        for j in range(3):
            pieces = []
            for _, own, count_lines in level_rows(height, 1):
                padded = jnp.concatenate(
                    [none, products[:, own * width : (own + count_lines) * width], none], axis=1
                )
                total = jnp.zeros((DELTA_ROWS, (count_lines + 2) * width), f32)
                for i in range(3):
                    tap = (3 * i + j) * DELTA_ROWS
                    at = slice(i * width, (i + count_lines + 2) * width)
                    total = total + padded[tap : tap + DELTA_ROWS, at]
                pieces.append(total)
            columns.append(jnp.concatenate(pieces, axis=1))
        sums = columns[1] + turned(columns[0], 1, 1, width) + turned(columns[2], -1, 1, width)
        for index, (padded, own, count_lines) in enumerate(level_rows(height, 1)):
            own_at = slice(own * width, (own + count_lines) * width)
            start, end = padded * width, (padded + count_lines + 2) * width
            partial = sums[:, start + width : end - width] - target[b, :, own_at]
            values[b, :, start : start + width] = sums[:, start : start + width]
            values[b, :, start + width : end - width] = partial
            values[b, :, end - width : end] = sums[:, end - width : end]
            own_end = (own + count_lines) * width
            upper = (
                partial[:, :width],
                sums[:, start : start + width],
                mask[b, :, own * width : (own + 1) * width],
            )
            lower = (
                partial[:, (count_lines - 1) * width :],
                sums[:, end - width : end],
                mask[b, :, own_end - width : own_end],
            )
            for out, values_of in ((first, upper), (last, lower)):
                for kind, line in enumerate(values_of):
                    if index < 2:
                        out[b, kind, :, index * width : (index + 1) * width] = line
                    else:
                        moved = pltpu.roll(line, half, 1)
                        lane = lax.broadcasted_iota(jnp.int32, line.shape, 1)
                        mixed = jnp.where(lane < half, out[b, kind, :, width : 2 * width], moved)
                        out[b, kind, :, width : 2 * width] = mixed
    swapped(first, last, pair, other, True)


def level_rows(height, rim):
    result, padded, own = [], 0, 0
    for count in (height, height // 2, height // 4):
        result.append((padded, own, count))
        padded, own = padded + count + 2 * rim, own + count
    return result


def head_kernel(height, levels, pair_in, other_in, head, values, mask, count, *refs):
    head_grad, grad_four, grad_five, pair, other, loss = refs[:6]
    taps, wide, above, below, first, last = refs[6:]
    swapped(above, below, pair_in, other_in, False)
    crops, _, width, channels = levels.shape
    inverse = 1.0 / jnp.maximum(count[0, 0], 1.0)
    plan = level_rows(height, 1)
    summed = jnp.zeros((DELTA_ROWS, LANES), f32)
    total_grad = jnp.zeros((9 * DELTA_ROWS, channels), f32)
    low_height, low_width = height // 2, width // 2
    def came(ref, b, kind, index):
        if index == 0:
            return ref[b, kind, :, :width]
        line = ref[b, kind, :, width : 2 * width]
        if index == 2:
            line = pltpu.roll(line, width // 2, 1)
        lane = lax.broadcasted_iota(jnp.int32, line.shape, 1)
        return jnp.where(lane < width >> index, line, 0.0)

    for b in range(crops):
        partial, weights = [], []
        for index, (padded, own, lines) in enumerate(plan):
            rows = [
                values[b, :, line * width : (line + 1) * width]
                for line in range(padded, padded + lines + 2)
            ]
            rows[0] = rows[0] + came(above, b, 0, index)
            rows[1] = rows[1] + came(above, b, 1, index)
            rows[lines] = rows[lines] + came(below, b, 1, index)
            rows[lines + 1] = rows[lines + 1] + came(below, b, 0, index)
            partial += rows
            weights += [
                came(above, b, 2, index),
                mask[b, :, own * width : (own + lines) * width],
                came(below, b, 2, index),
            ]
        mismatch = jnp.concatenate(partial, axis=1)
        weight = jnp.concatenate(weights, axis=1)
        magnitude = jnp.abs(mismatch)
        losses = weight * jnp.where(
            magnitude < box_beta, 0.5 * mismatch * mismatch / box_beta, magnitude - 0.5 * box_beta
        )
        for padded, own, lines in plan:
            for line in range(padded + 1, padded + 1 + lines):
                summed = summed + losses[:, line * width : (line + 1) * width]
        middle = weight * jnp.clip(mismatch / box_beta, -1.0, 1.0) * inverse
        middle = middle.astype(bf16).astype(f32)
        shifted = [turned(middle, -1, 1, width), middle, turned(middle, 1, 1, width)]
        for i in range(3):
            for j in range(3):
                for padded, own, lines in plan:
                    at = (padded + 2 - i) * width
                    taps[
                        (3 * i + j) * DELTA_ROWS : (3 * i + j + 1) * DELTA_ROWS,
                        own * width : (own + lines) * width,
                    ] = shifted[j][:, at : at + lines * width].astype(bf16)
        around = taps[...]
        lines_all = levels.shape[1]
        total_grad = total_grad + dot(around, levels[b].reshape(lines_all * width, channels))
        back = dot(around, head[...], ((0,), (0,))).reshape(lines_all, width, channels)
        rounded = back[:height].astype(bf16)
        grad_four[b] = rounded
        first[b, :width] = rounded[0]
        last[b, :width] = rounded[height - 1]
        for q in range(low_height // 2):
            up = doubled_columns(wide, back[height + low_height + q, : low_width // 2])
            for row in (2 * q, 2 * q + 1):
                low = (back[height + row, :low_width] + 0.25 * up).astype(bf16)
                grad_five[b, row] = low
                if row == 0:
                    first[b, width:] = low
                if row == low_height - 1:
                    last[b, width:] = low
    swapped(first, last, pair, other, True)
    head_grad[...] = total_grad
    loss[0, 0] = jnp.sum(summed)


def conv_grad_kernel(n_rows, input_four, input_five, pair_in, other_in, grad_four, grad_five, *refs):
    outs, (turned_rows, sums_four, sums_five, above, below) = refs[:-5], refs[-5:]
    swapped(above, below, pair_in, other_in, False)
    crops, height, width, channels = input_four.shape
    low_height, low_width = input_five.shape[1:3]
    padding = jnp.zeros((width - low_width, channels), bf16)
    for own, grad, edge, sums in (
        (input_four, grad_four, 0, sums_four),
        (input_five, grad_five, width, sums_five),
    ):
        lines, extent = own.shape[1:3]

        def widened(row):
            if extent == width:
                return row
            return jnp.concatenate([row, padding], axis=0)

        for b in range(crops):
            for r in range(lines + 2):
                if r == 0:
                    row = above[b, edge : edge + extent]
                elif r == lines + 1:
                    row = below[b, edge : edge + extent]
                else:
                    row = own[b, r - 1]
                turned_rows[:, r * width : (r + 1) * width] = widened(row).T
            left = jnp.concatenate(
                [turned_rows[:, i * width : (i + lines) * width] for i in range(3)], axis=0
            )
            middle = jnp.concatenate([widened(grad[b, r]) for r in range(lines)], axis=0)
            wide = middle.astype(f32)
            right = jnp.concatenate(
                [
                    turned(wide, -1, 0, width).astype(bf16),
                    middle,
                    turned(wide, 1, 0, width).astype(bf16),
                ],
                axis=1,
            )
            for i in range(3):
                product = dot(left[i * channels : (i + 1) * channels], right)
                for j in range(3):
                    at = slice((3 * i + j) * channels, (3 * i + j + 1) * channels)
                    block = product[:, j * channels : (j + 1) * channels]
                    if b == 0:
                        sums[at, :] = block
                    else:
                        sums[at, :] += block
    me = lax.axis_index("rows")
    part = 9 * channels // n_rows
    low = len(outs)
    for index in range(n_rows):
        at = pl.ds(pl.multiple_of((index ^ me) * part, part), part)
        out, j = outs[index % low], index // low
        out[j, :, :channels] = sums_four[at, :].astype(bf16)
        out[j, :, channels:] = sums_five[at, :].astype(bf16)


def merged_grad_kernel(grad_four, grad_five, pair_in, other_in, kernel_four, kernel_five, *refs):
    lat_four, lat_five, spread_four, spread_five, fold, above, below = refs
    swapped(above, below, pair_in, other_in, False)
    crops, height, width, channels = grad_four.shape
    low_height, low_width = grad_five.shape[1:3]
    fill_padded(spread_four, grad_four, above, below, 0)
    fill_padded(spread_five, grad_five, above, below, width)
    rows = 4
    for b in range(crops):
        low = three_taps(spread_five, b, 0, low_height, kernel_five, -1)
        low = low.reshape(low_height, low_width, channels)
        for r in range(0, height, rows):
            back = three_taps(spread_four, b, r, rows, kernel_four, -1)
            at = (b * height + r) * width
            lat_four[at : at + rows * width, :] = back.astype(bf16)
            for h in range(0, channels, LANES):
                fold[...] = back[:, h : h + LANES]
                for q in range(rows // 2):
                    total = low[r // 2 + q, :, h : h + LANES]
                    folded = jnp.zeros_like(total)
                    for line in (2 * q * width, (2 * q + 1) * width):
                        for side in range(2):
                            folded = folded + fold[pl.ds(line + side, low_width, stride=2), :]
                    at_low = (b * low_height + r // 2 + q) * low_width
                    lat_five[at_low : at_low + low_width, h : h + LANES] = (total + folded).astype(bf16)


def section_grad_kernel(n_rows, n_batch, deltas, own, four, five, lat_four, lat_five, head_grad, loss, kept, *refs):
    outs, (sums_four, sums_five, flat) = refs[:-3], refs[-3:]
    crops, height, width, depth = four.shape
    low_height, low_width, low_depth = five.shape[1:]
    me = lax.axis_index("rows")
    part_four, part_five = depth // n_rows, low_depth // n_rows
    positions = crops * height * width
    low_positions = crops * low_height * low_width
    turned_four = lat_four[...].T
    turned_five = lat_five[...].T
    step = 256
    for at in range(0, depth, step):
        block = four[:, :, :, at : at + step].reshape(positions, step)
        sums_four[at : at + step, :] = dot(turned_four, block).T
    for at in range(0, low_depth, step):
        block = five[:, :, :, at : at + step].reshape(low_positions, step)
        sums_five[at : at + step, :] = dot(turned_five, block).T
    channels = head_grad.shape[1]
    flat[:, 9 * channels :] = jnp.zeros((DELTA_ROWS, flat.shape[1] - 9 * channels), f32)
    for t in range(9):
        flat[:, t * channels : (t + 1) * channels] = head_grad[
            t * DELTA_ROWS : (t + 1) * DELTA_ROWS, :
        ]
    line = lax.broadcasted_iota(jnp.int32, (DELTA_ROWS, LANES), 0)
    lane = lax.broadcasted_iota(jnp.int32, (DELTA_ROWS, LANES), 1)
    spot = (line - deltas) * LANES + lane - 3 * (me * n_batch + lax.axis_index("batch"))
    place = jnp.zeros((DELTA_ROWS, LANES), f32)
    for piece, value in enumerate(pieces_of(jnp.full(place.shape, loss[0, 0], f32))):
        place = jnp.where((line >= deltas) & (spot == piece), value, place)
    high = kept.shape[0]
    low = n_rows // high
    for index in range(n_rows):
        k, j = index % low, index // low
        out = kept.at[j] if k == 0 else outs[k - 1].at[j]
        owner = index ^ me
        at = pl.ds(pl.multiple_of(owner * part_four, part_four), part_four)
        out[:part_four, :] = sums_four[at, :].astype(bf16)
        at = pl.ds(pl.multiple_of(owner * part_five, part_five), part_five)
        out[part_four : part_four + part_five, :] = sums_five[at, :].astype(bf16)
        pieces = []
        for z in range(n_batch):
            start = (owner * n_batch + z) * own
            at = pl.ds(pl.multiple_of(start // LANES * LANES, LANES), 2 * LANES)
            square = pltpu.roll(flat[:, at], (2 * LANES - start % LANES) % (2 * LANES), 1)[:, :LANES]
            square = jnp.where((line < deltas) & (lane < own), square, place)
            pieces.append(joined(square))
        out[part_four + part_five :, :] = jnp.concatenate(pieces, axis=0).astype(bf16)


def adamw_into(outs, weight, gradient, mean, square):
    for out, value in zip(outs, adamw_update(weight, gradient, mean, square)):
        out[...] = value


def conv_step_kernel(count, own, *refs):
    came, (weight, mean, square, first, second, new) = refs[:count], refs[count:]
    channels = weight.shape[2]
    total = own[...]
    for piece in came:
        total = total + piece[...].astype(f32)
    for k in range(2):
        adamw_into(
            (first.at[k], second.at[k], new.at[k]),
            weight[k],
            total[:, k * channels : (k + 1) * channels],
            mean[k],
            square[k],
        )


def lateral_step_kernel(count, own, *refs):
    came, inputs, outs, loss = refs[:count], refs[count : count + 9], refs[count + 9 : -1], refs[-1]
    total = own[...]
    for piece in came:
        total = total + piece[...].astype(f32)
    lines = inputs[0].shape[0]
    deltas, rows = inputs[6].shape
    square = parted(total[total.shape[0] - 8 :])
    gradients = (total[:lines], total[lines : total.shape[0] - 8], square[:deltas, :rows])
    for k, gradient in enumerate(gradients):
        weight, mean, second = (ref[...] for ref in inputs[3 * k : 3 * k + 3])
        adamw_into(outs[3 * k : 3 * k + 3], weight, gradient, mean, second)
    line = lax.broadcasted_iota(jnp.int32, square.shape, 0)
    loss[0, 0] = jnp.sum(jnp.where(line >= deltas, square, 0.0))


def on_device(
    section_four,
    section_five,
    target_four,
    target_five,
    target_six,
    anchor_four,
    anchor_five,
    anchor_six,
    lateral_four,
    lateral_five,
    output_conv,
    delta_head,
    mean_four,
    mean_five,
    mean_conv,
    mean_head,
    square_four,
    square_five,
    square_conv,
    square_head,
):
    n_rows, n_batch = lax.axis_size("rows"), lax.axis_size("batch")
    _, low_group, high_group = row_groups()
    crops, height, width, depth = section_four.shape
    low_height, low_width, low_depth = section_five.shape[1:]
    four_n, five_n, conv_n = lateral_four.shape[0], lateral_five.shape[0], output_conv.shape[1]
    channels, deltas = delta_head.shape[0] * n_rows * n_batch // 9, delta_head.shape[1]
    shape = jax.ShapeDtypeStruct

    flat = [jnp.transpose(a, (0, 3, 1, 2)) for a in (anchor_four, anchor_five, anchor_six)]
    sources = [lateral_four, lateral_five, delta_head.T, *flat]
    (lateral,) = call(
        pack_kernel,
        "pack",
        sources,
        [shape((four_n + five_n + 8, channels), bf16)],
        [pltpu.VMEM((DELTA_ROWS, LANES), f32)]
        + [pltpu.VMEM(v.shape, v.dtype) for v in sources]
        + [pltpu.SemaphoreType.DMA((len(sources),))],
        apart=len(sources),
    )
    parts = gathered_batch(lateral)
    lateral = jnp.concatenate(
        [p[:four_n] for p in parts]
        + [p[four_n : four_n + five_n] for p in parts]
        + [p[four_n + five_n :] for p in parts]
    )
    laterals = gathered_high(lateral)

    conv = jnp.concatenate([output_conv[0], output_conv[1]], axis=1).astype(bf16)
    conv, _ = lax.optimization_barrier((conv, lateral))
    conv = jnp.concatenate(gathered_batch(conv))

    lines = height + low_height + low_height // 2
    flat, _ = lax.optimization_barrier(
        (
            [
                jnp.transpose(t, (0, 3, 1, 2))
                for t in (
                    target_four,
                    target_five,
                    target_six,
                    anchor_four,
                    anchor_five,
                    anchor_six,
                )
            ],
            lateral,
        )
    )
    target, mask = call(
        planes_kernel,
        "planes",
        [*flat, section_four, section_five],
        [shape((crops, DELTA_ROWS, lines * LANES), f32)] * 2,
    )
    laterals, target, mask = lax.optimization_barrier((laterals, target, mask))
    laterals = gathered_low(laterals)
    convs = gathered_high(conv)

    edge = width + low_width
    input_rims = [pltpu.VMEM((crops, edge, channels), bf16)] * 2
    head_rims = [pltpu.VMEM((crops, 3, DELTA_ROWS, 2 * width), f32)] * 2
    input_four, input_five, pair, other = call(
        functools.partial(lateral_kernel, n_rows),
        "laterals",
        [section_four, section_five, *laterals],
        [
            shape((crops, height, width, channels), bf16),
            shape((crops, low_height, low_width, channels), bf16),
            shape((crops, edge, channels), bf16),
            shape((crops, edge, channels), bf16),
        ],
        [
            pltpu.VMEM((depth, channels), bf16),
            pltpu.VMEM((low_depth, channels), bf16),
            pltpu.VMEM((channels // LANES, width, LANES), f32),
        ]
        + input_rims,
        flops=2 * crops * channels * (height * width * depth + low_height * low_width * low_depth),
    )
    pair_in, other_in = from_neighbours(pair, other)
    convs, pair_in, other_in = lax.optimization_barrier((convs, pair_in, other_in))
    convs = gathered_low(convs)

    conv_flops = 18 * crops * channels * channels * (height * width + low_height * low_width)
    head, count = call(
        functools.partial(head_weights_kernel, n_rows, n_batch, deltas, conv_n),
        "head_weights",
        laterals,
        [shape((9 * DELTA_ROWS, channels), bf16), shape((1, 1), f32)],
        [pltpu.VMEM((DELTA_ROWS, 9 * channels + 2 * LANES), f32)],
        scalar_outs=1,
    )
    levels, values, pair, other, kernel_four, kernel_five = call(
        functools.partial(output_kernel, n_rows),
        "outputs",
        [input_four, input_five, pair_in, other_in, head, target, mask, *convs],
        [
            shape((crops, lines, width, channels), bf16),
            shape((crops, DELTA_ROWS, (lines + 6) * width), f32),
            shape((crops, 3, DELTA_ROWS, 2 * width), f32),
            shape((crops, 3, DELTA_ROWS, 2 * width), f32),
            shape((9 * channels, channels), bf16),
            shape((9 * channels, channels), bf16),
        ],
        [
            pltpu.VMEM((crops, height + 2, width, channels), bf16),
            pltpu.VMEM((crops, low_height + 2, low_width, channels), bf16),
            pltpu.VMEM((low_height * low_width, LANES), f32),
        ]
        + input_rims
        + head_rims,
        flops=conv_flops,
    )
    pair, other = from_neighbours(pair, other)

    head_flops = 18 * DELTA_ROWS * crops * lines * width * channels
    head_grad, grad_four, grad_five, pair, other, loss = call(
        functools.partial(head_kernel, height),
        "heads",
        [levels, pair, other, head, values, mask, count],
        [
            shape((9 * DELTA_ROWS, channels), f32),
            shape((crops, height, width, channels), bf16),
            shape((crops, low_height, low_width, channels), bf16),
            shape((crops, edge, channels), bf16),
            shape((crops, edge, channels), bf16),
            shape((1, 1), f32),
        ],
        [
            pltpu.VMEM((9 * DELTA_ROWS, lines * width), bf16),
            pltpu.VMEM((channels // LANES, low_width, LANES), f32),
        ]
        + head_rims
        + input_rims,
        flops=3 * head_flops,
        scalars=1,
        scalar_outs=1,
    )
    pair, other = from_neighbours(pair, other)

    conv_width = 2 * channels
    conv_blocks = call(
        functools.partial(conv_grad_kernel, n_rows),
        "conv_grads",
        [input_four, input_five, pair_in, other_in, grad_four, grad_five],
        [shape((high_group, n_batch * conv_n, conv_width), bf16)] * low_group,
        [
            pltpu.VMEM((channels, (height + 2) * width), bf16),
            pltpu.VMEM((9 * channels, channels), f32),
            pltpu.VMEM((9 * channels, channels), f32),
        ]
        + input_rims,
        flops=conv_flops,
    )

    positions, low_positions = crops * height * width, crops * low_height * low_width
    conv_blocks, pair, other = lax.optimization_barrier((conv_blocks, pair, other))
    conv_partial = summed_low(conv_blocks)
    pair, other, conv_partial = lax.optimization_barrier((pair, other, conv_partial))
    lat_four, lat_five = call(
        merged_grad_kernel,
        "merged_grads",
        [grad_four, grad_five, pair, other, kernel_four, kernel_five],
        [shape((positions, channels), bf16), shape((low_positions, channels), bf16)],
        [
            pltpu.VMEM((crops, height + 2, width, channels), bf16),
            pltpu.VMEM((crops, low_height + 2, low_width, channels), bf16),
            pltpu.VMEM((4 * width, LANES), f32),
        ]
        + input_rims,
        flops=conv_flops,
    )
    conv_sum = summed_high(conv_partial)

    lateral_n = four_n + five_n + 8
    lateral_kept, *lateral_moved = call(
        functools.partial(section_grad_kernel, n_rows, n_batch, deltas, conv_n),
        "lateral_grads",
        [section_four, section_five, lat_four, lat_five, head_grad, loss],
        [shape((high_group, n_batch * lateral_n, channels), bf16)] * low_group,
        [
            pltpu.VMEM((depth, channels), f32),
            pltpu.VMEM((low_depth, channels), f32),
            pltpu.VMEM((DELTA_ROWS, 9 * channels + 2 * LANES), f32),
        ],
        flops=1,
        scalars=1,
    )
    lateral_moved, conv_sum = lax.optimization_barrier((lateral_moved, conv_sum))
    lateral_partial = summed_low([lateral_kept, *lateral_moved])
    lateral_sum = summed_high(lateral_partial)
    conv_shares = shared_batch(conv_sum.reshape(n_batch, conv_n, conv_width))
    conv_shares, lateral_sum = lax.optimization_barrier((conv_shares, lateral_sum))
    first_conv, second_conv, weight_conv = call(
        functools.partial(conv_step_kernel, n_batch - 1),
        "conv_step",
        [*conv_shares, output_conv, mean_conv, square_conv],
        [shape(output_conv.shape, f32)] * 3,
    )
    ends = (n_batch * four_n, n_batch * (four_n + five_n))
    lateral_sum = jnp.concatenate(
        [
            part.reshape(n_batch, -1, channels)
            for part in (
                lateral_sum[: ends[0]],
                lateral_sum[ends[0] : ends[1]],
                lateral_sum[ends[1] :],
            )
        ],
        axis=1,
    )
    turned_head = [v.T for v in (delta_head, mean_head, square_head)]
    outs = call(
        functools.partial(lateral_step_kernel, n_batch - 1),
        "lateral_step",
        [
            *shared_batch(lateral_sum),
            lateral_four,
            mean_four,
            square_four,
            lateral_five,
            mean_five,
            square_five,
            *turned_head,
        ],
        [shape(lateral_four.shape, f32)] * 3
        + [shape(lateral_five.shape, f32)] * 3
        + [shape(turned_head[0].shape, f32)] * 3
        + [shape((1, 1), f32)],
        scalar_outs=1,
    )
    first_four, second_four, weight_four, first_five, second_five, weight_five = outs[:6]
    first_head, second_head, weight_head = (v.T for v in outs[6:9])
    loss_sum = outs[9]
    return (
        loss_sum[0, 0],
        count[0, 0],
        first_four,
        first_five,
        first_conv,
        first_head,
        second_four,
        second_five,
        second_conv,
        second_head,
        weight_four,
        weight_five,
        weight_conv,
        weight_head,
    )


def solution(mesh):
    split = P("batch", "rows", None, None)
    whole, pair = P(("rows", "batch"), None), P(None, ("rows", "batch"), None)
    weights = (whole, whole, pair, whole)
    return jax.shard_map(
        on_device,
        mesh=mesh,
        in_specs=(split,) * 8 + weights * 3,
        out_specs=(P(), P()) + weights * 3,
        check_vma=False,
    )
```

```python
import functools
import math

import jax
import jax.numpy as jnp
from jax import lax
from jax.experimental import pallas as pl
from jax.experimental.pallas import tpu as pltpu
from jax.sharding import PartitionSpec as P

STEP = 5

LANES = 128
DELTA_ROWS = 16
SPARE_BYTES = 12 * 1024 * 1024
ALL_BYTES = 60 * 1024 * 1024

box_beta = 1.0 / 9.0
beta_one = 0.5
beta_two = 0.5
learn_rate = 0.02
weight_decay = 0.01
epsilon = 1e-08

bf16 = jnp.bfloat16
f32 = jnp.float32


def adamw_update(weight, gradient, mean, square):
    first = beta_one * mean + (1.0 - beta_one) * gradient
    second = beta_two * square + (1.0 - beta_two) * gradient * gradient
    corrected_first = first / (1.0 - beta_one**STEP)
    corrected_second = second / (1.0 - beta_two**STEP)
    return (
        first,
        second,
        weight
        - learn_rate
        * (corrected_first / (jnp.sqrt(corrected_second) + epsilon) + weight_decay * weight),
    )


def sent(value, axis, mask):
    count = lax.axis_size(axis)
    return lax.ppermute(value, axis, [(i, i ^ mask) for i in range(count)])


def gathered_batch(piece):
    count, me = lax.axis_size("batch"), lax.axis_index("batch")
    stacked = jnp.stack([piece] + [sent(piece, "batch", k) for k in range(1, count)])
    return [lax.dynamic_index_in_dim(stacked, t ^ me, 0, keepdims=False) for t in range(count)]


def row_groups():
    count = lax.axis_size("rows")
    low = max(count // 4, 1)
    return count, low, count // low


def gathered_high(piece):
    _, low, high = row_groups()
    return [piece] + [sent(piece, "rows", j * low) for j in range(1, high)]


def gathered_low(held):
    count, low, high = row_groups()
    result = [None] * count
    for j in range(high):
        result[j * low] = held[j]
        for k in range(1, low):
            result[j * low + k] = sent(held[j], "rows", k)
    return result


def summed_low(blocks):
    _, low, high = row_groups()
    came = []
    for k in range(1, low):
        whole = isinstance(blocks[k], jax.Array)
        came.append(
            sent(blocks[k], "rows", k) if whole else [sent(block, "rows", k) for block in blocks[k]]
        )
    return [
        sum((c[j].astype(f32) for c in came), blocks[0][j].astype(f32)) for j in range(high)
    ]


def sent_high(partial):
    _, low, high = row_groups()
    return [sent(partial[j].astype(bf16), "rows", j * low) for j in range(1, high)]


def shared_batch(blocks):
    count, me = lax.axis_size("batch"), lax.axis_index("batch")
    own = lax.dynamic_index_in_dim(blocks, me, 0, keepdims=False)
    came = []
    for k in range(1, count):
        block = lax.dynamic_index_in_dim(blocks, me ^ k, 0, keepdims=False).astype(bf16)
        came.append(sent(block, "batch", k))
    return [own, *came]


def from_neighbours(pair, other):
    count = lax.axis_size("rows")
    links = [(i, i + 1) for i in range(1, count - 1, 2)]
    return sent(pair, "rows", 1), lax.ppermute(other, "rows", links + [(j, i) for i, j in links])


def call(kernel, name, args, outs, scratch=(), flops=0, scalars=0, scalar_outs=0, apart=0):
    vmem, smem = pl.BlockSpec(memory_space=pltpu.VMEM), pl.BlockSpec(memory_space=pltpu.SMEM)
    hbm = pl.BlockSpec(memory_space=pltpu.HBM)
    size = sum(a.size * a.dtype.itemsize for a in (*args, *outs))
    held = sum(
        math.prod(ref.shape) * jnp.dtype(ref.dtype).itemsize
        for ref in scratch
        if ref.memory_space == pltpu.VMEM
    )
    return pl.pallas_call(
        kernel,
        out_shape=list(outs),
        in_specs=[hbm] * apart + [vmem] * (len(args) - scalars - apart) + [smem] * scalars,
        out_specs=[vmem] * (len(outs) - scalar_outs) + [smem] * scalar_outs,
        scratch_shapes=list(scratch),
        compiler_params=pltpu.CompilerParams(vmem_limit_bytes=ALL_BYTES if apart else held + SPARE_BYTES),
        cost_estimate=pl.CostEstimate(flops=flops, bytes_accessed=size, transcendentals=0),
        name=name,
    )(*args)


def swapped(upper, lower, pair, other, outward):
    odd = lax.axis_index("rows") % 2 == 1

    def move(one, two):
        for ref, side in ((one, pair), (two, other)):
            if outward:
                side[...] = ref[...]
            else:
                ref[...] = side[...]

    pl.when(odd)(lambda: move(upper, lower))
    pl.when(jnp.logical_not(odd))(lambda: move(lower, upper))


def dot(left, right, dims=((1,), (0,))):
    return lax.dot_general(left, right, (dims, ((), ())), preferred_element_type=f32)


def turned(value, step, axis, width):
    size = value.shape[axis]
    column = lax.broadcasted_iota(jnp.int32, value.shape, axis) % width
    rolled = pltpu.roll(value, step % size, axis)
    return jnp.where(column == (0 if step == 1 else width - 1), 0.0, rolled)


def doubled_columns(ref, row):
    count = row.shape[0]
    for h in range(ref.shape[0]):
        part = row[:, h * LANES : (h + 1) * LANES]
        ref[h, pl.ds(0, count, stride=2), :] = part
        ref[h, pl.ds(1, count, stride=2), :] = part
    return jnp.concatenate([ref[h] for h in range(ref.shape[0])], axis=1)


def pieces_of(value):
    high = value.astype(bf16).astype(f32)
    middle = (value - high).astype(bf16).astype(f32)
    return high, middle, value - high - middle


def pack_kernel(*refs):
    sources, packed, square, held, arrived = refs[:6], refs[6], refs[7], refs[8:14], refs[14]
    copies = [
        pltpu.make_async_copy(source, target, arrived.at[k])
        for k, (source, target) in enumerate(zip(sources, held))
    ]
    for copy in copies:
        copy.start()
    for copy in copies:
        copy.wait()
    four, five, head, anchor_four, anchor_five, anchor_six = held
    lines = four.shape[0] + five.shape[0]
    packed[: four.shape[0]] = four[...].astype(bf16)
    packed[four.shape[0] : lines] = five[...].astype(bf16)
    total = jnp.zeros((1, 1), f32)
    for anchor in (anchor_four, anchor_five, anchor_six):
        total = total + jnp.sum(anchor[...].astype(f32), keepdims=True).reshape(1, 1)
    square[...] = jnp.zeros_like(square)
    square[: head.shape[0], : head.shape[1]] = head[...]
    spare = square[...]
    line = lax.broadcasted_iota(jnp.int32, spare.shape, 0)
    lane = lax.broadcasted_iota(jnp.int32, spare.shape, 1)
    for k, piece in enumerate(pieces_of(jnp.broadcast_to(total, spare.shape))):
        spare = jnp.where((line == head.shape[0]) & (lane == k), piece, spare)
    packed[lines:] = joined(spare).astype(bf16)


def joined(square):
    return jnp.concatenate([square[:8], square[8:]], axis=1)


def parted(lines):
    return jnp.concatenate([lines[:, :LANES], lines[:, LANES:]], axis=0)


def head_weights_kernel(n_rows, n_batch, deltas, own, *refs):
    pieces, (head, count, flat) = refs[:n_rows], refs[n_rows:]
    channels = head.shape[1]
    me = lax.axis_index("rows")
    flat[...] = jnp.zeros_like(flat)
    line = lax.broadcasted_iota(jnp.int32, (DELTA_ROWS, LANES), 0)
    total = jnp.zeros((DELTA_ROWS, LANES), f32)
    for k in range(n_rows):
        lines = pieces[k][pieces[k].shape[0] - 8 * n_batch :].astype(f32)
        for z in range(n_batch):
            square = parted(lines[8 * z : 8 * z + 8])
            total = total + jnp.where(line >= deltas, square, 0.0)
            square = jnp.where(line < deltas, square, 0.0)
            place = ((me ^ k) * n_batch + z) * own
            wide = jnp.concatenate([square, jnp.zeros_like(square)], axis=1)
            wide = pltpu.roll(wide, place % LANES, 1)
            at = pl.ds(pl.multiple_of(place // LANES * LANES, LANES), 2 * LANES)
            flat[:, at] += wide
    for t in range(9):
        block = flat[:, t * channels : (t + 1) * channels].astype(bf16)
        head[t * DELTA_ROWS : (t + 1) * DELTA_ROWS, :] = block
    count[0, 0] = jnp.sum(total)


def planes_kernel(*refs):
    targets, anchors, (target, mask) = refs[:3], refs[3:6], refs[-2:]
    crops, deltas = targets[0].shape[:2]
    own = 0
    target[:, deltas:, :] = jnp.zeros((crops, target.shape[1] - deltas, target.shape[2]), f32)
    mask[:, deltas:, :] = jnp.zeros((crops, mask.shape[1] - deltas, mask.shape[2]), f32)
    for target_ref, anchor_ref in zip(targets, anchors):
        _, count, lines, width = anchor_ref.shape
        share = deltas // count
        for b in range(crops):
            for r in range(lines):
                at, rest = own + r * LANES, LANES - width
                target[b, :deltas, at : at + width] = target_ref[b, :, r, :]
                if rest:
                    target[b, :deltas, at + width : at + LANES] = jnp.zeros((deltas, rest), f32)
                    mask[b, :deltas, at + width : at + LANES] = jnp.zeros((deltas, rest), f32)
                for a in range(count):
                    row = anchor_ref[b, a, r : r + 1, :].astype(f32)
                    mask[b, a * share : (a + 1) * share, at : at + width] = jnp.broadcast_to(
                        row, (share, width)
                    )
        own += lines * LANES


def lateral_kernel(n_rows, four, five, *refs):
    pieces, rest = refs[:n_rows], refs[n_rows:]
    input_four, input_five, pair, other, kernel_four, kernel_five, wide, first, last = rest[1:]
    mask = rest[0]
    crops, height, width, depth = four.shape
    low_height, low_width = five.shape[1:3]
    me = lax.axis_index("rows")
    part_four, part_five = depth // n_rows, five.shape[3] // n_rows
    for k in range(n_rows):
        owner = me ^ k
        at_four = pl.multiple_of(owner * part_four, part_four)
        at_five = pl.multiple_of(owner * part_five, part_five)
        kernel_four[pl.ds(at_four, part_four), :] = pieces[k][:part_four]
        kernel_five[pl.ds(at_five, part_five), :] = pieces[k][part_four : part_four + part_five]
    for b in range(crops):
        low = dot(five[b].reshape(low_height * low_width, -1), kernel_five[...])
        low_rounded = low.astype(bf16).reshape(low_height, low_width, -1)
        input_five[b] = low_rounded
        first[b, width : width + low_width] = low_rounded[0]
        last[b, width : width + low_width] = low_rounded[low_height - 1]
        for q in range(low_height):
            up = doubled_columns(wide, low[q * low_width : (q + 1) * low_width])
            rows = four[b, 2 * q : 2 * q + 2].reshape(2 * width, depth)
            merged = dot(rows, kernel_four[...]).reshape(2, width, -1) + up[None]
            rounded = merged.astype(bf16)
            input_four[b, 2 * q : 2 * q + 2] = rounded
            if q == 0:
                first[b, :width] = rounded[0]
            if q == low_height - 1:
                last[b, :width] = rounded[1]
        edge, half = width + low_width, width // 2
        lane = lax.broadcasted_iota(jnp.int32, (DELTA_ROWS, width), 1)
        plan = level_rows(height, 1)
        for ref, end in ((first, 0), (last, 1)):
            lines = []
            for _, own, count in plan:
                at = (own + (count - 1) * end) * width
                lines.append(mask[b, :, at : at + width])
            small = jnp.where(lane < half, lines[1], pltpu.roll(lines[2], half, 1))
            ref[b, edge:, :width] = lines[0].astype(bf16)
            ref[b, edge:, width:] = small.astype(bf16)
    swapped(first, last, pair, other, True)


def three_taps(source, b, start, rows, weights, step):
    width, channels = source.shape[2:]
    parts = []
    for j in range(3):
        taps = range(3) if step == 1 else (2, 1, 0)
        left = jnp.concatenate(
            [
                source[b, start + i : start + i + rows].reshape(rows * width, channels)
                for i in range(3)
            ],
            axis=1,
        )
        blocks = [weights[(3 * i + j) * channels : (3 * i + j + 1) * channels] for i in taps]
        if step == 1:
            parts.append(dot(left, jnp.concatenate(blocks, axis=0)))
        else:
            parts.append(dot(left, jnp.concatenate(blocks, axis=1), ((1,), (1,))))
    return parts[1] + turned(parts[0], step, 0, width) + turned(parts[2], -step, 0, width)


def fill_padded(padded, own, above, below, start):
    height, width = own.shape[1:3]
    for b in range(own.shape[0]):
        padded[b, 0] = above[b, start : start + width]
        padded[b, 1 : height + 1] = own[b]
        padded[b, height + 1] = below[b, start : start + width]


def output_kernel(n_rows, deltas, input_four, input_five, pair_in, other_in, head, target, mask, *refs):
    pieces, rest = refs[:n_rows], refs[n_rows:]
    levels, values, pair, other, kernel_four, kernel_five = rest[:6]
    spread_four, spread_five, spare, above, below, first, last = rest[6:]
    swapped(above, below, pair_in, other_in, False)
    crops, height, width, channels = input_four.shape
    low_height, low_width = input_five.shape[1:3]
    me = lax.axis_index("rows")
    part = 9 * channels // n_rows
    for k in range(n_rows):
        at = pl.multiple_of((me ^ k) * part, part)
        kernel_four[pl.ds(at, part), :] = pieces[k][:, :channels]
        kernel_five[pl.ds(at, part), :] = pieces[k][:, channels:]
    fill_padded(spread_four, input_four, above, below, 0)
    fill_padded(spread_five, input_five, above, below, width)
    low_start, top_start = height, height + low_height
    half = width // 2
    levels[:, low_start:, half:, :] = jnp.zeros(
        (crops, levels.shape[1] - low_start, width - half, channels), bf16
    )
    quarter = low_width // 2
    levels[:, top_start:, quarter:, :] = jnp.zeros(
        (crops, levels.shape[1] - top_start, width - quarter, channels), bf16
    )
    rows = 4
    for b in range(crops):
        low = three_taps(spread_five, b, 0, low_height, kernel_five, 1)
        low_rounded = low.astype(bf16).reshape(low_height, low_width, channels)
        levels[b, low_start:top_start, :low_width, :] = low_rounded
        for h in range(0, channels, LANES):
            spare[: low_height * low_width, :] = low[:, h : h + LANES]
            for q in range(low_height // 2):
                total = jnp.zeros((quarter, LANES), f32)
                for at in (2 * q * low_width, (2 * q + 1) * low_width):
                    for side in range(2):
                        total = total + spare[pl.ds(at + side, quarter, stride=2), :]
                pooled = (0.25 * total).astype(bf16)
                levels[b, top_start + q, :quarter, h : h + LANES] = pooled
        for r in range(0, height, rows):
            sums = three_taps(spread_four, b, r, rows, kernel_four, 1)
            rounded = sums.astype(bf16).reshape(rows, width, channels)
            levels[b, r : r + rows] = rounded
        lines_all = levels.shape[1]
        products = dot(
            head[...], levels[b].reshape(lines_all * width, channels), ((1,), (1,))
        )
        none = jnp.zeros((products.shape[0], 2 * width), f32)
        columns = []
        for j in range(3):
            pieces = []
            for _, own, count_lines in level_rows(height, 1):
                padded = jnp.concatenate(
                    [none, products[:, own * width : (own + count_lines) * width], none], axis=1
                )
                total = jnp.zeros((DELTA_ROWS, (count_lines + 2) * width), f32)
                for i in range(3):
                    tap = (3 * i + j) * DELTA_ROWS
                    at = slice(i * width, (i + count_lines + 2) * width)
                    total = total + padded[tap : tap + DELTA_ROWS, at]
                pieces.append(total)
            columns.append(jnp.concatenate(pieces, axis=1))
        sums = columns[1] + turned(columns[0], 1, 1, width) + turned(columns[2], -1, 1, width)
        for index, (padded, own, count_lines) in enumerate(level_rows(height, 1)):
            own_at = slice(own * width, (own + count_lines) * width)
            start, end = padded * width, (padded + count_lines + 2) * width
            partial = sums[:, start + width : end - width] - target[b, :, own_at]
            values[b, :, start : start + width] = sums[:, start : start + width]
            values[b, :, start + width : end - width] = partial
            values[b, :, end - width : end] = sums[:, end - width : end]
            upper = (partial[:, :width], sums[:, start : start + width])
            lower = (partial[:, (count_lines - 1) * width :], sums[:, end - width : end])
            for out, values_of in ((first, upper), (last, lower)):
                for kind, line in enumerate(values_of):
                    lines, line = slice(kind * deltas, (kind + 1) * deltas), line[:deltas]
                    if index < 2:
                        out[b, lines, index * width : (index + 1) * width] = line
                    else:
                        moved = pltpu.roll(line, half, 1)
                        lane = lax.broadcasted_iota(jnp.int32, line.shape, 1)
                        mixed = jnp.where(lane < half, out[b, lines, width : 2 * width], moved)
                        out[b, lines, width : 2 * width] = mixed
    swapped(first, last, pair, other, True)


def level_rows(height, rim):
    result, padded, own = [], 0, 0
    for count in (height, height // 2, height // 4):
        result.append((padded, own, count))
        padded, own = padded + count + 2 * rim, own + count
    return result


def head_kernel(height, deltas, levels, pair_in, other_in, pair_mask, other_mask, head, values, mask, count, *refs):
    head_grad, grad_four, grad_five, pair, other, loss = refs[:6]
    taps, wide, above, below, first, last, mask_above, mask_below = refs[6:]
    swapped(above, below, pair_in, other_in, False)
    swapped(mask_above, mask_below, pair_mask, other_mask, False)
    edge = first.shape[1]
    crops, _, width, channels = levels.shape
    inverse = 1.0 / jnp.maximum(count[0, 0], 1.0)
    plan = level_rows(height, 1)
    summed = jnp.zeros((DELTA_ROWS, LANES), f32)
    total_grad = jnp.zeros((9 * DELTA_ROWS, channels), f32)
    low_height, low_width = height // 2, width // 2
    def small_level(line, index):
        if index == 2:
            line = pltpu.roll(line, width // 2, 1)
        lane = lax.broadcasted_iota(jnp.int32, line.shape, 1)
        return jnp.where(lane < width >> index, line, 0.0)

    def came(ref, b, kind, index):
        at = slice(0, width) if index == 0 else slice(width, 2 * width)
        line = ref[b, kind * deltas : (kind + 1) * deltas, at]
        line = jnp.concatenate([line, jnp.zeros((DELTA_ROWS - deltas, width), f32)], axis=0)
        return small_level(line, index)

    def mask_line(ref, b, index):
        at = slice(0, width) if index == 0 else slice(width, 2 * width)
        return small_level(ref[b, edge:, at].astype(f32), index)

    for b in range(crops):
        partial, weights = [], []
        for index, (padded, own, lines) in enumerate(plan):
            rows = [
                values[b, :, line * width : (line + 1) * width]
                for line in range(padded, padded + lines + 2)
            ]
            rows[0] = rows[0] + came(above, b, 0, index)
            rows[1] = rows[1] + came(above, b, 1, index)
            rows[lines] = rows[lines] + came(below, b, 1, index)
            rows[lines + 1] = rows[lines + 1] + came(below, b, 0, index)
            partial += rows
            weights += [
                mask_line(mask_above, b, index),
                mask[b, :, own * width : (own + lines) * width],
                mask_line(mask_below, b, index),
            ]
        mismatch = jnp.concatenate(partial, axis=1)
        weight = jnp.concatenate(weights, axis=1)
        magnitude = jnp.abs(mismatch)
        losses = weight * jnp.where(
            magnitude < box_beta, 0.5 * mismatch * mismatch / box_beta, magnitude - 0.5 * box_beta
        )
        for padded, own, lines in plan:
            for line in range(padded + 1, padded + 1 + lines):
                summed = summed + losses[:, line * width : (line + 1) * width]
        middle = weight * jnp.clip(mismatch / box_beta, -1.0, 1.0) * inverse
        middle = middle.astype(bf16).astype(f32)
        shifted = [turned(middle, -1, 1, width), middle, turned(middle, 1, 1, width)]
        for i in range(3):
            for j in range(3):
                for padded, own, lines in plan:
                    at = (padded + 2 - i) * width
                    taps[
                        (3 * i + j) * DELTA_ROWS : (3 * i + j + 1) * DELTA_ROWS,
                        own * width : (own + lines) * width,
                    ] = shifted[j][:, at : at + lines * width].astype(bf16)
        around = taps[...]
        lines_all = levels.shape[1]
        total_grad = total_grad + dot(around, levels[b].reshape(lines_all * width, channels))
        back = dot(around, head[...], ((0,), (0,))).reshape(lines_all, width, channels)
        rounded = back[:height].astype(bf16)
        grad_four[b] = rounded
        first[b, :width] = rounded[0]
        last[b, :width] = rounded[height - 1]
        for q in range(low_height // 2):
            up = doubled_columns(wide, back[height + low_height + q, : low_width // 2])
            for row in (2 * q, 2 * q + 1):
                low = (back[height + row, :low_width] + 0.25 * up).astype(bf16)
                grad_five[b, row] = low
                if row == 0:
                    first[b, width:] = low
                if row == low_height - 1:
                    last[b, width:] = low
    swapped(first, last, pair, other, True)
    head_grad[...] = total_grad
    loss[0, 0] = jnp.sum(summed)


def conv_grad_kernel(n_rows, input_four, input_five, pair_in, other_in, grad_four, grad_five, *refs):
    outs, (turned_rows, sums_four, sums_five, above, below) = refs[:-5], refs[-5:]
    swapped(above, below, pair_in, other_in, False)
    crops, height, width, channels = input_four.shape
    low_height, low_width = input_five.shape[1:3]
    padding = jnp.zeros((width - low_width, channels), bf16)
    for own, grad, edge, sums in (
        (input_four, grad_four, 0, sums_four),
        (input_five, grad_five, width, sums_five),
    ):
        lines, extent = own.shape[1:3]

        def widened(row):
            if extent == width:
                return row
            return jnp.concatenate([row, padding], axis=0)

        for b in range(crops):
            for r in range(lines + 2):
                if r == 0:
                    row = above[b, edge : edge + extent]
                elif r == lines + 1:
                    row = below[b, edge : edge + extent]
                else:
                    row = own[b, r - 1]
                turned_rows[:, r * width : (r + 1) * width] = widened(row).T
            left = jnp.concatenate(
                [turned_rows[:, i * width : (i + lines) * width] for i in range(3)], axis=0
            )
            middle = jnp.concatenate([widened(grad[b, r]) for r in range(lines)], axis=0)
            wide = middle.astype(f32)
            right = jnp.concatenate(
                [
                    turned(wide, -1, 0, width).astype(bf16),
                    middle,
                    turned(wide, 1, 0, width).astype(bf16),
                ],
                axis=1,
            )
            for i in range(3):
                product = dot(left[i * channels : (i + 1) * channels], right)
                for j in range(3):
                    at = slice((3 * i + j) * channels, (3 * i + j + 1) * channels)
                    block = product[:, j * channels : (j + 1) * channels]
                    if b == 0:
                        sums[at, :] = block
                    else:
                        sums[at, :] += block
    me = lax.axis_index("rows")
    part = 9 * channels // n_rows
    low = len(outs)
    for index in range(n_rows):
        at = pl.ds(pl.multiple_of((index ^ me) * part, part), part)
        out, j = outs[index % low], index // low
        out[j, :, :channels] = sums_four[at, :].astype(bf16)
        out[j, :, channels:] = sums_five[at, :].astype(bf16)


def merged_grad_kernel(grad_four, grad_five, pair_in, other_in, kernel_four, kernel_five, *refs):
    lat_four, lat_five, spread_four, spread_five, fold, above, below = refs
    swapped(above, below, pair_in, other_in, False)
    crops, height, width, channels = grad_four.shape
    low_height, low_width = grad_five.shape[1:3]
    fill_padded(spread_four, grad_four, above, below, 0)
    fill_padded(spread_five, grad_five, above, below, width)
    rows = 4
    for b in range(crops):
        low = three_taps(spread_five, b, 0, low_height, kernel_five, -1)
        low = low.reshape(low_height, low_width, channels)
        for r in range(0, height, rows):
            back = three_taps(spread_four, b, r, rows, kernel_four, -1)
            at = (b * height + r) * width
            lat_four[at : at + rows * width, :] = back.astype(bf16)
            for h in range(0, channels, LANES):
                fold[...] = back[:, h : h + LANES]
                for q in range(rows // 2):
                    total = low[r // 2 + q, :, h : h + LANES]
                    folded = jnp.zeros_like(total)
                    for line in (2 * q * width, (2 * q + 1) * width):
                        for side in range(2):
                            folded = folded + fold[pl.ds(line + side, low_width, stride=2), :]
                    at_low = (b * low_height + r // 2 + q) * low_width
                    lat_five[at_low : at_low + low_width, h : h + LANES] = (total + folded).astype(bf16)


def section_grad_kernel(n_rows, n_batch, deltas, own, four, five, lat_four, lat_five, head_grad, loss, kept, *refs):
    outs, (sums_four, sums_five, flat) = refs[:-3], refs[-3:]
    crops, height, width, depth = four.shape
    low_height, low_width, low_depth = five.shape[1:]
    me = lax.axis_index("rows")
    part_four, part_five = depth // n_rows, low_depth // n_rows
    positions = crops * height * width
    low_positions = crops * low_height * low_width
    turned_four = lat_four[...].T
    turned_five = lat_five[...].T
    step = 256
    for at in range(0, depth, step):
        block = four[:, :, :, at : at + step].reshape(positions, step)
        sums_four[at : at + step, :] = dot(turned_four, block).T
    for at in range(0, low_depth, step):
        block = five[:, :, :, at : at + step].reshape(low_positions, step)
        sums_five[at : at + step, :] = dot(turned_five, block).T
    channels = head_grad.shape[1]
    flat[:, 9 * channels :] = jnp.zeros((DELTA_ROWS, flat.shape[1] - 9 * channels), f32)
    for t in range(9):
        flat[:, t * channels : (t + 1) * channels] = head_grad[
            t * DELTA_ROWS : (t + 1) * DELTA_ROWS, :
        ]
    line = lax.broadcasted_iota(jnp.int32, (DELTA_ROWS, LANES), 0)
    lane = lax.broadcasted_iota(jnp.int32, (DELTA_ROWS, LANES), 1)
    spot = (line - deltas) * LANES + lane - 3 * (me * n_batch + lax.axis_index("batch"))
    place = jnp.zeros((DELTA_ROWS, LANES), f32)
    for piece, value in enumerate(pieces_of(jnp.full(place.shape, loss[0, 0], f32))):
        place = jnp.where((line >= deltas) & (spot == piece), value, place)
    high = kept.shape[0]
    low = n_rows // high
    for index in range(n_rows):
        k, j = index % low, index // low
        out = kept.at[j] if k == 0 else outs[k - 1].at[j]
        owner = index ^ me
        at = pl.ds(pl.multiple_of(owner * part_four, part_four), part_four)
        out[:part_four, :] = sums_four[at, :].astype(bf16)
        at = pl.ds(pl.multiple_of(owner * part_five, part_five), part_five)
        out[part_four : part_four + part_five, :] = sums_five[at, :].astype(bf16)
        pieces = []
        for z in range(n_batch):
            start = (owner * n_batch + z) * own
            at = pl.ds(pl.multiple_of(start // LANES * LANES, LANES), 2 * LANES)
            square = pltpu.roll(flat[:, at], (2 * LANES - start % LANES) % (2 * LANES), 1)[:, :LANES]
            square = jnp.where((line < deltas) & (lane < own), square, place)
            pieces.append(joined(square))
        out[part_four + part_five :, :] = jnp.concatenate(pieces, axis=0).astype(bf16)


def total_kernel(own, *refs):
    total = own[...]
    for piece in refs[:-1]:
        total = total + piece[...].astype(f32)
    refs[-1][...] = total


def adamw_into(outs, weight, gradient, mean, square):
    for out, value in zip(outs, adamw_update(weight, gradient, mean, square)):
        out[...] = value


def conv_step_kernel(count, own, *refs):
    came, (weight, mean, square, first, second, new) = refs[:count], refs[count:]
    channels = weight.shape[2]
    total = own[...]
    for piece in came:
        total = total + piece[...].astype(f32)
    for k in range(2):
        adamw_into(
            (first.at[k], second.at[k], new.at[k]),
            weight[k],
            total[:, k * channels : (k + 1) * channels],
            mean[k],
            square[k],
        )


def lateral_step_kernel(count, own, *refs):
    came, inputs, outs, loss = refs[:count], refs[count : count + 9], refs[count + 9 : -1], refs[-1]
    total = own[...]
    for piece in came:
        total = total + piece[...].astype(f32)
    lines = inputs[0].shape[0]
    deltas, rows = inputs[6].shape
    square = parted(total[total.shape[0] - 8 :])
    gradients = (total[:lines], total[lines : total.shape[0] - 8], square[:deltas, :rows])
    for k, gradient in enumerate(gradients):
        weight, mean, second = (ref[...] for ref in inputs[3 * k : 3 * k + 3])
        adamw_into(outs[3 * k : 3 * k + 3], weight, gradient, mean, second)
    line = lax.broadcasted_iota(jnp.int32, square.shape, 0)
    loss[0, 0] = jnp.sum(jnp.where(line >= deltas, square, 0.0))


def on_device(
    section_four,
    section_five,
    target_four,
    target_five,
    target_six,
    anchor_four,
    anchor_five,
    anchor_six,
    lateral_four,
    lateral_five,
    output_conv,
    delta_head,
    mean_four,
    mean_five,
    mean_conv,
    mean_head,
    square_four,
    square_five,
    square_conv,
    square_head,
):
    n_rows, n_batch = lax.axis_size("rows"), lax.axis_size("batch")
    _, low_group, high_group = row_groups()
    crops, height, width, depth = section_four.shape
    low_height, low_width, low_depth = section_five.shape[1:]
    four_n, five_n, conv_n = lateral_four.shape[0], lateral_five.shape[0], output_conv.shape[1]
    channels, deltas = delta_head.shape[0] * n_rows * n_batch // 9, delta_head.shape[1]
    shape = jax.ShapeDtypeStruct

    flat = [jnp.transpose(a, (0, 3, 1, 2)) for a in (anchor_four, anchor_five, anchor_six)]
    sources = [lateral_four, lateral_five, delta_head.T, *flat]
    (lateral,) = call(
        pack_kernel,
        "pack",
        sources,
        [shape((four_n + five_n + 8, channels), bf16)],
        [pltpu.VMEM((DELTA_ROWS, LANES), f32)]
        + [pltpu.VMEM(v.shape, v.dtype) for v in sources]
        + [pltpu.SemaphoreType.DMA((len(sources),))],
        apart=len(sources),
    )
    parts = gathered_batch(lateral)
    lateral = jnp.concatenate(
        [p[:four_n] for p in parts]
        + [p[four_n : four_n + five_n] for p in parts]
        + [p[four_n + five_n :] for p in parts]
    )
    laterals = gathered_high(lateral)

    conv = jnp.concatenate([output_conv[0], output_conv[1]], axis=1).astype(bf16)
    conv, _ = lax.optimization_barrier((conv, lateral))
    conv = jnp.concatenate(gathered_batch(conv))

    lines = height + low_height + low_height // 2
    flat, _ = lax.optimization_barrier(
        (
            [
                jnp.transpose(t, (0, 3, 1, 2))
                for t in (
                    target_four,
                    target_five,
                    target_six,
                    anchor_four,
                    anchor_five,
                    anchor_six,
                )
            ],
            lateral,
        )
    )
    target, mask = call(
        planes_kernel,
        "planes",
        [*flat, section_four, section_five],
        [shape((crops, DELTA_ROWS, lines * LANES), f32)] * 2,
    )
    laterals, target, mask = lax.optimization_barrier((laterals, target, mask))
    laterals = gathered_low(laterals)
    convs = gathered_high(conv)

    edge = width + low_width
    full_edge = edge + DELTA_ROWS
    input_rims = [pltpu.VMEM((crops, full_edge, channels), bf16)] * 2
    grad_rims = [pltpu.VMEM((crops, edge, channels), bf16)] * 2
    head_rims = [pltpu.VMEM((crops, 2 * deltas, 2 * width), f32)] * 2
    input_four, input_five, pair, other = call(
        functools.partial(lateral_kernel, n_rows),
        "laterals",
        [section_four, section_five, *laterals, mask],
        [
            shape((crops, height, width, channels), bf16),
            shape((crops, low_height, low_width, channels), bf16),
            shape((crops, full_edge, channels), bf16),
            shape((crops, full_edge, channels), bf16),
        ],
        [
            pltpu.VMEM((depth, channels), bf16),
            pltpu.VMEM((low_depth, channels), bf16),
            pltpu.VMEM((channels // LANES, width, LANES), f32),
        ]
        + input_rims,
        flops=2 * crops * channels * (height * width * depth + low_height * low_width * low_depth),
    )
    pair_in, other_in = from_neighbours(pair, other)
    head, count = call(
        functools.partial(head_weights_kernel, n_rows, n_batch, deltas, conv_n),
        "head_weights",
        laterals,
        [shape((9 * DELTA_ROWS, channels), bf16), shape((1, 1), f32)],
        [pltpu.VMEM((DELTA_ROWS, 9 * channels + 2 * LANES), f32)],
        scalar_outs=1,
    )
    convs, pair_in, other_in, head = lax.optimization_barrier((convs, pair_in, other_in, head))
    convs = gathered_low(convs)

    conv_flops = 18 * crops * channels * channels * (height * width + low_height * low_width)
    levels, values, pair, other, kernel_four, kernel_five = call(
        functools.partial(output_kernel, n_rows, deltas),
        "outputs",
        [input_four, input_five, pair_in, other_in, head, target, mask, *convs],
        [
            shape((crops, lines, width, channels), bf16),
            shape((crops, DELTA_ROWS, (lines + 6) * width), f32),
            shape((crops, 2 * deltas, 2 * width), f32),
            shape((crops, 2 * deltas, 2 * width), f32),
            shape((9 * channels, channels), bf16),
            shape((9 * channels, channels), bf16),
        ],
        [
            pltpu.VMEM((crops, height + 2, width, channels), bf16),
            pltpu.VMEM((crops, low_height + 2, low_width, channels), bf16),
            pltpu.VMEM((low_height * low_width, LANES), f32),
        ]
        + input_rims
        + head_rims,
        flops=conv_flops,
    )
    pair, other = from_neighbours(pair, other)

    head_flops = 18 * DELTA_ROWS * crops * lines * width * channels
    head_grad, grad_four, grad_five, pair, other, loss = call(
        functools.partial(head_kernel, height, deltas),
        "heads",
        [levels, pair, other, pair_in, other_in, head, values, mask, count],
        [
            shape((9 * DELTA_ROWS, channels), f32),
            shape((crops, height, width, channels), bf16),
            shape((crops, low_height, low_width, channels), bf16),
            shape((crops, edge, channels), bf16),
            shape((crops, edge, channels), bf16),
            shape((1, 1), f32),
        ],
        [
            pltpu.VMEM((9 * DELTA_ROWS, lines * width), bf16),
            pltpu.VMEM((channels // LANES, low_width, LANES), f32),
        ]
        + head_rims
        + grad_rims
        + input_rims,
        flops=3 * head_flops,
        scalars=1,
        scalar_outs=1,
    )
    pair, other = from_neighbours(pair, other)

    conv_width = 2 * channels
    conv_blocks = call(
        functools.partial(conv_grad_kernel, n_rows),
        "conv_grads",
        [input_four, input_five, pair_in, other_in, grad_four, grad_five],
        [shape((high_group, n_batch * conv_n, conv_width), bf16)] * low_group,
        [
            pltpu.VMEM((channels, (height + 2) * width), bf16),
            pltpu.VMEM((9 * channels, channels), f32),
            pltpu.VMEM((9 * channels, channels), f32),
        ]
        + input_rims,
        flops=conv_flops,
    )

    positions, low_positions = crops * height * width, crops * low_height * low_width
    conv_partial = summed_low(conv_blocks)
    pair, other, _ = lax.optimization_barrier((pair, other, conv_partial))
    lat_four, lat_five = call(
        merged_grad_kernel,
        "merged_grads",
        [grad_four, grad_five, pair, other, kernel_four, kernel_five],
        [shape((positions, channels), bf16), shape((low_positions, channels), bf16)],
        [
            pltpu.VMEM((crops, height + 2, width, channels), bf16),
            pltpu.VMEM((crops, low_height + 2, low_width, channels), bf16),
            pltpu.VMEM((4 * width, LANES), f32),
        ]
        + grad_rims,
        flops=conv_flops,
    )
    (conv_sum,) = call(
        total_kernel,
        "conv_total",
        [conv_partial[0], *sent_high(conv_partial)],
        [shape(conv_partial[0].shape, f32)],
        flops=20_000_000_000,
    )

    lateral_n = four_n + five_n + 8
    lateral_kept, *lateral_moved = call(
        functools.partial(section_grad_kernel, n_rows, n_batch, deltas, conv_n),
        "lateral_grads",
        [section_four, section_five, lat_four, lat_five, head_grad, loss],
        [shape((high_group, n_batch * lateral_n, channels), bf16)] * low_group,
        [
            pltpu.VMEM((depth, channels), f32),
            pltpu.VMEM((low_depth, channels), f32),
            pltpu.VMEM((DELTA_ROWS, 9 * channels + 2 * LANES), f32),
        ],
        flops=1,
        scalars=1,
    )
    lateral_partial = summed_low([lateral_kept, *lateral_moved])
    lateral_partial, conv_sum = lax.optimization_barrier((lateral_partial, conv_sum))
    lateral_sum = sum((v.astype(f32) for v in sent_high(lateral_partial)), lateral_partial[0])
    conv_shares = shared_batch(conv_sum.reshape(n_batch, conv_n, conv_width))
    conv_shares, lateral_sum = lax.optimization_barrier((conv_shares, lateral_sum))
    first_conv, second_conv, weight_conv = call(
        functools.partial(conv_step_kernel, n_batch - 1),
        "conv_step",
        [*conv_shares, output_conv, mean_conv, square_conv],
        [shape(output_conv.shape, f32)] * 3,
    )
    ends = (n_batch * four_n, n_batch * (four_n + five_n))
    lateral_sum = jnp.concatenate(
        [
            part.reshape(n_batch, -1, channels)
            for part in (
                lateral_sum[: ends[0]],
                lateral_sum[ends[0] : ends[1]],
                lateral_sum[ends[1] :],
            )
        ],
        axis=1,
    )
    turned_head = [v.T for v in (delta_head, mean_head, square_head)]
    outs = call(
        functools.partial(lateral_step_kernel, n_batch - 1),
        "lateral_step",
        [
            *shared_batch(lateral_sum),
            lateral_four,
            mean_four,
            square_four,
            lateral_five,
            mean_five,
            square_five,
            *turned_head,
        ],
        [shape(lateral_four.shape, f32)] * 3
        + [shape(lateral_five.shape, f32)] * 3
        + [shape(turned_head[0].shape, f32)] * 3
        + [shape((1, 1), f32)],
        scalar_outs=1,
    )
    first_four, second_four, weight_four, first_five, second_five, weight_five = outs[:6]
    first_head, second_head, weight_head = (v.T for v in outs[6:9])
    loss_sum = outs[9]
    return (
        loss_sum[0, 0],
        count[0, 0],
        first_four,
        first_five,
        first_conv,
        first_head,
        second_four,
        second_five,
        second_conv,
        second_head,
        weight_four,
        weight_five,
        weight_conv,
        weight_head,
    )


def solution(mesh):
    split = P("batch", "rows", None, None)
    whole, pair = P(("rows", "batch"), None), P(None, ("rows", "batch"), None)
    weights = (whole, whole, pair, whole)
    return jax.shard_map(
        on_device,
        mesh=mesh,
        in_specs=(split,) * 8 + weights * 3,
        out_specs=(P(), P()) + weights * 3,
        check_vma=False,
    )
```

```python
import functools
import math

import jax
import jax.numpy as jnp
from jax import lax
from jax.experimental import pallas as pl
from jax.experimental.pallas import tpu as pltpu
from jax.sharding import PartitionSpec as P

STEP = 5

LANES = 128
DELTA_ROWS = 16
SPARE_BYTES = 12 * 1024 * 1024
ALL_BYTES = 60 * 1024 * 1024

box_beta = 1.0 / 9.0
beta_one = 0.5
beta_two = 0.5
learn_rate = 0.02
weight_decay = 0.01
epsilon = 1e-08

bf16 = jnp.bfloat16
f32 = jnp.float32


def adamw_update(weight, gradient, mean, square):
    first = beta_one * mean + (1.0 - beta_one) * gradient
    second = beta_two * square + (1.0 - beta_two) * gradient * gradient
    corrected_first = first / (1.0 - beta_one**STEP)
    corrected_second = second / (1.0 - beta_two**STEP)
    return (
        first,
        second,
        weight
        - learn_rate
        * (corrected_first / (jnp.sqrt(corrected_second) + epsilon) + weight_decay * weight),
    )


def sent(value, axis, mask):
    count = lax.axis_size(axis)
    return lax.ppermute(value, axis, [(i, i ^ mask) for i in range(count)])


def gathered_batch(piece):
    count, me = lax.axis_size("batch"), lax.axis_index("batch")
    stacked = jnp.stack([piece] + [sent(piece, "batch", k) for k in range(1, count)])
    return [lax.dynamic_index_in_dim(stacked, t ^ me, 0, keepdims=False) for t in range(count)]


def row_groups():
    count = lax.axis_size("rows")
    low = max(count // 4, 1)
    return count, low, count // low


def gathered_high(piece):
    _, low, high = row_groups()
    return [piece] + [sent(piece, "rows", j * low) for j in range(1, high)]


def gathered_low(held):
    _, low, _ = row_groups()
    result = [None] * (low * len(held))
    for j in range(len(held)):
        result[j * low] = held[j]
        for k in range(1, low):
            result[j * low + k] = sent(held[j], "rows", k)
    return result


def summed_low(blocks):
    _, low, high = row_groups()
    came = []
    for k in range(1, low):
        whole = isinstance(blocks[k], jax.Array)
        came.append(
            sent(blocks[k], "rows", k) if whole else [sent(block, "rows", k) for block in blocks[k]]
        )
    return [
        sum((c[j].astype(f32) for c in came), blocks[0][j].astype(f32)) for j in range(high)
    ]


def sent_high(partial):
    _, low, high = row_groups()
    return [sent(partial[j].astype(bf16), "rows", j * low) for j in range(1, high)]


def shared_batch(blocks):
    count, me = lax.axis_size("batch"), lax.axis_index("batch")
    own = lax.dynamic_index_in_dim(blocks, me, 0, keepdims=False)
    came = []
    for k in range(1, count):
        block = lax.dynamic_index_in_dim(blocks, me ^ k, 0, keepdims=False).astype(bf16)
        came.append(sent(block, "batch", k))
    return [own, *came]


def from_neighbours(pair, other):
    count = lax.axis_size("rows")
    links = [(i, i + 1) for i in range(1, count - 1, 2)]
    return sent(pair, "rows", 1), lax.ppermute(other, "rows", links + [(j, i) for i, j in links])


def call(kernel, name, args, outs, scratch=(), flops=0, scalars=0, scalar_outs=0, apart=0):
    vmem, smem = pl.BlockSpec(memory_space=pltpu.VMEM), pl.BlockSpec(memory_space=pltpu.SMEM)
    hbm = pl.BlockSpec(memory_space=pltpu.HBM)
    size = sum(a.size * a.dtype.itemsize for a in (*args, *outs))
    held = sum(
        math.prod(ref.shape) * jnp.dtype(ref.dtype).itemsize
        for ref in scratch
        if ref.memory_space == pltpu.VMEM
    )
    return pl.pallas_call(
        kernel,
        out_shape=list(outs),
        in_specs=[hbm] * apart + [vmem] * (len(args) - scalars - apart) + [smem] * scalars,
        out_specs=[vmem] * (len(outs) - scalar_outs) + [smem] * scalar_outs,
        scratch_shapes=list(scratch),
        compiler_params=pltpu.CompilerParams(vmem_limit_bytes=ALL_BYTES if apart else held + SPARE_BYTES),
        cost_estimate=pl.CostEstimate(flops=flops, bytes_accessed=size, transcendentals=0),
        name=name,
    )(*args)


def swapped(upper, lower, pair, other, outward):
    odd = lax.axis_index("rows") % 2 == 1

    def move(one, two):
        for ref, side in ((one, pair), (two, other)):
            if outward:
                side[...] = ref[...]
            else:
                ref[...] = side[...]

    pl.when(odd)(lambda: move(upper, lower))
    pl.when(jnp.logical_not(odd))(lambda: move(lower, upper))


def dot(left, right, dims=((1,), (0,))):
    return lax.dot_general(left, right, (dims, ((), ())), preferred_element_type=f32)


def turned(value, step, axis, width):
    size = value.shape[axis]
    column = lax.broadcasted_iota(jnp.int32, value.shape, axis) % width
    rolled = pltpu.roll(value, step % size, axis)
    return jnp.where(column == (0 if step == 1 else width - 1), 0.0, rolled)


def doubled_columns(ref, row):
    count = row.shape[0]
    for h in range(ref.shape[0]):
        part = row[:, h * LANES : (h + 1) * LANES]
        ref[h, pl.ds(0, count, stride=2), :] = part
        ref[h, pl.ds(1, count, stride=2), :] = part
    return jnp.concatenate([ref[h] for h in range(ref.shape[0])], axis=1)


def pieces_of(value):
    high = value.astype(bf16).astype(f32)
    middle = (value - high).astype(bf16).astype(f32)
    return high, middle, value - high - middle


def pack_kernel(*refs):
    sources, packed, square, held, arrived = refs[:6], refs[6], refs[7], refs[8:14], refs[14]
    copies = [
        pltpu.make_async_copy(source, target, arrived.at[k])
        for k, (source, target) in enumerate(zip(sources, held))
    ]
    for copy in copies:
        copy.start()
    for copy in copies:
        copy.wait()
    four, five, head, anchor_four, anchor_five, anchor_six = held
    lines = four.shape[0] + five.shape[0]
    packed[: four.shape[0]] = four[...].astype(bf16)
    packed[four.shape[0] : lines] = five[...].astype(bf16)
    total = jnp.zeros((1, 1), f32)
    for anchor in (anchor_four, anchor_five, anchor_six):
        total = total + jnp.sum(anchor[...].astype(f32), keepdims=True).reshape(1, 1)
    square[...] = jnp.zeros_like(square)
    square[: head.shape[0], : head.shape[1]] = head[...]
    spare = square[...]
    line = lax.broadcasted_iota(jnp.int32, spare.shape, 0)
    lane = lax.broadcasted_iota(jnp.int32, spare.shape, 1)
    for k, piece in enumerate(pieces_of(jnp.broadcast_to(total, spare.shape))):
        spare = jnp.where((line == head.shape[0]) & (lane == k), piece, spare)
    packed[lines:] = joined(spare).astype(bf16)


def joined(square):
    return jnp.concatenate([square[:8], square[8:]], axis=1)


def parted(lines):
    return jnp.concatenate([lines[:, :LANES], lines[:, LANES:]], axis=0)


def head_weights_kernel(n_rows, n_batch, deltas, own, *refs):
    pieces, (head, count, flat) = refs[:n_rows], refs[n_rows:]
    channels = head.shape[1]
    me = lax.axis_index("rows")
    flat[...] = jnp.zeros_like(flat)
    line = lax.broadcasted_iota(jnp.int32, (DELTA_ROWS, LANES), 0)
    total = jnp.zeros((DELTA_ROWS, LANES), f32)
    for k in range(n_rows):
        lines = pieces[k][pieces[k].shape[0] - 8 * n_batch :].astype(f32)
        for z in range(n_batch):
            square = parted(lines[8 * z : 8 * z + 8])
            total = total + jnp.where(line >= deltas, square, 0.0)
            square = jnp.where(line < deltas, square, 0.0)
            place = ((me ^ k) * n_batch + z) * own
            wide = jnp.concatenate([square, jnp.zeros_like(square)], axis=1)
            wide = pltpu.roll(wide, place % LANES, 1)
            at = pl.ds(pl.multiple_of(place // LANES * LANES, LANES), 2 * LANES)
            flat[:, at] += wide
    for t in range(9):
        block = flat[:, t * channels : (t + 1) * channels].astype(bf16)
        head[t * DELTA_ROWS : (t + 1) * DELTA_ROWS, :] = block
    count[0, 0] = jnp.sum(total)


def planes_kernel(*refs):
    targets, anchors, (target, mask) = refs[:3], refs[3:6], refs[-2:]
    crops, deltas = targets[0].shape[:2]
    own = 0
    target[:, deltas:, :] = jnp.zeros((crops, target.shape[1] - deltas, target.shape[2]), f32)
    mask[:, deltas:, :] = jnp.zeros((crops, mask.shape[1] - deltas, mask.shape[2]), f32)
    for target_ref, anchor_ref in zip(targets, anchors):
        _, count, lines, width = anchor_ref.shape
        share = deltas // count
        for b in range(crops):
            for r in range(lines):
                at, rest = own + r * LANES, LANES - width
                target[b, :deltas, at : at + width] = target_ref[b, :, r, :]
                if rest:
                    target[b, :deltas, at + width : at + LANES] = jnp.zeros((deltas, rest), f32)
                    mask[b, :deltas, at + width : at + LANES] = jnp.zeros((deltas, rest), f32)
                for a in range(count):
                    row = anchor_ref[b, a, r : r + 1, :].astype(f32)
                    mask[b, a * share : (a + 1) * share, at : at + width] = jnp.broadcast_to(
                        row, (share, width)
                    )
        own += lines * LANES


def lateral_kernel(n_rows, four, five, *refs):
    pieces, rest = refs[:n_rows], refs[n_rows:]
    input_four, input_five, pair, other, kernel_four, kernel_five, wide, first, last = rest[1:]
    mask = rest[0]
    crops, height, width, depth = four.shape
    low_height, low_width = five.shape[1:3]
    me = lax.axis_index("rows")
    part_four, part_five = depth // n_rows, five.shape[3] // n_rows
    for k in range(n_rows):
        owner = me ^ k
        at_four = pl.multiple_of(owner * part_four, part_four)
        at_five = pl.multiple_of(owner * part_five, part_five)
        kernel_four[pl.ds(at_four, part_four), :] = pieces[k][:part_four]
        kernel_five[pl.ds(at_five, part_five), :] = pieces[k][part_four : part_four + part_five]
    for b in range(crops):
        low = dot(five[b].reshape(low_height * low_width, -1), kernel_five[...])
        low_rounded = low.astype(bf16).reshape(low_height, low_width, -1)
        input_five[b] = low_rounded
        first[b, width : width + low_width] = low_rounded[0]
        last[b, width : width + low_width] = low_rounded[low_height - 1]
        for q in range(low_height):
            up = doubled_columns(wide, low[q * low_width : (q + 1) * low_width])
            rows = four[b, 2 * q : 2 * q + 2].reshape(2 * width, depth)
            merged = dot(rows, kernel_four[...]).reshape(2, width, -1) + up[None]
            rounded = merged.astype(bf16)
            input_four[b, 2 * q : 2 * q + 2] = rounded
            if q == 0:
                first[b, :width] = rounded[0]
            if q == low_height - 1:
                last[b, :width] = rounded[1]
        edge, half = width + low_width, width // 2
        lane = lax.broadcasted_iota(jnp.int32, (DELTA_ROWS, width), 1)
        plan = level_rows(height, 1)
        for ref, end in ((first, 0), (last, 1)):
            lines = []
            for _, own, count in plan:
                at = (own + (count - 1) * end) * width
                lines.append(mask[b, :, at : at + width])
            small = jnp.where(lane < half, lines[1], pltpu.roll(lines[2], half, 1))
            ref[b, edge:, :width] = lines[0].astype(bf16)
            ref[b, edge:, width:] = small.astype(bf16)
    swapped(first, last, pair, other, True)


def three_taps(source, b, start, rows, weights, step):
    width, channels = source.shape[2:]
    parts = []
    for j in range(3):
        taps = range(3) if step == 1 else (2, 1, 0)
        left = jnp.concatenate(
            [
                source[b, start + i : start + i + rows].reshape(rows * width, channels)
                for i in range(3)
            ],
            axis=1,
        )
        blocks = [weights[(3 * i + j) * channels : (3 * i + j + 1) * channels] for i in taps]
        if step == 1:
            parts.append(dot(left, jnp.concatenate(blocks, axis=0)))
        else:
            parts.append(dot(left, jnp.concatenate(blocks, axis=1), ((1,), (1,))))
    return parts[1] + turned(parts[0], step, 0, width) + turned(parts[2], -step, 0, width)


def fill_padded(padded, own, above, below, start):
    height, width = own.shape[1:3]
    for b in range(own.shape[0]):
        padded[b, 0] = above[b, start : start + width]
        padded[b, 1 : height + 1] = own[b]
        padded[b, height + 1] = below[b, start : start + width]


def output_kernel(n_rows, deltas, input_four, input_five, pair_in, other_in, head, target, mask, *refs):
    pieces, rest = refs[:n_rows], refs[n_rows:]
    levels, values, pair, other, kernel_four, kernel_five = rest[:6]
    spread_four, spread_five, spare, above, below, first, last = rest[6:]
    swapped(above, below, pair_in, other_in, False)
    crops, height, width, channels = input_four.shape
    low_height, low_width = input_five.shape[1:3]
    me = lax.axis_index("rows")
    part = 9 * channels // n_rows
    for k in range(n_rows):
        at = pl.multiple_of((me ^ k) * part, part)
        kernel_four[pl.ds(at, part), :] = pieces[k][:, :channels]
        kernel_five[pl.ds(at, part), :] = pieces[k][:, channels:]
    fill_padded(spread_four, input_four, above, below, 0)
    fill_padded(spread_five, input_five, above, below, width)
    low_start, top_start = height, height + low_height
    half = width // 2
    levels[:, low_start:, half:, :] = jnp.zeros(
        (crops, levels.shape[1] - low_start, width - half, channels), bf16
    )
    quarter = low_width // 2
    levels[:, top_start:, quarter:, :] = jnp.zeros(
        (crops, levels.shape[1] - top_start, width - quarter, channels), bf16
    )
    rows = 4
    for b in range(crops):
        low = three_taps(spread_five, b, 0, low_height, kernel_five, 1)
        low_rounded = low.astype(bf16).reshape(low_height, low_width, channels)
        levels[b, low_start:top_start, :low_width, :] = low_rounded
        for h in range(0, channels, LANES):
            spare[: low_height * low_width, :] = low[:, h : h + LANES]
            for q in range(low_height // 2):
                total = jnp.zeros((quarter, LANES), f32)
                for at in (2 * q * low_width, (2 * q + 1) * low_width):
                    for side in range(2):
                        total = total + spare[pl.ds(at + side, quarter, stride=2), :]
                pooled = (0.25 * total).astype(bf16)
                levels[b, top_start + q, :quarter, h : h + LANES] = pooled
        for r in range(0, height, rows):
            sums = three_taps(spread_four, b, r, rows, kernel_four, 1)
            rounded = sums.astype(bf16).reshape(rows, width, channels)
            levels[b, r : r + rows] = rounded
        lines_all = levels.shape[1]
        products = dot(
            head[...], levels[b].reshape(lines_all * width, channels), ((1,), (1,))
        )
        none = jnp.zeros((products.shape[0], 2 * width), f32)
        columns = []
        for j in range(3):
            pieces = []
            for _, own, count_lines in level_rows(height, 1):
                padded = jnp.concatenate(
                    [none, products[:, own * width : (own + count_lines) * width], none], axis=1
                )
                total = jnp.zeros((DELTA_ROWS, (count_lines + 2) * width), f32)
                for i in range(3):
                    tap = (3 * i + j) * DELTA_ROWS
                    at = slice(i * width, (i + count_lines + 2) * width)
                    total = total + padded[tap : tap + DELTA_ROWS, at]
                pieces.append(total)
            columns.append(jnp.concatenate(pieces, axis=1))
        sums = columns[1] + turned(columns[0], 1, 1, width) + turned(columns[2], -1, 1, width)
        for index, (padded, own, count_lines) in enumerate(level_rows(height, 1)):
            own_at = slice(own * width, (own + count_lines) * width)
            start, end = padded * width, (padded + count_lines + 2) * width
            partial = sums[:, start + width : end - width] - target[b, :, own_at]
            values[b, :, start : start + width] = sums[:, start : start + width]
            values[b, :, start + width : end - width] = partial
            values[b, :, end - width : end] = sums[:, end - width : end]
            upper = (partial[:, :width], sums[:, start : start + width])
            lower = (partial[:, (count_lines - 1) * width :], sums[:, end - width : end])
            for out, values_of in ((first, upper), (last, lower)):
                for kind, line in enumerate(values_of):
                    lines, line = slice(kind * deltas, (kind + 1) * deltas), line[:deltas]
                    if index < 2:
                        out[b, lines, index * width : (index + 1) * width] = line
                    else:
                        moved = pltpu.roll(line, half, 1)
                        lane = lax.broadcasted_iota(jnp.int32, line.shape, 1)
                        mixed = jnp.where(lane < half, out[b, lines, width : 2 * width], moved)
                        out[b, lines, width : 2 * width] = mixed
    swapped(first, last, pair, other, True)


def level_rows(height, rim):
    result, padded, own = [], 0, 0
    for count in (height, height // 2, height // 4):
        result.append((padded, own, count))
        padded, own = padded + count + 2 * rim, own + count
    return result


def head_kernel(height, deltas, levels, pair_in, other_in, pair_mask, other_mask, head, values, mask, count, *refs):
    head_grad, grad_four, grad_five, pair, other, loss = refs[:6]
    taps, wide, above, below, first, last, mask_above, mask_below = refs[6:]
    swapped(above, below, pair_in, other_in, False)
    swapped(mask_above, mask_below, pair_mask, other_mask, False)
    edge = first.shape[1]
    crops, _, width, channels = levels.shape
    inverse = 1.0 / jnp.maximum(count[0, 0], 1.0)
    plan = level_rows(height, 1)
    summed = jnp.zeros((DELTA_ROWS, LANES), f32)
    total_grad = jnp.zeros((9 * DELTA_ROWS, channels), f32)
    low_height, low_width = height // 2, width // 2
    def small_level(line, index):
        if index == 2:
            line = pltpu.roll(line, width // 2, 1)
        lane = lax.broadcasted_iota(jnp.int32, line.shape, 1)
        return jnp.where(lane < width >> index, line, 0.0)

    def came(ref, b, kind, index):
        at = slice(0, width) if index == 0 else slice(width, 2 * width)
        line = ref[b, kind * deltas : (kind + 1) * deltas, at]
        line = jnp.concatenate([line, jnp.zeros((DELTA_ROWS - deltas, width), f32)], axis=0)
        return small_level(line, index)

    def mask_line(ref, b, index):
        at = slice(0, width) if index == 0 else slice(width, 2 * width)
        return small_level(ref[b, edge:, at].astype(f32), index)

    for b in range(crops):
        partial, weights = [], []
        for index, (padded, own, lines) in enumerate(plan):
            rows = [
                values[b, :, line * width : (line + 1) * width]
                for line in range(padded, padded + lines + 2)
            ]
            rows[0] = rows[0] + came(above, b, 0, index)
            rows[1] = rows[1] + came(above, b, 1, index)
            rows[lines] = rows[lines] + came(below, b, 1, index)
            rows[lines + 1] = rows[lines + 1] + came(below, b, 0, index)
            partial += rows
            weights += [
                mask_line(mask_above, b, index),
                mask[b, :, own * width : (own + lines) * width],
                mask_line(mask_below, b, index),
            ]
        mismatch = jnp.concatenate(partial, axis=1)
        weight = jnp.concatenate(weights, axis=1)
        magnitude = jnp.abs(mismatch)
        losses = weight * jnp.where(
            magnitude < box_beta, 0.5 * mismatch * mismatch / box_beta, magnitude - 0.5 * box_beta
        )
        for padded, own, lines in plan:
            for line in range(padded + 1, padded + 1 + lines):
                summed = summed + losses[:, line * width : (line + 1) * width]
        middle = weight * jnp.clip(mismatch / box_beta, -1.0, 1.0) * inverse
        middle = middle.astype(bf16).astype(f32)
        shifted = [turned(middle, -1, 1, width), middle, turned(middle, 1, 1, width)]
        for i in range(3):
            for j in range(3):
                for padded, own, lines in plan:
                    at = (padded + 2 - i) * width
                    taps[
                        (3 * i + j) * DELTA_ROWS : (3 * i + j + 1) * DELTA_ROWS,
                        own * width : (own + lines) * width,
                    ] = shifted[j][:, at : at + lines * width].astype(bf16)
        around = taps[...]
        lines_all = levels.shape[1]
        total_grad = total_grad + dot(around, levels[b].reshape(lines_all * width, channels))
        back = dot(around, head[...], ((0,), (0,))).reshape(lines_all, width, channels)
        rounded = back[:height].astype(bf16)
        grad_four[b] = rounded
        first[b, :width] = rounded[0]
        last[b, :width] = rounded[height - 1]
        for q in range(low_height // 2):
            up = doubled_columns(wide, back[height + low_height + q, : low_width // 2])
            for row in (2 * q, 2 * q + 1):
                low = (back[height + row, :low_width] + 0.25 * up).astype(bf16)
                grad_five[b, row] = low
                if row == 0:
                    first[b, width:] = low
                if row == low_height - 1:
                    last[b, width:] = low
    swapped(first, last, pair, other, True)
    head_grad[...] = total_grad
    loss[0, 0] = jnp.sum(summed)


def conv_grad_kernel(n_rows, input_four, input_five, pair_in, other_in, grad_four, grad_five, *refs):
    outs, (turned_rows, sums_four, sums_five, above, below) = refs[:-5], refs[-5:]
    swapped(above, below, pair_in, other_in, False)
    crops, height, width, channels = input_four.shape
    low_height, low_width = input_five.shape[1:3]
    for own, grad, edge, sums in (
        (input_four, grad_four, 0, sums_four),
        (input_five, grad_five, width, sums_five),
    ):
        lines, extent = own.shape[1:3]
        beside = width // extent
        starts = range(0, crops, beside)

        def padded_row(b, r):
            if r == 0:
                return above[b, edge : edge + extent]
            if r == lines + 1:
                return below[b, edge : edge + extent]
            return own[b, r - 1]

        for g, start in enumerate(starts):
            for r in range(lines + 2):
                row = [padded_row(b, r) for b in range(start, start + beside)]
                at = (g * (lines + 2) + r) * width
                turned_rows[:, at : at + width] = jnp.concatenate(row, axis=0).T
        middle = jnp.concatenate(
            [
                grad[b, r]
                for start in starts
                for r in range(lines)
                for b in range(start, start + beside)
            ],
            axis=0,
        )
        wide = middle.astype(f32)
        right = jnp.concatenate(
            [
                turned(wide, -1, 0, extent).astype(bf16),
                middle,
                turned(wide, 1, 0, extent).astype(bf16),
            ],
            axis=1,
        )
        for i in range(3):
            left = []
            for g in range(len(starts)):
                at = (g * (lines + 2) + i) * width
                left.append(turned_rows[:, at : at + lines * width])
            product = dot(jnp.concatenate(left, axis=1), right).astype(bf16)
            for j in range(3):
                at = slice((3 * i + j) * channels, (3 * i + j + 1) * channels)
                sums[at, :] = product[:, j * channels : (j + 1) * channels]
    me = lax.axis_index("rows")
    part = 9 * channels // n_rows
    low = len(outs)
    for index in range(n_rows):
        at = pl.ds(pl.multiple_of((index ^ me) * part, part), part)
        out, j = outs[index % low], index // low
        out[j, :, :channels] = sums_four[at, :]
        out[j, :, channels:] = sums_five[at, :]


def merged_grad_kernel(grad_four, grad_five, pair_in, other_in, kernel_four, kernel_five, *refs):
    lat_four, lat_five, spread_four, spread_five, fold, above, below = refs
    swapped(above, below, pair_in, other_in, False)
    crops, height, width, channels = grad_four.shape
    low_height, low_width = grad_five.shape[1:3]
    fill_padded(spread_four, grad_four, above, below, 0)
    fill_padded(spread_five, grad_five, above, below, width)
    rows = 4
    for b in range(crops):
        low = three_taps(spread_five, b, 0, low_height, kernel_five, -1)
        low = low.reshape(low_height, low_width, channels)
        for r in range(0, height, rows):
            back = three_taps(spread_four, b, r, rows, kernel_four, -1)
            at = (b * height + r) * width
            lat_four[at : at + rows * width, :] = back.astype(bf16)
            for h in range(0, channels, LANES):
                fold[...] = back[:, h : h + LANES]
                for q in range(rows // 2):
                    total = low[r // 2 + q, :, h : h + LANES]
                    folded = jnp.zeros_like(total)
                    for line in (2 * q * width, (2 * q + 1) * width):
                        for side in range(2):
                            folded = folded + fold[pl.ds(line + side, low_width, stride=2), :]
                    at_low = (b * low_height + r // 2 + q) * low_width
                    lat_five[at_low : at_low + low_width, h : h + LANES] = (total + folded).astype(bf16)


def section_grad_kernel(n_rows, n_batch, deltas, own, four, five, lat_four, lat_five, head_grad, loss, kept, *refs):
    outs, (sums_four, sums_five, flat) = refs[:-3], refs[-3:]
    crops, height, width, depth = four.shape
    low_height, low_width, low_depth = five.shape[1:]
    me = lax.axis_index("rows")
    part_four, part_five = depth // n_rows, low_depth // n_rows
    positions = crops * height * width
    low_positions = crops * low_height * low_width
    turned_four = lat_four[...].T
    turned_five = lat_five[...].T
    step = 256
    for at in range(0, depth, step):
        block = four[:, :, :, at : at + step].reshape(positions, step)
        sums_four[at : at + step, :] = dot(turned_four, block).astype(bf16).T
    for at in range(0, low_depth, step):
        block = five[:, :, :, at : at + step].reshape(low_positions, step)
        sums_five[at : at + step, :] = dot(turned_five, block).astype(bf16).T
    channels = head_grad.shape[1]
    flat[:, 9 * channels :] = jnp.zeros((DELTA_ROWS, flat.shape[1] - 9 * channels), f32)
    for t in range(9):
        flat[:, t * channels : (t + 1) * channels] = head_grad[
            t * DELTA_ROWS : (t + 1) * DELTA_ROWS, :
        ]
    line = lax.broadcasted_iota(jnp.int32, (DELTA_ROWS, LANES), 0)
    lane = lax.broadcasted_iota(jnp.int32, (DELTA_ROWS, LANES), 1)
    spot = (line - deltas) * LANES + lane - 3 * (me * n_batch + lax.axis_index("batch"))
    place = jnp.zeros((DELTA_ROWS, LANES), f32)
    for piece, value in enumerate(pieces_of(jnp.full(place.shape, loss[0, 0], f32))):
        place = jnp.where((line >= deltas) & (spot == piece), value, place)
    high = kept.shape[0]
    low = n_rows // high
    for index in range(n_rows):
        k, j = index % low, index // low
        out = kept.at[j] if k == 0 else outs[k - 1].at[j]
        owner = index ^ me
        at = pl.ds(pl.multiple_of(owner * part_four, part_four), part_four)
        out[:part_four, :] = sums_four[at, :]
        at = pl.ds(pl.multiple_of(owner * part_five, part_five), part_five)
        out[part_four : part_four + part_five, :] = sums_five[at, :]
        pieces = []
        for z in range(n_batch):
            start = (owner * n_batch + z) * own
            at = pl.ds(pl.multiple_of(start // LANES * LANES, LANES), 2 * LANES)
            square = pltpu.roll(flat[:, at], (2 * LANES - start % LANES) % (2 * LANES), 1)[:, :LANES]
            square = jnp.where((line < deltas) & (lane < own), square, place)
            pieces.append(joined(square))
        out[part_four + part_five :, :] = jnp.concatenate(pieces, axis=0).astype(bf16)


def total_kernel(own, *refs):
    total = own[...]
    for piece in refs[:-1]:
        total = total + piece[...].astype(f32)
    refs[-1][...] = total


def adamw_into(outs, weight, gradient, mean, square):
    for out, value in zip(outs, adamw_update(weight, gradient, mean, square)):
        out[...] = value


def conv_step_kernel(count, own, *refs):
    came, (weight, mean, square, first, second, new) = refs[:count], refs[count:]
    channels = weight.shape[2]
    total = own[...]
    for piece in came:
        total = total + piece[...].astype(f32)
    for k in range(2):
        adamw_into(
            (first.at[k], second.at[k], new.at[k]),
            weight[k],
            total[:, k * channels : (k + 1) * channels],
            mean[k],
            square[k],
        )


def lateral_step_kernel(count, own, *refs):
    came, inputs, outs, loss = refs[:count], refs[count : count + 9], refs[count + 9 : -1], refs[-1]
    total = own[...]
    for piece in came:
        total = total + piece[...].astype(f32)
    lines = inputs[0].shape[0]
    deltas, rows = inputs[6].shape
    square = parted(total[total.shape[0] - 8 :])
    gradients = (total[:lines], total[lines : total.shape[0] - 8], square[:deltas, :rows])
    for k, gradient in enumerate(gradients):
        weight, mean, second = (ref[...] for ref in inputs[3 * k : 3 * k + 3])
        adamw_into(outs[3 * k : 3 * k + 3], weight, gradient, mean, second)
    line = lax.broadcasted_iota(jnp.int32, square.shape, 0)
    loss[0, 0] = jnp.sum(jnp.where(line >= deltas, square, 0.0))


def on_device(
    section_four,
    section_five,
    target_four,
    target_five,
    target_six,
    anchor_four,
    anchor_five,
    anchor_six,
    lateral_four,
    lateral_five,
    output_conv,
    delta_head,
    mean_four,
    mean_five,
    mean_conv,
    mean_head,
    square_four,
    square_five,
    square_conv,
    square_head,
):
    n_rows, n_batch = lax.axis_size("rows"), lax.axis_size("batch")
    _, low_group, high_group = row_groups()
    crops, height, width, depth = section_four.shape
    low_height, low_width, low_depth = section_five.shape[1:]
    four_n, five_n, conv_n = lateral_four.shape[0], lateral_five.shape[0], output_conv.shape[1]
    channels, deltas = delta_head.shape[0] * n_rows * n_batch // 9, delta_head.shape[1]
    shape = jax.ShapeDtypeStruct

    flat = [jnp.transpose(a, (0, 3, 1, 2)) for a in (anchor_four, anchor_five, anchor_six)]
    sources = [lateral_four, lateral_five, delta_head.T, *flat]
    (lateral,) = call(
        pack_kernel,
        "pack",
        sources,
        [shape((four_n + five_n + 8, channels), bf16)],
        [pltpu.VMEM((DELTA_ROWS, LANES), f32)]
        + [pltpu.VMEM(v.shape, v.dtype) for v in sources]
        + [pltpu.SemaphoreType.DMA((len(sources),))],
        apart=len(sources),
    )
    parts = gathered_batch(lateral)
    lateral = jnp.concatenate(
        [p[:four_n] for p in parts]
        + [p[four_n : four_n + five_n] for p in parts]
        + [p[four_n + five_n :] for p in parts]
    )
    laterals = gathered_high(lateral)

    conv = jnp.concatenate([output_conv[0], output_conv[1]], axis=1).astype(bf16)
    conv, _ = lax.optimization_barrier((conv, lateral))
    conv = jnp.concatenate(gathered_batch(conv))

    lines = height + low_height + low_height // 2
    flat, _ = lax.optimization_barrier(
        (
            [
                jnp.transpose(t, (0, 3, 1, 2))
                for t in (
                    target_four,
                    target_five,
                    target_six,
                    anchor_four,
                    anchor_five,
                    anchor_six,
                )
            ],
            lateral,
        )
    )
    target, mask = call(
        planes_kernel,
        "planes",
        [*flat, section_four, section_five],
        [shape((crops, DELTA_ROWS, lines * LANES), f32)] * 2,
    )
    laterals, target, mask = lax.optimization_barrier((laterals, target, mask))
    laterals = gathered_low(laterals)
    convs = gathered_high(conv)

    edge = width + low_width
    full_edge = edge + DELTA_ROWS
    input_rims = [pltpu.VMEM((crops, full_edge, channels), bf16)] * 2
    grad_rims = [pltpu.VMEM((crops, edge, channels), bf16)] * 2
    head_rims = [pltpu.VMEM((crops, 2 * deltas, 2 * width), f32)] * 2
    input_four, input_five, pair, other = call(
        functools.partial(lateral_kernel, n_rows),
        "laterals",
        [section_four, section_five, *laterals, mask],
        [
            shape((crops, height, width, channels), bf16),
            shape((crops, low_height, low_width, channels), bf16),
            shape((crops, full_edge, channels), bf16),
            shape((crops, full_edge, channels), bf16),
        ],
        [
            pltpu.VMEM((depth, channels), bf16),
            pltpu.VMEM((low_depth, channels), bf16),
            pltpu.VMEM((channels // LANES, width, LANES), f32),
        ]
        + input_rims,
        flops=2 * crops * channels * (height * width * depth + low_height * low_width * low_depth),
    )
    pair_in, other_in = from_neighbours(pair, other)
    head, count = call(
        functools.partial(head_weights_kernel, n_rows, n_batch, deltas, conv_n),
        "head_weights",
        laterals,
        [shape((9 * DELTA_ROWS, channels), bf16), shape((1, 1), f32)],
        [pltpu.VMEM((DELTA_ROWS, 9 * channels + 2 * LANES), f32)],
        scalar_outs=1,
    )
    pair_in, other_in, head = lax.optimization_barrier((pair_in, other_in, head))
    early = (0, high_group - 1)
    early_convs = [
        lax.optimization_barrier((convs[j], pair_in, other_in))[0] for j in early
    ]
    early_low = gathered_low(early_convs)
    late = [j for j in range(high_group) if j not in early]
    late_convs, early_low = lax.optimization_barrier(([convs[j] for j in late], early_low))
    late_low = gathered_low(late_convs)
    convs = [None] * n_rows
    for group, lows in ((early, early_low), (late, late_low)):
        for i, j in enumerate(group):
            convs[j * low_group : (j + 1) * low_group] = lows[i * low_group : (i + 1) * low_group]

    conv_flops = 18 * crops * channels * channels * (height * width + low_height * low_width)
    levels, values, pair, other, kernel_four, kernel_five = call(
        functools.partial(output_kernel, n_rows, deltas),
        "outputs",
        [input_four, input_five, pair_in, other_in, head, target, mask, *convs],
        [
            shape((crops, lines, width, channels), bf16),
            shape((crops, DELTA_ROWS, (lines + 6) * width), f32),
            shape((crops, 2 * deltas, 2 * width), f32),
            shape((crops, 2 * deltas, 2 * width), f32),
            shape((9 * channels, channels), bf16),
            shape((9 * channels, channels), bf16),
        ],
        [
            pltpu.VMEM((crops, height + 2, width, channels), bf16),
            pltpu.VMEM((crops, low_height + 2, low_width, channels), bf16),
            pltpu.VMEM((low_height * low_width, LANES), f32),
        ]
        + input_rims
        + head_rims,
        flops=conv_flops,
    )
    pair, other = from_neighbours(pair, other)

    head_flops = 18 * DELTA_ROWS * crops * lines * width * channels
    head_grad, grad_four, grad_five, pair, other, loss = call(
        functools.partial(head_kernel, height, deltas),
        "heads",
        [levels, pair, other, pair_in, other_in, head, values, mask, count],
        [
            shape((9 * DELTA_ROWS, channels), f32),
            shape((crops, height, width, channels), bf16),
            shape((crops, low_height, low_width, channels), bf16),
            shape((crops, edge, channels), bf16),
            shape((crops, edge, channels), bf16),
            shape((1, 1), f32),
        ],
        [
            pltpu.VMEM((9 * DELTA_ROWS, lines * width), bf16),
            pltpu.VMEM((channels // LANES, low_width, LANES), f32),
        ]
        + head_rims
        + grad_rims
        + input_rims,
        flops=3 * head_flops,
        scalars=1,
        scalar_outs=1,
    )
    pair, other = from_neighbours(pair, other)

    conv_width = 2 * channels
    conv_blocks = call(
        functools.partial(conv_grad_kernel, n_rows),
        "conv_grads",
        [input_four, input_five, pair_in, other_in, grad_four, grad_five],
        [shape((high_group, n_batch * conv_n, conv_width), bf16)] * low_group,
        [
            pltpu.VMEM((channels, crops * (height + 2) * width), bf16),
            pltpu.VMEM((9 * channels, channels), bf16),
            pltpu.VMEM((9 * channels, channels), bf16),
        ]
        + input_rims,
        flops=conv_flops,
    )

    positions, low_positions = crops * height * width, crops * low_height * low_width
    conv_partial = summed_low(conv_blocks)
    pair, other, _ = lax.optimization_barrier((pair, other, conv_partial))
    lat_four, lat_five = call(
        merged_grad_kernel,
        "merged_grads",
        [grad_four, grad_five, pair, other, kernel_four, kernel_five],
        [shape((positions, channels), bf16), shape((low_positions, channels), bf16)],
        [
            pltpu.VMEM((crops, height + 2, width, channels), bf16),
            pltpu.VMEM((crops, low_height + 2, low_width, channels), bf16),
            pltpu.VMEM((4 * width, LANES), f32),
        ]
        + grad_rims,
        flops=conv_flops,
    )
    (conv_sum,) = call(
        total_kernel,
        "conv_total",
        [conv_partial[0], *sent_high(conv_partial)],
        [shape(conv_partial[0].shape, f32)],
        flops=20_000_000_000,
    )

    lateral_n = four_n + five_n + 8
    lateral_kept, *lateral_moved = call(
        functools.partial(section_grad_kernel, n_rows, n_batch, deltas, conv_n),
        "lateral_grads",
        [section_four, section_five, lat_four, lat_five, head_grad, loss],
        [shape((high_group, n_batch * lateral_n, channels), bf16)] * low_group,
        [
            pltpu.VMEM((depth, channels), bf16),
            pltpu.VMEM((low_depth, channels), bf16),
            pltpu.VMEM((DELTA_ROWS, 9 * channels + 2 * LANES), f32),
        ],
        flops=1,
        scalars=1,
    )
    lateral_partial = summed_low([lateral_kept, *lateral_moved])
    lateral_partial, conv_sum = lax.optimization_barrier((lateral_partial, conv_sum))
    lateral_sum = sum((v.astype(f32) for v in sent_high(lateral_partial)), lateral_partial[0])
    conv_shares = shared_batch(conv_sum.reshape(n_batch, conv_n, conv_width))
    conv_shares, lateral_sum = lax.optimization_barrier((conv_shares, lateral_sum))
    first_conv, second_conv, weight_conv = call(
        functools.partial(conv_step_kernel, n_batch - 1),
        "conv_step",
        [*conv_shares, output_conv, mean_conv, square_conv],
        [shape(output_conv.shape, f32)] * 3,
    )
    ends = (n_batch * four_n, n_batch * (four_n + five_n))
    lateral_sum = jnp.concatenate(
        [
            part.reshape(n_batch, -1, channels)
            for part in (
                lateral_sum[: ends[0]],
                lateral_sum[ends[0] : ends[1]],
                lateral_sum[ends[1] :],
            )
        ],
        axis=1,
    )
    turned_head = [v.T for v in (delta_head, mean_head, square_head)]
    outs = call(
        functools.partial(lateral_step_kernel, n_batch - 1),
        "lateral_step",
        [
            *shared_batch(lateral_sum),
            lateral_four,
            mean_four,
            square_four,
            lateral_five,
            mean_five,
            square_five,
            *turned_head,
        ],
        [shape(lateral_four.shape, f32)] * 3
        + [shape(lateral_five.shape, f32)] * 3
        + [shape(turned_head[0].shape, f32)] * 3
        + [shape((1, 1), f32)],
        scalar_outs=1,
    )
    first_four, second_four, weight_four, first_five, second_five, weight_five = outs[:6]
    first_head, second_head, weight_head = (v.T for v in outs[6:9])
    loss_sum = outs[9]
    return (
        loss_sum[0, 0],
        count[0, 0],
        first_four,
        first_five,
        first_conv,
        first_head,
        second_four,
        second_five,
        second_conv,
        second_head,
        weight_four,
        weight_five,
        weight_conv,
        weight_head,
    )


def solution(mesh):
    split = P("batch", "rows", None, None)
    whole, pair = P(("rows", "batch"), None), P(None, ("rows", "batch"), None)
    weights = (whole, whole, pair, whole)
    return jax.shard_map(
        on_device,
        mesh=mesh,
        in_specs=(split,) * 8 + weights * 3,
        out_specs=(P(), P()) + weights * 3,
        check_vma=False,
    )
```

```python
import functools
import math

import jax
import jax.numpy as jnp
from jax import lax
from jax.experimental import pallas as pl
from jax.experimental.pallas import tpu as pltpu
from jax.sharding import PartitionSpec as P

STEP = 5

LANES = 128
DELTA_ROWS = 16
SPARE_BYTES = 12 * 1024 * 1024
ALL_BYTES = 60 * 1024 * 1024

box_beta = 1.0 / 9.0
beta_one = 0.5
beta_two = 0.5
learn_rate = 0.02
weight_decay = 0.01
epsilon = 1e-08

bf16 = jnp.bfloat16
f32 = jnp.float32


def adamw_update(weight, gradient, mean, square):
    first = beta_one * mean + (1.0 - beta_one) * gradient
    second = beta_two * square + (1.0 - beta_two) * gradient * gradient
    corrected_first = first / (1.0 - beta_one**STEP)
    corrected_second = second / (1.0 - beta_two**STEP)
    return (
        first,
        second,
        weight
        - learn_rate
        * (corrected_first / (jnp.sqrt(corrected_second) + epsilon) + weight_decay * weight),
    )


def sent(value, axis, mask):
    count = lax.axis_size(axis)
    return lax.ppermute(value, axis, [(i, i ^ mask) for i in range(count)])


def gathered_batch(piece):
    count, me = lax.axis_size("batch"), lax.axis_index("batch")
    stacked = jnp.stack([piece] + [sent(piece, "batch", k) for k in range(1, count)])
    return [lax.dynamic_index_in_dim(stacked, t ^ me, 0, keepdims=False) for t in range(count)]


def row_groups():
    count = lax.axis_size("rows")
    low = max(count // 4, 1)
    return count, low, count // low


def gathered_high(piece):
    _, low, high = row_groups()
    return [piece] + [sent(piece, "rows", j * low) for j in range(1, high)]


def gathered_low(held):
    _, low, _ = row_groups()
    result = [None] * (low * len(held))
    for j in range(len(held)):
        result[j * low] = held[j]
        for k in range(1, low):
            result[j * low + k] = sent(held[j], "rows", k)
    return result


def summed_low(blocks):
    _, low, high = row_groups()
    came = []
    for k in range(1, low):
        whole = isinstance(blocks[k], jax.Array)
        came.append(
            sent(blocks[k], "rows", k) if whole else [sent(block, "rows", k) for block in blocks[k]]
        )
    return [
        sum((c[j].astype(f32) for c in came), blocks[0][j].astype(f32)) for j in range(high)
    ]


def sent_high(partial):
    _, low, high = row_groups()
    return [sent(partial[j].astype(bf16), "rows", j * low) for j in range(1, high)]


def shared_batch(blocks):
    count, me = lax.axis_size("batch"), lax.axis_index("batch")
    own = lax.dynamic_index_in_dim(blocks, me, 0, keepdims=False)
    came = []
    for k in range(1, count):
        block = lax.dynamic_index_in_dim(blocks, me ^ k, 0, keepdims=False).astype(bf16)
        came.append(sent(block, "batch", k))
    return [own, *came]


def from_neighbours(pair, other):
    count = lax.axis_size("rows")
    links = [(i, i + 1) for i in range(1, count - 1, 2)]
    return sent(pair, "rows", 1), lax.ppermute(other, "rows", links + [(j, i) for i, j in links])


def call(kernel, name, args, outs, scratch=(), flops=0, scalars=0, scalar_outs=0, apart=0):
    vmem, smem = pl.BlockSpec(memory_space=pltpu.VMEM), pl.BlockSpec(memory_space=pltpu.SMEM)
    hbm = pl.BlockSpec(memory_space=pltpu.HBM)
    size = sum(a.size * a.dtype.itemsize for a in (*args, *outs))
    held = sum(
        math.prod(ref.shape) * jnp.dtype(ref.dtype).itemsize
        for ref in scratch
        if ref.memory_space == pltpu.VMEM
    )
    return pl.pallas_call(
        kernel,
        out_shape=list(outs),
        in_specs=[hbm] * apart + [vmem] * (len(args) - scalars - apart) + [smem] * scalars,
        out_specs=[vmem] * (len(outs) - scalar_outs) + [smem] * scalar_outs,
        scratch_shapes=list(scratch),
        compiler_params=pltpu.CompilerParams(vmem_limit_bytes=ALL_BYTES if apart else held + SPARE_BYTES),
        cost_estimate=pl.CostEstimate(flops=flops, bytes_accessed=size, transcendentals=0),
        name=name,
    )(*args)


def swapped(upper, lower, pair, other, outward):
    odd = lax.axis_index("rows") % 2 == 1

    def move(one, two):
        for ref, side in ((one, pair), (two, other)):
            if outward:
                side[...] = ref[...]
            else:
                ref[...] = side[...]

    pl.when(odd)(lambda: move(upper, lower))
    pl.when(jnp.logical_not(odd))(lambda: move(lower, upper))


def dot(left, right, dims=((1,), (0,))):
    return lax.dot_general(left, right, (dims, ((), ())), preferred_element_type=f32)


def turned(value, step, axis, width):
    size = value.shape[axis]
    column = lax.broadcasted_iota(jnp.int32, value.shape, axis) % width
    rolled = pltpu.roll(value, step % size, axis)
    return jnp.where(column == (0 if step == 1 else width - 1), 0.0, rolled)


def doubled_columns(ref, row):
    count = row.shape[0]
    for h in range(ref.shape[0]):
        part = row[:, h * LANES : (h + 1) * LANES]
        ref[h, pl.ds(0, count, stride=2), :] = part
        ref[h, pl.ds(1, count, stride=2), :] = part
    return jnp.concatenate([ref[h] for h in range(ref.shape[0])], axis=1)


def pieces_of(value):
    high = value.astype(bf16).astype(f32)
    middle = (value - high).astype(bf16).astype(f32)
    return high, middle, value - high - middle


def pack_kernel(*refs):
    sources, packed, square, held, arrived = refs[:6], refs[6], refs[7], refs[8:14], refs[14]
    copies = [
        pltpu.make_async_copy(source, target, arrived.at[k])
        for k, (source, target) in enumerate(zip(sources, held))
    ]
    for copy in copies:
        copy.start()
    for copy in copies:
        copy.wait()
    four, five, head, anchor_four, anchor_five, anchor_six = held
    lines = four.shape[0] + five.shape[0]
    packed[: four.shape[0]] = four[...].astype(bf16)
    packed[four.shape[0] : lines] = five[...].astype(bf16)
    total = jnp.zeros((1, 1), f32)
    for anchor in (anchor_four, anchor_five, anchor_six):
        total = total + jnp.sum(anchor[...].astype(f32), keepdims=True).reshape(1, 1)
    square[...] = jnp.zeros_like(square)
    square[: head.shape[0], : head.shape[1]] = head[...]
    spare = square[...]
    line = lax.broadcasted_iota(jnp.int32, spare.shape, 0)
    lane = lax.broadcasted_iota(jnp.int32, spare.shape, 1)
    for k, piece in enumerate(pieces_of(jnp.broadcast_to(total, spare.shape))):
        spare = jnp.where((line == head.shape[0]) & (lane == k), piece, spare)
    packed[lines:] = joined(spare).astype(bf16)


def joined(square):
    return jnp.concatenate([square[:8], square[8:]], axis=1)


def parted(lines):
    return jnp.concatenate([lines[:, :LANES], lines[:, LANES:]], axis=0)


def head_weights_kernel(n_rows, n_batch, deltas, own, *refs):
    pieces, (head, count, flat) = refs[:n_rows], refs[n_rows:]
    channels = head.shape[1]
    me = lax.axis_index("rows")
    flat[...] = jnp.zeros_like(flat)
    line = lax.broadcasted_iota(jnp.int32, (DELTA_ROWS, LANES), 0)
    total = jnp.zeros((DELTA_ROWS, LANES), f32)
    for k in range(n_rows):
        lines = pieces[k][pieces[k].shape[0] - 8 * n_batch :].astype(f32)
        for z in range(n_batch):
            square = parted(lines[8 * z : 8 * z + 8])
            total = total + jnp.where(line >= deltas, square, 0.0)
            square = jnp.where(line < deltas, square, 0.0)
            place = ((me ^ k) * n_batch + z) * own
            wide = jnp.concatenate([square, jnp.zeros_like(square)], axis=1)
            wide = pltpu.roll(wide, place % LANES, 1)
            at = pl.ds(pl.multiple_of(place // LANES * LANES, LANES), 2 * LANES)
            flat[:, at] += wide
    for t in range(9):
        block = flat[:, t * channels : (t + 1) * channels].astype(bf16)
        head[t * DELTA_ROWS : (t + 1) * DELTA_ROWS, :] = block
    count[0, 0] = jnp.sum(total)


def planes_kernel(*refs):
    targets, anchors, (target, mask) = refs[:3], refs[3:6], refs[-2:]
    crops, deltas = targets[0].shape[:2]
    own = 0
    target[:, deltas:, :] = jnp.zeros((crops, target.shape[1] - deltas, target.shape[2]), f32)
    mask[:, deltas:, :] = jnp.zeros((crops, mask.shape[1] - deltas, mask.shape[2]), f32)
    for target_ref, anchor_ref in zip(targets, anchors):
        _, count, lines, width = anchor_ref.shape
        share = deltas // count
        for b in range(crops):
            for r in range(lines):
                at, rest = own + r * LANES, LANES - width
                target[b, :deltas, at : at + width] = target_ref[b, :, r, :]
                if rest:
                    target[b, :deltas, at + width : at + LANES] = jnp.zeros((deltas, rest), f32)
                    mask[b, :deltas, at + width : at + LANES] = jnp.zeros((deltas, rest), f32)
                for a in range(count):
                    row = anchor_ref[b, a, r : r + 1, :].astype(f32)
                    mask[b, a * share : (a + 1) * share, at : at + width] = jnp.broadcast_to(
                        row, (share, width)
                    )
        own += lines * LANES


def lateral_kernel(n_rows, four, five, *refs):
    pieces, rest = refs[:n_rows], refs[n_rows:]
    input_four, input_five, pair, other, kernel_four, kernel_five, wide, first, last = rest[1:]
    mask = rest[0]
    crops, height, width, depth = four.shape
    low_height, low_width = five.shape[1:3]
    me = lax.axis_index("rows")
    part_four, part_five = depth // n_rows, five.shape[3] // n_rows
    for k in range(n_rows):
        owner = me ^ k
        at_four = pl.multiple_of(owner * part_four, part_four)
        at_five = pl.multiple_of(owner * part_five, part_five)
        kernel_four[pl.ds(at_four, part_four), :] = pieces[k][:part_four]
        kernel_five[pl.ds(at_five, part_five), :] = pieces[k][part_four : part_four + part_five]
    for b in range(crops):
        low = dot(five[b].reshape(low_height * low_width, -1), kernel_five[...])
        low_rounded = low.astype(bf16).reshape(low_height, low_width, -1)
        input_five[b] = low_rounded
        first[b, width : width + low_width] = low_rounded[0]
        last[b, width : width + low_width] = low_rounded[low_height - 1]
        for q in range(low_height):
            up = doubled_columns(wide, low[q * low_width : (q + 1) * low_width])
            rows = four[b, 2 * q : 2 * q + 2].reshape(2 * width, depth)
            merged = dot(rows, kernel_four[...]).reshape(2, width, -1) + up[None]
            rounded = merged.astype(bf16)
            input_four[b, 2 * q : 2 * q + 2] = rounded
            if q == 0:
                first[b, :width] = rounded[0]
            if q == low_height - 1:
                last[b, :width] = rounded[1]
        edge, half = width + low_width, width // 2
        lane = lax.broadcasted_iota(jnp.int32, (DELTA_ROWS, width), 1)
        plan = level_rows(height, 1)
        for ref, end in ((first, 0), (last, 1)):
            lines = []
            for _, own, count in plan:
                at = (own + (count - 1) * end) * width
                lines.append(mask[b, :, at : at + width])
            small = jnp.where(lane < half, lines[1], pltpu.roll(lines[2], half, 1))
            ref[b, edge:, :width] = lines[0].astype(bf16)
            ref[b, edge:, width:] = small.astype(bf16)
    swapped(first, last, pair, other, True)


def three_taps(source, b, start, rows, weights, step):
    width, channels = source.shape[2:]
    parts = []
    for j in range(3):
        taps = range(3) if step == 1 else (2, 1, 0)
        left = jnp.concatenate(
            [
                source[b, start + i : start + i + rows].reshape(rows * width, channels)
                for i in range(3)
            ],
            axis=1,
        )
        blocks = [weights[(3 * i + j) * channels : (3 * i + j + 1) * channels] for i in taps]
        if step == 1:
            parts.append(dot(left, jnp.concatenate(blocks, axis=0)))
        else:
            parts.append(dot(left, jnp.concatenate(blocks, axis=1), ((1,), (1,))))
    return parts[1] + turned(parts[0], step, 0, width) + turned(parts[2], -step, 0, width)


def fill_padded(padded, own, above, below, start):
    height, width = own.shape[1:3]
    for b in range(own.shape[0]):
        padded[b, 0] = above[b, start : start + width]
        padded[b, 1 : height + 1] = own[b]
        padded[b, height + 1] = below[b, start : start + width]


def output_kernel(n_rows, deltas, input_four, input_five, pair_in, other_in, head, target, mask, *refs):
    pieces, rest = refs[:n_rows], refs[n_rows:]
    levels, values, pair, other, kernel_four, kernel_five = rest[:6]
    spread_four, spread_five, spare, above, below, first, last = rest[6:]
    swapped(above, below, pair_in, other_in, False)
    crops, height, width, channels = input_four.shape
    low_height, low_width = input_five.shape[1:3]
    me = lax.axis_index("rows")
    part = 9 * channels // n_rows
    for k in range(n_rows):
        at = pl.multiple_of((me ^ k) * part, part)
        kernel_four[pl.ds(at, part), :] = pieces[k][:, :channels]
        kernel_five[pl.ds(at, part), :] = pieces[k][:, channels:]
    fill_padded(spread_four, input_four, above, below, 0)
    fill_padded(spread_five, input_five, above, below, width)
    low_start, top_start = height, height + low_height
    half = width // 2
    levels[:, low_start:, half:, :] = jnp.zeros(
        (crops, levels.shape[1] - low_start, width - half, channels), bf16
    )
    quarter = low_width // 2
    levels[:, top_start:, quarter:, :] = jnp.zeros(
        (crops, levels.shape[1] - top_start, width - quarter, channels), bf16
    )
    rows = 4
    for b in range(crops):
        low = three_taps(spread_five, b, 0, low_height, kernel_five, 1)
        low_rounded = low.astype(bf16).reshape(low_height, low_width, channels)
        levels[b, low_start:top_start, :low_width, :] = low_rounded
        for h in range(0, channels, LANES):
            spare[: low_height * low_width, :] = low[:, h : h + LANES]
            for q in range(low_height // 2):
                total = jnp.zeros((quarter, LANES), f32)
                for at in (2 * q * low_width, (2 * q + 1) * low_width):
                    for side in range(2):
                        total = total + spare[pl.ds(at + side, quarter, stride=2), :]
                pooled = (0.25 * total).astype(bf16)
                levels[b, top_start + q, :quarter, h : h + LANES] = pooled
        for r in range(0, height, rows):
            sums = three_taps(spread_four, b, r, rows, kernel_four, 1)
            rounded = sums.astype(bf16).reshape(rows, width, channels)
            levels[b, r : r + rows] = rounded
        lines_all = levels.shape[1]
        products = dot(
            head[...], levels[b].reshape(lines_all * width, channels), ((1,), (1,))
        )
        none = jnp.zeros((products.shape[0], 2 * width), f32)
        columns = []
        for j in range(3):
            pieces = []
            for _, own, count_lines in level_rows(height, 1):
                padded = jnp.concatenate(
                    [none, products[:, own * width : (own + count_lines) * width], none], axis=1
                )
                total = jnp.zeros((DELTA_ROWS, (count_lines + 2) * width), f32)
                for i in range(3):
                    tap = (3 * i + j) * DELTA_ROWS
                    at = slice(i * width, (i + count_lines + 2) * width)
                    total = total + padded[tap : tap + DELTA_ROWS, at]
                pieces.append(total)
            columns.append(jnp.concatenate(pieces, axis=1))
        sums = columns[1] + turned(columns[0], 1, 1, width) + turned(columns[2], -1, 1, width)
        for index, (padded, own, count_lines) in enumerate(level_rows(height, 1)):
            own_at = slice(own * width, (own + count_lines) * width)
            start, end = padded * width, (padded + count_lines + 2) * width
            partial = sums[:, start + width : end - width] - target[b, :, own_at]
            values[b, :, start : start + width] = sums[:, start : start + width]
            values[b, :, start + width : end - width] = partial
            values[b, :, end - width : end] = sums[:, end - width : end]
            upper = (partial[:, :width], sums[:, start : start + width])
            lower = (partial[:, (count_lines - 1) * width :], sums[:, end - width : end])
            for out, values_of in ((first, upper), (last, lower)):
                for kind, line in enumerate(values_of):
                    lines, line = slice(kind * deltas, (kind + 1) * deltas), line[:deltas]
                    if index < 2:
                        out[b, lines, index * width : (index + 1) * width] = line
                    else:
                        moved = pltpu.roll(line, half, 1)
                        lane = lax.broadcasted_iota(jnp.int32, line.shape, 1)
                        mixed = jnp.where(lane < half, out[b, lines, width : 2 * width], moved)
                        out[b, lines, width : 2 * width] = mixed
    swapped(first, last, pair, other, True)


def level_rows(height, rim):
    result, padded, own = [], 0, 0
    for count in (height, height // 2, height // 4):
        result.append((padded, own, count))
        padded, own = padded + count + 2 * rim, own + count
    return result


def head_kernel(height, deltas, levels, pair_in, other_in, pair_mask, other_mask, head, values, mask, count, *refs):
    head_grad, grad_four, grad_five, pair, other, loss = refs[:6]
    taps, wide, above, below, first, last, mask_above, mask_below = refs[6:]
    swapped(above, below, pair_in, other_in, False)
    swapped(mask_above, mask_below, pair_mask, other_mask, False)
    edge = first.shape[1]
    crops, _, width, channels = levels.shape
    inverse = 1.0 / jnp.maximum(count[0, 0], 1.0)
    plan = level_rows(height, 1)
    summed = jnp.zeros((DELTA_ROWS, LANES), f32)
    total_grad = jnp.zeros((9 * DELTA_ROWS, channels), f32)
    low_height, low_width = height // 2, width // 2
    def small_level(line, index):
        if index == 2:
            line = pltpu.roll(line, width // 2, 1)
        lane = lax.broadcasted_iota(jnp.int32, line.shape, 1)
        return jnp.where(lane < width >> index, line, 0.0)

    def came(ref, b, kind, index):
        at = slice(0, width) if index == 0 else slice(width, 2 * width)
        line = ref[b, kind * deltas : (kind + 1) * deltas, at]
        line = jnp.concatenate([line, jnp.zeros((DELTA_ROWS - deltas, width), f32)], axis=0)
        return small_level(line, index)

    def mask_line(ref, b, index):
        at = slice(0, width) if index == 0 else slice(width, 2 * width)
        return small_level(ref[b, edge:, at].astype(f32), index)

    for b in range(crops):
        partial, weights = [], []
        for index, (padded, own, lines) in enumerate(plan):
            rows = [
                values[b, :, line * width : (line + 1) * width]
                for line in range(padded, padded + lines + 2)
            ]
            rows[0] = rows[0] + came(above, b, 0, index)
            rows[1] = rows[1] + came(above, b, 1, index)
            rows[lines] = rows[lines] + came(below, b, 1, index)
            rows[lines + 1] = rows[lines + 1] + came(below, b, 0, index)
            partial += rows
            weights += [
                mask_line(mask_above, b, index),
                mask[b, :, own * width : (own + lines) * width],
                mask_line(mask_below, b, index),
            ]
        mismatch = jnp.concatenate(partial, axis=1)
        weight = jnp.concatenate(weights, axis=1)
        magnitude = jnp.abs(mismatch)
        ratio = mismatch * (1.0 / box_beta)
        losses = weight * jnp.where(
            magnitude < box_beta, 0.5 * mismatch * ratio, magnitude - 0.5 * box_beta
        )
        for padded, own, lines in plan:
            for line in range(padded + 1, padded + 1 + lines):
                summed = summed + losses[:, line * width : (line + 1) * width]
        middle = weight * jnp.clip(ratio, -1.0, 1.0) * inverse
        middle = middle.astype(bf16).astype(f32)
        shifted = [turned(middle, -1, 1, width), middle, turned(middle, 1, 1, width)]
        shifted = [value.astype(bf16) for value in shifted]
        for i in range(3):
            for j in range(3):
                for padded, own, lines in plan:
                    at = (padded + 2 - i) * width
                    taps[
                        (3 * i + j) * DELTA_ROWS : (3 * i + j + 1) * DELTA_ROWS,
                        own * width : (own + lines) * width,
                    ] = shifted[j][:, at : at + lines * width]
        around = taps[...]
        lines_all = levels.shape[1]
        total_grad = total_grad + dot(around, levels[b].reshape(lines_all * width, channels))
        back = dot(around, head[...], ((0,), (0,))).reshape(lines_all, width, channels)
        rounded = back[:height].astype(bf16)
        grad_four[b] = rounded
        first[b, :width] = rounded[0]
        last[b, :width] = rounded[height - 1]
        for q in range(low_height // 2):
            up = doubled_columns(wide, back[height + low_height + q, : low_width // 2])
            for row in (2 * q, 2 * q + 1):
                low = (back[height + row, :low_width] + 0.25 * up).astype(bf16)
                grad_five[b, row] = low
                if row == 0:
                    first[b, width:] = low
                if row == low_height - 1:
                    last[b, width:] = low
    swapped(first, last, pair, other, True)
    head_grad[...] = total_grad
    loss[0, 0] = jnp.sum(summed)


def conv_grad_kernel(n_rows, input_four, input_five, pair_in, other_in, grad_four, grad_five, *refs):
    outs, (turned_rows, sums_four, sums_five, above, below) = refs[:-5], refs[-5:]
    swapped(above, below, pair_in, other_in, False)
    crops, height, width, channels = input_four.shape
    low_height, low_width = input_five.shape[1:3]
    for own, grad, edge, sums in (
        (input_four, grad_four, 0, sums_four),
        (input_five, grad_five, width, sums_five),
    ):
        lines, extent = own.shape[1:3]
        beside = width // extent
        starts = range(0, crops, beside)

        def padded_row(b, r):
            if r == 0:
                return above[b, edge : edge + extent]
            if r == lines + 1:
                return below[b, edge : edge + extent]
            return own[b, r - 1]

        for g, start in enumerate(starts):
            for r in range(lines + 2):
                row = [padded_row(b, r) for b in range(start, start + beside)]
                at = (g * (lines + 2) + r) * width
                turned_rows[:, at : at + width] = jnp.concatenate(row, axis=0).T
        middle = jnp.concatenate(
            [
                grad[b, r]
                for start in starts
                for r in range(lines)
                for b in range(start, start + beside)
            ],
            axis=0,
        )
        wide = middle.astype(f32)
        right = jnp.concatenate(
            [
                turned(wide, -1, 0, extent).astype(bf16),
                middle,
                turned(wide, 1, 0, extent).astype(bf16),
            ],
            axis=1,
        )
        for i in range(3):
            left = []
            for g in range(len(starts)):
                at = (g * (lines + 2) + i) * width
                left.append(turned_rows[:, at : at + lines * width])
            product = dot(jnp.concatenate(left, axis=1), right).astype(bf16)
            for j in range(3):
                at = slice((3 * i + j) * channels, (3 * i + j + 1) * channels)
                sums[at, :] = product[:, j * channels : (j + 1) * channels]
    me = lax.axis_index("rows")
    part = 9 * channels // n_rows
    low = len(outs)
    for index in range(n_rows):
        at = pl.ds(pl.multiple_of((index ^ me) * part, part), part)
        out, j = outs[index % low], index // low
        out[j, :, :channels] = sums_four[at, :]
        out[j, :, channels:] = sums_five[at, :]


def merged_grad_kernel(grad_four, grad_five, pair_in, other_in, kernel_four, kernel_five, *refs):
    lat_four, lat_five, spread_four, spread_five, fold, above, below = refs
    swapped(above, below, pair_in, other_in, False)
    crops, height, width, channels = grad_four.shape
    low_height, low_width = grad_five.shape[1:3]
    fill_padded(spread_four, grad_four, above, below, 0)
    fill_padded(spread_five, grad_five, above, below, width)
    rows = 4
    for b in range(crops):
        low = three_taps(spread_five, b, 0, low_height, kernel_five, -1)
        low = low.reshape(low_height, low_width, channels)
        for r in range(0, height, rows):
            back = three_taps(spread_four, b, r, rows, kernel_four, -1)
            at = (b * height + r) * width
            lat_four[at : at + rows * width, :] = back.astype(bf16)
            for h in range(0, channels, LANES):
                fold[...] = back[:, h : h + LANES]
                for q in range(rows // 2):
                    total = low[r // 2 + q, :, h : h + LANES]
                    folded = jnp.zeros_like(total)
                    for line in (2 * q * width, (2 * q + 1) * width):
                        for side in range(2):
                            folded = folded + fold[pl.ds(line + side, low_width, stride=2), :]
                    at_low = (b * low_height + r // 2 + q) * low_width
                    lat_five[at_low : at_low + low_width, h : h + LANES] = (total + folded).astype(bf16)


def section_grad_kernel(n_rows, n_batch, deltas, own, four, five, lat_four, lat_five, head_grad, loss, kept, *refs):
    outs, (sums_four, sums_five, flat) = refs[:-3], refs[-3:]
    crops, height, width, depth = four.shape
    low_height, low_width, low_depth = five.shape[1:]
    me = lax.axis_index("rows")
    part_four, part_five = depth // n_rows, low_depth // n_rows
    positions = crops * height * width
    low_positions = crops * low_height * low_width
    turned_four = lat_four[...].T
    turned_five = lat_five[...].T
    step = 256
    for at in range(0, depth, step):
        block = four[:, :, :, at : at + step].reshape(positions, step)
        sums_four[at : at + step, :] = dot(turned_four, block).astype(bf16).T
    for at in range(0, low_depth, step):
        block = five[:, :, :, at : at + step].reshape(low_positions, step)
        sums_five[at : at + step, :] = dot(turned_five, block).astype(bf16).T
    channels = head_grad.shape[1]
    flat[:, 9 * channels :] = jnp.zeros((DELTA_ROWS, flat.shape[1] - 9 * channels), f32)
    for t in range(9):
        flat[:, t * channels : (t + 1) * channels] = head_grad[
            t * DELTA_ROWS : (t + 1) * DELTA_ROWS, :
        ]
    line = lax.broadcasted_iota(jnp.int32, (DELTA_ROWS, LANES), 0)
    lane = lax.broadcasted_iota(jnp.int32, (DELTA_ROWS, LANES), 1)
    spot = (line - deltas) * LANES + lane - 3 * (me * n_batch + lax.axis_index("batch"))
    place = jnp.zeros((DELTA_ROWS, LANES), f32)
    for piece, value in enumerate(pieces_of(jnp.full(place.shape, loss[0, 0], f32))):
        place = jnp.where((line >= deltas) & (spot == piece), value, place)
    high = kept.shape[0]
    low = n_rows // high
    for index in range(n_rows):
        k, j = index % low, index // low
        out = kept.at[j] if k == 0 else outs[k - 1].at[j]
        owner = index ^ me
        at = pl.ds(pl.multiple_of(owner * part_four, part_four), part_four)
        out[:part_four, :] = sums_four[at, :]
        at = pl.ds(pl.multiple_of(owner * part_five, part_five), part_five)
        out[part_four : part_four + part_five, :] = sums_five[at, :]
        pieces = []
        for z in range(n_batch):
            start = (owner * n_batch + z) * own
            at = pl.ds(pl.multiple_of(start // LANES * LANES, LANES), 2 * LANES)
            square = pltpu.roll(flat[:, at], (2 * LANES - start % LANES) % (2 * LANES), 1)[:, :LANES]
            square = jnp.where((line < deltas) & (lane < own), square, place)
            pieces.append(joined(square))
        out[part_four + part_five :, :] = jnp.concatenate(pieces, axis=0).astype(bf16)


def total_kernel(own, *refs):
    total = own[...]
    for piece in refs[:-1]:
        total = total + piece[...].astype(f32)
    refs[-1][...] = total


def adamw_into(outs, weight, gradient, mean, square):
    for out, value in zip(outs, adamw_update(weight, gradient, mean, square)):
        out[...] = value


def conv_step_kernel(count, own, *refs):
    came, (weight, mean, square, first, second, new) = refs[:count], refs[count:]
    channels = weight.shape[2]
    total = own[...]
    for piece in came:
        total = total + piece[...].astype(f32)
    for k in range(2):
        adamw_into(
            (first.at[k], second.at[k], new.at[k]),
            weight[k],
            total[:, k * channels : (k + 1) * channels],
            mean[k],
            square[k],
        )


def lateral_step_kernel(count, own, *refs):
    came, inputs, outs, loss = refs[:count], refs[count : count + 9], refs[count + 9 : -1], refs[-1]
    total = own[...]
    for piece in came:
        total = total + piece[...].astype(f32)
    lines = inputs[0].shape[0]
    deltas, rows = inputs[6].shape
    square = parted(total[total.shape[0] - 8 :])
    gradients = (total[:lines], total[lines : total.shape[0] - 8], square[:deltas, :rows])
    for k, gradient in enumerate(gradients):
        weight, mean, second = (ref[...] for ref in inputs[3 * k : 3 * k + 3])
        adamw_into(outs[3 * k : 3 * k + 3], weight, gradient, mean, second)
    line = lax.broadcasted_iota(jnp.int32, square.shape, 0)
    loss[0, 0] = jnp.sum(jnp.where(line >= deltas, square, 0.0))


def on_device(
    section_four,
    section_five,
    target_four,
    target_five,
    target_six,
    anchor_four,
    anchor_five,
    anchor_six,
    lateral_four,
    lateral_five,
    output_conv,
    delta_head,
    mean_four,
    mean_five,
    mean_conv,
    mean_head,
    square_four,
    square_five,
    square_conv,
    square_head,
):
    n_rows, n_batch = lax.axis_size("rows"), lax.axis_size("batch")
    _, low_group, high_group = row_groups()
    crops, height, width, depth = section_four.shape
    low_height, low_width, low_depth = section_five.shape[1:]
    four_n, five_n, conv_n = lateral_four.shape[0], lateral_five.shape[0], output_conv.shape[1]
    channels, deltas = delta_head.shape[0] * n_rows * n_batch // 9, delta_head.shape[1]
    shape = jax.ShapeDtypeStruct

    flat = [jnp.transpose(a, (0, 3, 1, 2)) for a in (anchor_four, anchor_five, anchor_six)]
    sources = [lateral_four, lateral_five, delta_head.T, *flat]
    (lateral,) = call(
        pack_kernel,
        "pack",
        sources,
        [shape((four_n + five_n + 8, channels), bf16)],
        [pltpu.VMEM((DELTA_ROWS, LANES), f32)]
        + [pltpu.VMEM(v.shape, v.dtype) for v in sources]
        + [pltpu.SemaphoreType.DMA((len(sources),))],
        apart=len(sources),
    )
    parts = gathered_batch(lateral)
    lateral = jnp.concatenate(
        [p[:four_n] for p in parts]
        + [p[four_n : four_n + five_n] for p in parts]
        + [p[four_n + five_n :] for p in parts]
    )
    laterals = gathered_high(lateral)

    conv = jnp.concatenate([output_conv[0], output_conv[1]], axis=1).astype(bf16)
    conv = jnp.concatenate(gathered_batch(conv))

    lines = height + low_height + low_height // 2
    flat, _ = lax.optimization_barrier(
        (
            [
                jnp.transpose(t, (0, 3, 1, 2))
                for t in (
                    target_four,
                    target_five,
                    target_six,
                    anchor_four,
                    anchor_five,
                    anchor_six,
                )
            ],
            lateral,
        )
    )
    target, mask = call(
        planes_kernel,
        "planes",
        [*flat, section_four, section_five],
        [shape((crops, DELTA_ROWS, lines * LANES), f32)] * 2,
    )
    laterals, target, mask = lax.optimization_barrier((laterals, target, mask))
    laterals = gathered_low(laterals)
    convs = gathered_high(conv)

    edge = width + low_width
    full_edge = edge + DELTA_ROWS
    input_rims = [pltpu.VMEM((crops, full_edge, channels), bf16)] * 2
    grad_rims = [pltpu.VMEM((crops, edge, channels), bf16)] * 2
    head_rims = [pltpu.VMEM((crops, 2 * deltas, 2 * width), f32)] * 2
    input_four, input_five, pair, other = call(
        functools.partial(lateral_kernel, n_rows),
        "laterals",
        [section_four, section_five, *laterals, mask],
        [
            shape((crops, height, width, channels), bf16),
            shape((crops, low_height, low_width, channels), bf16),
            shape((crops, full_edge, channels), bf16),
            shape((crops, full_edge, channels), bf16),
        ],
        [
            pltpu.VMEM((depth, channels), bf16),
            pltpu.VMEM((low_depth, channels), bf16),
            pltpu.VMEM((channels // LANES, width, LANES), f32),
        ]
        + input_rims,
        flops=2 * crops * channels * (height * width * depth + low_height * low_width * low_depth),
    )
    pair_in, other_in = from_neighbours(pair, other)
    head, count = call(
        functools.partial(head_weights_kernel, n_rows, n_batch, deltas, conv_n),
        "head_weights",
        laterals,
        [shape((9 * DELTA_ROWS, channels), bf16), shape((1, 1), f32)],
        [pltpu.VMEM((DELTA_ROWS, 9 * channels + 2 * LANES), f32)],
        scalar_outs=1,
    )
    pair_in, other_in, head = lax.optimization_barrier((pair_in, other_in, head))
    early = (0, high_group - 1)
    early_convs = [
        lax.optimization_barrier((convs[j], pair_in, other_in))[0] for j in early
    ]
    early_low = gathered_low(early_convs)
    late = [j for j in range(high_group) if j not in early]
    late_convs, early_low = lax.optimization_barrier(([convs[j] for j in late], early_low))
    late_low = gathered_low(late_convs)
    convs = [None] * n_rows
    for group, lows in ((early, early_low), (late, late_low)):
        for i, j in enumerate(group):
            convs[j * low_group : (j + 1) * low_group] = lows[i * low_group : (i + 1) * low_group]

    conv_flops = 18 * crops * channels * channels * (height * width + low_height * low_width)
    levels, values, pair, other, kernel_four, kernel_five = call(
        functools.partial(output_kernel, n_rows, deltas),
        "outputs",
        [input_four, input_five, pair_in, other_in, head, target, mask, *convs],
        [
            shape((crops, lines, width, channels), bf16),
            shape((crops, DELTA_ROWS, (lines + 6) * width), f32),
            shape((crops, 2 * deltas, 2 * width), f32),
            shape((crops, 2 * deltas, 2 * width), f32),
            shape((9 * channels, channels), bf16),
            shape((9 * channels, channels), bf16),
        ],
        [
            pltpu.VMEM((crops, height + 2, width, channels), bf16),
            pltpu.VMEM((crops, low_height + 2, low_width, channels), bf16),
            pltpu.VMEM((low_height * low_width, LANES), f32),
        ]
        + input_rims
        + head_rims,
        flops=conv_flops,
    )
    pair, other = from_neighbours(pair, other)

    head_flops = 18 * DELTA_ROWS * crops * lines * width * channels
    head_grad, grad_four, grad_five, pair, other, loss = call(
        functools.partial(head_kernel, height, deltas),
        "heads",
        [levels, pair, other, pair_in, other_in, head, values, mask, count],
        [
            shape((9 * DELTA_ROWS, channels), f32),
            shape((crops, height, width, channels), bf16),
            shape((crops, low_height, low_width, channels), bf16),
            shape((crops, edge, channels), bf16),
            shape((crops, edge, channels), bf16),
            shape((1, 1), f32),
        ],
        [
            pltpu.VMEM((9 * DELTA_ROWS, lines * width), bf16),
            pltpu.VMEM((channels // LANES, low_width, LANES), f32),
        ]
        + head_rims
        + grad_rims
        + input_rims,
        flops=3 * head_flops,
        scalars=1,
        scalar_outs=1,
    )
    pair, other = from_neighbours(pair, other)

    conv_width = 2 * channels
    conv_blocks = call(
        functools.partial(conv_grad_kernel, n_rows),
        "conv_grads",
        [input_four, input_five, pair_in, other_in, grad_four, grad_five],
        [shape((high_group, n_batch * conv_n, conv_width), bf16)] * low_group,
        [
            pltpu.VMEM((channels, crops * (height + 2) * width), bf16),
            pltpu.VMEM((9 * channels, channels), bf16),
            pltpu.VMEM((9 * channels, channels), bf16),
        ]
        + input_rims,
        flops=conv_flops,
    )

    positions, low_positions = crops * height * width, crops * low_height * low_width
    conv_partial = summed_low(conv_blocks)
    pair, other, _ = lax.optimization_barrier((pair, other, conv_partial))
    lat_four, lat_five = call(
        merged_grad_kernel,
        "merged_grads",
        [grad_four, grad_five, pair, other, kernel_four, kernel_five],
        [shape((positions, channels), bf16), shape((low_positions, channels), bf16)],
        [
            pltpu.VMEM((crops, height + 2, width, channels), bf16),
            pltpu.VMEM((crops, low_height + 2, low_width, channels), bf16),
            pltpu.VMEM((4 * width, LANES), f32),
        ]
        + grad_rims,
        flops=conv_flops,
    )
    (conv_sum,) = call(
        total_kernel,
        "conv_total",
        [conv_partial[0], *sent_high(conv_partial)],
        [shape(conv_partial[0].shape, f32)],
        flops=20_000_000_000,
    )

    lateral_n = four_n + five_n + 8
    lateral_kept, *lateral_moved = call(
        functools.partial(section_grad_kernel, n_rows, n_batch, deltas, conv_n),
        "lateral_grads",
        [section_four, section_five, lat_four, lat_five, head_grad, loss],
        [shape((high_group, n_batch * lateral_n, channels), bf16)] * low_group,
        [
            pltpu.VMEM((depth, channels), bf16),
            pltpu.VMEM((low_depth, channels), bf16),
            pltpu.VMEM((DELTA_ROWS, 9 * channels + 2 * LANES), f32),
        ],
        flops=1,
        scalars=1,
    )
    lateral_partial = summed_low([lateral_kept, *lateral_moved])
    lateral_partial, conv_sum = lax.optimization_barrier((lateral_partial, conv_sum))
    lateral_sum = sum((v.astype(f32) for v in sent_high(lateral_partial)), lateral_partial[0])
    conv_shares = shared_batch(conv_sum.reshape(n_batch, conv_n, conv_width))
    conv_shares, lateral_sum = lax.optimization_barrier((conv_shares, lateral_sum))
    first_conv, second_conv, weight_conv = call(
        functools.partial(conv_step_kernel, n_batch - 1),
        "conv_step",
        [*conv_shares, output_conv, mean_conv, square_conv],
        [shape(output_conv.shape, f32)] * 3,
    )
    ends = (n_batch * four_n, n_batch * (four_n + five_n))
    lateral_sum = jnp.concatenate(
        [
            part.reshape(n_batch, -1, channels)
            for part in (
                lateral_sum[: ends[0]],
                lateral_sum[ends[0] : ends[1]],
                lateral_sum[ends[1] :],
            )
        ],
        axis=1,
    )
    turned_head = [v.T for v in (delta_head, mean_head, square_head)]
    outs = call(
        functools.partial(lateral_step_kernel, n_batch - 1),
        "lateral_step",
        [
            *shared_batch(lateral_sum),
            lateral_four,
            mean_four,
            square_four,
            lateral_five,
            mean_five,
            square_five,
            *turned_head,
        ],
        [shape(lateral_four.shape, f32)] * 3
        + [shape(lateral_five.shape, f32)] * 3
        + [shape(turned_head[0].shape, f32)] * 3
        + [shape((1, 1), f32)],
        scalar_outs=1,
    )
    first_four, second_four, weight_four, first_five, second_five, weight_five = outs[:6]
    first_head, second_head, weight_head = (v.T for v in outs[6:9])
    loss_sum = outs[9]
    return (
        loss_sum[0, 0],
        count[0, 0],
        first_four,
        first_five,
        first_conv,
        first_head,
        second_four,
        second_five,
        second_conv,
        second_head,
        weight_four,
        weight_five,
        weight_conv,
        weight_head,
    )


def solution(mesh):
    split = P("batch", "rows", None, None)
    whole, pair = P(("rows", "batch"), None), P(None, ("rows", "batch"), None)
    weights = (whole, whole, pair, whole)
    return jax.shard_map(
        on_device,
        mesh=mesh,
        in_specs=(split,) * 8 + weights * 3,
        out_specs=(P(), P()) + weights * 3,
        check_vma=False,
    )
```

```python
import functools
import math

import jax
import jax.numpy as jnp
from jax import lax
from jax.experimental import pallas as pl
from jax.experimental.pallas import tpu as pltpu
from jax.sharding import PartitionSpec as P

STEP = 5

LANES = 128
DELTA_ROWS = 16
SPARE_BYTES = 8 * 1024 * 1024
ALL_BYTES = 60 * 1024 * 1024

box_beta = 1.0 / 9.0
beta_one = 0.5
beta_two = 0.5
learn_rate = 0.02
weight_decay = 0.01
epsilon = 1e-08

bf16 = jnp.bfloat16
f32 = jnp.float32


def adamw_update(weight, gradient, mean, square):
    first = beta_one * mean + (1.0 - beta_one) * gradient
    second = beta_two * square + (1.0 - beta_two) * gradient * gradient
    corrected_first = first / (1.0 - beta_one**STEP)
    corrected_second = second / (1.0 - beta_two**STEP)
    return (
        first,
        second,
        weight
        - learn_rate
        * (corrected_first / (jnp.sqrt(corrected_second) + epsilon) + weight_decay * weight),
    )


def sent(value, axis, mask):
    count = lax.axis_size(axis)
    return lax.ppermute(value, axis, [(i, i ^ mask) for i in range(count)])


def gathered_batch(piece):
    count, me = lax.axis_size("batch"), lax.axis_index("batch")
    stacked = jnp.stack([piece] + [sent(piece, "batch", k) for k in range(1, count)])
    return [lax.dynamic_index_in_dim(stacked, t ^ me, 0, keepdims=False) for t in range(count)]


def row_groups():
    count = lax.axis_size("rows")
    low = max(count // 4, 1)
    return count, low, count // low


def gathered_high(piece):
    _, low, high = row_groups()
    return [piece] + [sent(piece, "rows", j * low) for j in range(1, high)]


def gathered_low(held):
    _, low, _ = row_groups()
    result = [None] * (low * len(held))
    for j in range(len(held)):
        result[j * low] = held[j]
        for k in range(1, low):
            result[j * low + k] = sent(held[j], "rows", k)
    return result


def summed_low(blocks):
    _, low, high = row_groups()
    came = []
    for k in range(1, low):
        whole = isinstance(blocks[k], jax.Array)
        came.append(
            sent(blocks[k], "rows", k) if whole else [sent(block, "rows", k) for block in blocks[k]]
        )
    return [
        sum((c[j].astype(f32) for c in came), blocks[0][j].astype(f32)) for j in range(high)
    ]


def sent_high(partial):
    _, low, high = row_groups()
    return [sent(partial[j].astype(bf16), "rows", j * low) for j in range(1, high)]


def shared_batch(blocks):
    count, me = lax.axis_size("batch"), lax.axis_index("batch")
    own = lax.dynamic_index_in_dim(blocks, me, 0, keepdims=False)
    came = []
    for k in range(1, count):
        block = lax.dynamic_index_in_dim(blocks, me ^ k, 0, keepdims=False).astype(bf16)
        came.append(sent(block, "batch", k))
    return [own, *came]


def from_neighbours(pair, other):
    count = lax.axis_size("rows")
    links = [(i, i + 1) for i in range(1, count - 1, 2)]
    return sent(pair, "rows", 1), lax.ppermute(other, "rows", links + [(j, i) for i, j in links])


def call(kernel, name, args, outs, scratch=(), flops=0, scalars=0, scalar_outs=0, apart=0):
    vmem, smem = pl.BlockSpec(memory_space=pltpu.VMEM), pl.BlockSpec(memory_space=pltpu.SMEM)
    hbm = pl.BlockSpec(memory_space=pltpu.HBM)
    size = sum(a.size * a.dtype.itemsize for a in (*args, *outs))
    held = sum(
        math.prod(ref.shape) * jnp.dtype(ref.dtype).itemsize
        for ref in scratch
        if ref.memory_space == pltpu.VMEM
    )
    return pl.pallas_call(
        kernel,
        out_shape=list(outs),
        in_specs=[hbm] * apart + [vmem] * (len(args) - scalars - apart) + [smem] * scalars,
        out_specs=[vmem] * (len(outs) - scalar_outs) + [smem] * scalar_outs,
        scratch_shapes=list(scratch),
        compiler_params=pltpu.CompilerParams(vmem_limit_bytes=ALL_BYTES if apart else held + SPARE_BYTES),
        cost_estimate=pl.CostEstimate(flops=flops, bytes_accessed=size, transcendentals=0),
        name=name,
    )(*args)


def swapped(upper, lower, pair, other, outward):
    odd = lax.axis_index("rows") % 2 == 1

    def move(one, two):
        for ref, side in ((one, pair), (two, other)):
            if outward:
                side[...] = ref[...]
            else:
                ref[...] = side[...]

    pl.when(odd)(lambda: move(upper, lower))
    pl.when(jnp.logical_not(odd))(lambda: move(lower, upper))


def dot(left, right, dims=((1,), (0,))):
    return lax.dot_general(left, right, (dims, ((), ())), preferred_element_type=f32)


def turned(value, step, axis, width):
    size = value.shape[axis]
    column = lax.broadcasted_iota(jnp.int32, value.shape, axis) % width
    rolled = pltpu.roll(value, step % size, axis)
    return jnp.where(column == (0 if step == 1 else width - 1), 0.0, rolled)


def doubled_columns(ref, row):
    count = row.shape[0]
    for h in range(ref.shape[0]):
        part = row[:, h * LANES : (h + 1) * LANES]
        ref[h, pl.ds(0, count, stride=2), :] = part
        ref[h, pl.ds(1, count, stride=2), :] = part
    return jnp.concatenate([ref[h] for h in range(ref.shape[0])], axis=1)


def pieces_of(value):
    high = value.astype(bf16).astype(f32)
    middle = (value - high).astype(bf16).astype(f32)
    return high, middle, value - high - middle


def pack_kernel(*refs):
    sources, packed, square, held, arrived = refs[:6], refs[6], refs[7], refs[8:14], refs[14]
    copies = [
        pltpu.make_async_copy(source, target, arrived.at[k])
        for k, (source, target) in enumerate(zip(sources, held))
    ]
    for copy in copies:
        copy.start()
    for copy in copies:
        copy.wait()
    four, five, head, anchor_four, anchor_five, anchor_six = held
    lines = four.shape[0] + five.shape[0]
    packed[: four.shape[0]] = four[...].astype(bf16)
    packed[four.shape[0] : lines] = five[...].astype(bf16)
    total = jnp.zeros((1, 1), f32)
    for anchor in (anchor_four, anchor_five, anchor_six):
        total = total + jnp.sum(anchor[...].astype(f32), keepdims=True).reshape(1, 1)
    square[...] = jnp.zeros_like(square)
    square[: head.shape[0], : head.shape[1]] = head[...]
    spare = square[...]
    line = lax.broadcasted_iota(jnp.int32, spare.shape, 0)
    lane = lax.broadcasted_iota(jnp.int32, spare.shape, 1)
    for k, piece in enumerate(pieces_of(jnp.broadcast_to(total, spare.shape))):
        spare = jnp.where((line == head.shape[0]) & (lane == k), piece, spare)
    packed[lines:] = joined(spare).astype(bf16)


def joined(square):
    return jnp.concatenate([square[:8], square[8:]], axis=1)


def parted(lines):
    return jnp.concatenate([lines[:, :LANES], lines[:, LANES:]], axis=0)


def head_weights_kernel(n_rows, n_batch, deltas, own, *refs):
    pieces, (head, count, flat) = refs[:n_rows], refs[n_rows:]
    channels = head.shape[1]
    me = lax.axis_index("rows")
    flat[...] = jnp.zeros_like(flat)
    line = lax.broadcasted_iota(jnp.int32, (DELTA_ROWS, LANES), 0)
    total = jnp.zeros((DELTA_ROWS, LANES), f32)
    for k in range(n_rows):
        lines = pieces[k][pieces[k].shape[0] - 8 * n_batch :].astype(f32)
        for z in range(n_batch):
            square = parted(lines[8 * z : 8 * z + 8])
            total = total + jnp.where(line >= deltas, square, 0.0)
            square = jnp.where(line < deltas, square, 0.0)
            place = ((me ^ k) * n_batch + z) * own
            wide = jnp.concatenate([square, jnp.zeros_like(square)], axis=1)
            wide = pltpu.roll(wide, place % LANES, 1)
            at = pl.ds(pl.multiple_of(place // LANES * LANES, LANES), 2 * LANES)
            flat[:, at] += wide
    for t in range(9):
        block = flat[:, t * channels : (t + 1) * channels].astype(bf16)
        head[t * DELTA_ROWS : (t + 1) * DELTA_ROWS, :] = block
    count[0, 0] = jnp.sum(total)


def planes_kernel(*refs):
    targets, anchors, (target, mask) = refs[:3], refs[3:6], refs[-2:]
    crops, deltas = targets[0].shape[:2]
    own = 0
    target[:, deltas:, :] = jnp.zeros((crops, target.shape[1] - deltas, target.shape[2]), f32)
    mask[:, deltas:, :] = jnp.zeros((crops, mask.shape[1] - deltas, mask.shape[2]), f32)
    for target_ref, anchor_ref in zip(targets, anchors):
        _, count, lines, width = anchor_ref.shape
        share = deltas // count
        for b in range(crops):
            for r in range(lines):
                at, rest = own + r * LANES, LANES - width
                target[b, :deltas, at : at + width] = target_ref[b, :, r, :]
                if rest:
                    target[b, :deltas, at + width : at + LANES] = jnp.zeros((deltas, rest), f32)
                    mask[b, :deltas, at + width : at + LANES] = jnp.zeros((deltas, rest), f32)
                for a in range(count):
                    row = anchor_ref[b, a, r : r + 1, :].astype(f32)
                    mask[b, a * share : (a + 1) * share, at : at + width] = jnp.broadcast_to(
                        row, (share, width)
                    )
        own += lines * LANES


def lateral_kernel(n_rows, four, five, *refs):
    pieces, rest = refs[:n_rows], refs[n_rows:]
    input_four, input_five, pair, other, kernel_four, kernel_five, wide, first, last = rest[1:]
    mask = rest[0]
    crops, height, width, depth = four.shape
    low_height, low_width = five.shape[1:3]
    me = lax.axis_index("rows")
    part_four, part_five = depth // n_rows, five.shape[3] // n_rows
    for k in range(n_rows):
        owner = me ^ k
        at_four = pl.multiple_of(owner * part_four, part_four)
        at_five = pl.multiple_of(owner * part_five, part_five)
        kernel_four[pl.ds(at_four, part_four), :] = pieces[k][:part_four]
        kernel_five[pl.ds(at_five, part_five), :] = pieces[k][part_four : part_four + part_five]
    for b in range(crops):
        low = dot(five[b].reshape(low_height * low_width, -1), kernel_five[...])
        low_rounded = low.astype(bf16).reshape(low_height, low_width, -1)
        input_five[b] = low_rounded
        first[b, width : width + low_width] = low_rounded[0]
        last[b, width : width + low_width] = low_rounded[low_height - 1]
        for q in range(low_height):
            up = doubled_columns(wide, low[q * low_width : (q + 1) * low_width])
            rows = four[b, 2 * q : 2 * q + 2].reshape(2 * width, depth)
            merged = dot(rows, kernel_four[...]).reshape(2, width, -1) + up[None]
            rounded = merged.astype(bf16)
            input_four[b, 2 * q : 2 * q + 2] = rounded
            if q == 0:
                first[b, :width] = rounded[0]
            if q == low_height - 1:
                last[b, :width] = rounded[1]
        edge, half = width + low_width, width // 2
        lane = lax.broadcasted_iota(jnp.int32, (DELTA_ROWS, width), 1)
        plan = level_rows(height, 1)
        for ref, end in ((first, 0), (last, 1)):
            lines = []
            for _, own, count in plan:
                at = (own + (count - 1) * end) * width
                lines.append(mask[b, :, at : at + width])
            small = jnp.where(lane < half, lines[1], pltpu.roll(lines[2], half, 1))
            ref[b, edge:, :width] = lines[0].astype(bf16)
            ref[b, edge:, width:] = small.astype(bf16)
    swapped(first, last, pair, other, True)


def three_taps(source, b, start, rows, weights, step):
    width, channels = source.shape[2:]
    parts = []
    for j in range(3):
        taps = range(3) if step == 1 else (2, 1, 0)
        left = jnp.concatenate(
            [
                source[b, start + i : start + i + rows].reshape(rows * width, channels)
                for i in range(3)
            ],
            axis=1,
        )
        blocks = [weights[(3 * i + j) * channels : (3 * i + j + 1) * channels] for i in taps]
        if step == 1:
            parts.append(dot(left, jnp.concatenate(blocks, axis=0)))
        else:
            parts.append(dot(left, jnp.concatenate(blocks, axis=1), ((1,), (1,))))
    return parts[1] + turned(parts[0], step, 0, width) + turned(parts[2], -step, 0, width)


def fill_padded(padded, own, above, below, start):
    height, width = own.shape[1:3]
    for b in range(own.shape[0]):
        padded[b, 0] = above[b, start : start + width]
        padded[b, 1 : height + 1] = own[b]
        padded[b, height + 1] = below[b, start : start + width]


def output_kernel(n_rows, deltas, input_four, input_five, pair_in, other_in, head, target, mask, *refs):
    pieces, rest = refs[:n_rows], refs[n_rows:]
    levels, values, pair, other, kernel_four, kernel_five = rest[:6]
    spread_four, spread_five, spare, above, below, first, last = rest[6:]
    swapped(above, below, pair_in, other_in, False)
    crops, height, width, channels = input_four.shape
    low_height, low_width = input_five.shape[1:3]
    me = lax.axis_index("rows")
    part = 9 * channels // n_rows
    for k in range(n_rows):
        at = pl.multiple_of((me ^ k) * part, part)
        kernel_four[pl.ds(at, part), :] = pieces[k][:, :channels]
        kernel_five[pl.ds(at, part), :] = pieces[k][:, channels:]
    fill_padded(spread_four, input_four, above, below, 0)
    fill_padded(spread_five, input_five, above, below, width)
    low_start, top_start = height, height + low_height
    half = width // 2
    levels[:, low_start:, half:, :] = jnp.zeros(
        (crops, levels.shape[1] - low_start, width - half, channels), bf16
    )
    quarter = low_width // 2
    levels[:, top_start:, quarter:, :] = jnp.zeros(
        (crops, levels.shape[1] - top_start, width - quarter, channels), bf16
    )
    rows = 4
    for b in range(crops):
        low = three_taps(spread_five, b, 0, low_height, kernel_five, 1)
        low_rounded = low.astype(bf16).reshape(low_height, low_width, channels)
        levels[b, low_start:top_start, :low_width, :] = low_rounded
        for h in range(0, channels, LANES):
            spare[: low_height * low_width, :] = low[:, h : h + LANES]
            for q in range(low_height // 2):
                total = jnp.zeros((quarter, LANES), f32)
                for at in (2 * q * low_width, (2 * q + 1) * low_width):
                    for side in range(2):
                        total = total + spare[pl.ds(at + side, quarter, stride=2), :]
                pooled = (0.25 * total).astype(bf16)
                levels[b, top_start + q, :quarter, h : h + LANES] = pooled
        for r in range(0, height, rows):
            sums = three_taps(spread_four, b, r, rows, kernel_four, 1)
            rounded = sums.astype(bf16).reshape(rows, width, channels)
            levels[b, r : r + rows] = rounded
        lines_all = levels.shape[1]
        products = dot(
            head[...], levels[b].reshape(lines_all * width, channels), ((1,), (1,))
        )
        none = jnp.zeros((products.shape[0], 2 * width), f32)
        columns = []
        for j in range(3):
            pieces = []
            for _, own, count_lines in level_rows(height, 1):
                padded = jnp.concatenate(
                    [none, products[:, own * width : (own + count_lines) * width], none], axis=1
                )
                total = jnp.zeros((DELTA_ROWS, (count_lines + 2) * width), f32)
                for i in range(3):
                    tap = (3 * i + j) * DELTA_ROWS
                    at = slice(i * width, (i + count_lines + 2) * width)
                    total = total + padded[tap : tap + DELTA_ROWS, at]
                pieces.append(total)
            columns.append(jnp.concatenate(pieces, axis=1))
        sums = columns[1] + turned(columns[0], 1, 1, width) + turned(columns[2], -1, 1, width)
        for index, (padded, own, count_lines) in enumerate(level_rows(height, 1)):
            own_at = slice(own * width, (own + count_lines) * width)
            start, end = padded * width, (padded + count_lines + 2) * width
            partial = sums[:, start + width : end - width] - target[b, :, own_at]
            values[b, :, start : start + width] = sums[:, start : start + width]
            values[b, :, start + width : end - width] = partial
            values[b, :, end - width : end] = sums[:, end - width : end]
            upper = (partial[:, :width], sums[:, start : start + width])
            lower = (partial[:, (count_lines - 1) * width :], sums[:, end - width : end])
            for out, values_of in ((first, upper), (last, lower)):
                for kind, line in enumerate(values_of):
                    lines, line = slice(kind * deltas, (kind + 1) * deltas), line[:deltas]
                    if index < 2:
                        out[b, lines, index * width : (index + 1) * width] = line
                    else:
                        moved = pltpu.roll(line, half, 1)
                        lane = lax.broadcasted_iota(jnp.int32, line.shape, 1)
                        mixed = jnp.where(lane < half, out[b, lines, width : 2 * width], moved)
                        out[b, lines, width : 2 * width] = mixed
    swapped(first, last, pair, other, True)


def level_rows(height, rim):
    result, padded, own = [], 0, 0
    for count in (height, height // 2, height // 4):
        result.append((padded, own, count))
        padded, own = padded + count + 2 * rim, own + count
    return result


def head_kernel(height, deltas, levels, pair_in, other_in, pair_mask, other_mask, head, values, mask, count, *refs):
    head_grad, grad_four, grad_five, pair, other, loss = refs[:6]
    taps, wide, above, below, first, last, mask_above, mask_below = refs[6:]
    swapped(above, below, pair_in, other_in, False)
    swapped(mask_above, mask_below, pair_mask, other_mask, False)
    edge = first.shape[1]
    crops, _, width, channels = levels.shape
    inverse = 1.0 / jnp.maximum(count[0, 0], 1.0)
    plan = level_rows(height, 1)
    summed = jnp.zeros((DELTA_ROWS, LANES), f32)
    total_grad = jnp.zeros((9 * DELTA_ROWS, channels), f32)
    low_height, low_width = height // 2, width // 2
    def small_level(line, index):
        if index == 2:
            line = pltpu.roll(line, width // 2, 1)
        lane = lax.broadcasted_iota(jnp.int32, line.shape, 1)
        return jnp.where(lane < width >> index, line, 0.0)

    def came(ref, b, kind, index):
        at = slice(0, width) if index == 0 else slice(width, 2 * width)
        line = ref[b, kind * deltas : (kind + 1) * deltas, at]
        line = jnp.concatenate([line, jnp.zeros((DELTA_ROWS - deltas, width), f32)], axis=0)
        return small_level(line, index)

    def mask_line(ref, b, index):
        at = slice(0, width) if index == 0 else slice(width, 2 * width)
        return small_level(ref[b, edge:, at].astype(f32), index)

    for b in range(crops):
        partial, weights = [], []
        for index, (padded, own, lines) in enumerate(plan):
            rows = [
                values[b, :, line * width : (line + 1) * width]
                for line in range(padded, padded + lines + 2)
            ]
            rows[0] = rows[0] + came(above, b, 0, index)
            rows[1] = rows[1] + came(above, b, 1, index)
            rows[lines] = rows[lines] + came(below, b, 1, index)
            rows[lines + 1] = rows[lines + 1] + came(below, b, 0, index)
            partial += rows
            weights += [
                mask_line(mask_above, b, index),
                mask[b, :, own * width : (own + lines) * width],
                mask_line(mask_below, b, index),
            ]
        mismatch = jnp.concatenate(partial, axis=1)
        weight = jnp.concatenate(weights, axis=1)
        magnitude = jnp.abs(mismatch)
        ratio = mismatch * (1.0 / box_beta)
        losses = weight * jnp.where(
            magnitude < box_beta, 0.5 * mismatch * ratio, magnitude - 0.5 * box_beta
        )
        for padded, own, lines in plan:
            for line in range(padded + 1, padded + 1 + lines):
                summed = summed + losses[:, line * width : (line + 1) * width]
        middle = weight * jnp.clip(ratio, -1.0, 1.0) * inverse
        middle = middle.astype(bf16).astype(f32)
        shifted = [turned(middle, -1, 1, width), middle, turned(middle, 1, 1, width)]
        shifted = [value.astype(bf16) for value in shifted]
        for i in range(3):
            for j in range(3):
                for padded, own, lines in plan:
                    at = (padded + 2 - i) * width
                    taps[
                        (3 * i + j) * DELTA_ROWS : (3 * i + j + 1) * DELTA_ROWS,
                        own * width : (own + lines) * width,
                    ] = shifted[j][:, at : at + lines * width]
        around = taps[...]
        lines_all = levels.shape[1]
        total_grad = total_grad + dot(around, levels[b].reshape(lines_all * width, channels))
        back = dot(around, head[...], ((0,), (0,))).reshape(lines_all, width, channels)
        rounded = back[:height].astype(bf16)
        grad_four[b] = rounded
        first[b, :width] = rounded[0]
        last[b, :width] = rounded[height - 1]
        for q in range(low_height // 2):
            up = doubled_columns(wide, back[height + low_height + q, : low_width // 2])
            for row in (2 * q, 2 * q + 1):
                low = (back[height + row, :low_width] + 0.25 * up).astype(bf16)
                grad_five[b, row] = low
                if row == 0:
                    first[b, width:] = low
                if row == low_height - 1:
                    last[b, width:] = low
    swapped(first, last, pair, other, True)
    head_grad[...] = total_grad
    loss[0, 0] = jnp.sum(summed)


def conv_grad_kernel(n_rows, input_four, input_five, pair_in, other_in, grad_four, grad_five, *refs):
    outs, (turned_rows, sums_four, sums_five, above, below) = refs[:-5], refs[-5:]
    swapped(above, below, pair_in, other_in, False)
    crops, height, width, channels = input_four.shape
    low_height, low_width = input_five.shape[1:3]
    for own, grad, edge, sums in (
        (input_four, grad_four, 0, sums_four),
        (input_five, grad_five, width, sums_five),
    ):
        lines, extent = own.shape[1:3]
        beside = width // extent
        starts = range(0, crops, beside)

        def padded_row(b, r):
            if r == 0:
                return above[b, edge : edge + extent]
            if r == lines + 1:
                return below[b, edge : edge + extent]
            return own[b, r - 1]

        for g, start in enumerate(starts):
            for r in range(lines + 2):
                row = [padded_row(b, r) for b in range(start, start + beside)]
                at = (g * (lines + 2) + r) * width
                turned_rows[:, at : at + width] = jnp.concatenate(row, axis=0).T
        middle = jnp.concatenate(
            [
                grad[b, r]
                for start in starts
                for r in range(lines)
                for b in range(start, start + beside)
            ],
            axis=0,
        )
        wide = middle.astype(f32)
        right = jnp.concatenate(
            [
                turned(wide, -1, 0, extent).astype(bf16),
                middle,
                turned(wide, 1, 0, extent).astype(bf16),
            ],
            axis=1,
        )
        for i in range(3):
            left = []
            for g in range(len(starts)):
                at = (g * (lines + 2) + i) * width
                left.append(turned_rows[:, at : at + lines * width])
            product = dot(jnp.concatenate(left, axis=1), right).astype(bf16)
            for j in range(3):
                at = slice((3 * i + j) * channels, (3 * i + j + 1) * channels)
                sums[at, :] = product[:, j * channels : (j + 1) * channels]
    me = lax.axis_index("rows")
    part = 9 * channels // n_rows
    low = len(outs)
    for index in range(n_rows):
        at = pl.ds(pl.multiple_of((index ^ me) * part, part), part)
        out, j = outs[index % low], index // low
        out[j, :, :channels] = sums_four[at, :]
        out[j, :, channels:] = sums_five[at, :]


def merged_grad_kernel(grad_four, grad_five, pair_in, other_in, kernel_four, kernel_five, *refs):
    lat_four, lat_five, spread_four, spread_five, fold, above, below = refs
    swapped(above, below, pair_in, other_in, False)
    crops, height, width, channels = grad_four.shape
    low_height, low_width = grad_five.shape[1:3]
    fill_padded(spread_four, grad_four, above, below, 0)
    fill_padded(spread_five, grad_five, above, below, width)
    rows = 4
    for b in range(crops):
        low = three_taps(spread_five, b, 0, low_height, kernel_five, -1)
        low = low.reshape(low_height, low_width, channels)
        for r in range(0, height, rows):
            back = three_taps(spread_four, b, r, rows, kernel_four, -1)
            at = (b * height + r) * width
            lat_four[at : at + rows * width, :] = back.astype(bf16)
            for h in range(0, channels, LANES):
                fold[...] = back[:, h : h + LANES]
                for q in range(rows // 2):
                    total = low[r // 2 + q, :, h : h + LANES]
                    folded = jnp.zeros_like(total)
                    for line in (2 * q * width, (2 * q + 1) * width):
                        for side in range(2):
                            folded = folded + fold[pl.ds(line + side, low_width, stride=2), :]
                    at_low = (b * low_height + r // 2 + q) * low_width
                    lat_five[at_low : at_low + low_width, h : h + LANES] = (total + folded).astype(bf16)


def section_grad_kernel(n_rows, n_batch, deltas, own, four, five, lat_four, lat_five, head_grad, loss, kept, *refs):
    outs, (sums_four, sums_five, flat) = refs[:-3], refs[-3:]
    crops, height, width, depth = four.shape
    low_height, low_width, low_depth = five.shape[1:]
    me = lax.axis_index("rows")
    part_four, part_five = depth // n_rows, low_depth // n_rows
    positions = crops * height * width
    low_positions = crops * low_height * low_width
    turned_four = lat_four[...].T
    turned_five = lat_five[...].T
    step = 256
    for at in range(0, depth, step):
        block = four[:, :, :, at : at + step].reshape(positions, step)
        sums_four[at : at + step, :] = dot(turned_four, block).astype(bf16).T
    for at in range(0, low_depth, step):
        block = five[:, :, :, at : at + step].reshape(low_positions, step)
        sums_five[at : at + step, :] = dot(turned_five, block).astype(bf16).T
    channels = head_grad.shape[1]
    flat[:, 9 * channels :] = jnp.zeros((DELTA_ROWS, flat.shape[1] - 9 * channels), f32)
    for t in range(9):
        flat[:, t * channels : (t + 1) * channels] = head_grad[
            t * DELTA_ROWS : (t + 1) * DELTA_ROWS, :
        ]
    line = lax.broadcasted_iota(jnp.int32, (DELTA_ROWS, LANES), 0)
    lane = lax.broadcasted_iota(jnp.int32, (DELTA_ROWS, LANES), 1)
    spot = (line - deltas) * LANES + lane - 3 * (me * n_batch + lax.axis_index("batch"))
    place = jnp.zeros((DELTA_ROWS, LANES), f32)
    for piece, value in enumerate(pieces_of(jnp.full(place.shape, loss[0, 0], f32))):
        place = jnp.where((line >= deltas) & (spot == piece), value, place)
    high = kept.shape[0]
    low = n_rows // high
    for index in range(n_rows):
        k, j = index % low, index // low
        out = kept.at[j] if k == 0 else outs[k - 1].at[j]
        owner = index ^ me
        at = pl.ds(pl.multiple_of(owner * part_four, part_four), part_four)
        out[:part_four, :] = sums_four[at, :]
        at = pl.ds(pl.multiple_of(owner * part_five, part_five), part_five)
        out[part_four : part_four + part_five, :] = sums_five[at, :]
        pieces = []
        for z in range(n_batch):
            start = (owner * n_batch + z) * own
            at = pl.ds(pl.multiple_of(start // LANES * LANES, LANES), 2 * LANES)
            square = pltpu.roll(flat[:, at], (2 * LANES - start % LANES) % (2 * LANES), 1)[:, :LANES]
            square = jnp.where((line < deltas) & (lane < own), square, place)
            pieces.append(joined(square))
        out[part_four + part_five :, :] = jnp.concatenate(pieces, axis=0).astype(bf16)


def total_kernel(own, *refs):
    total = own[...]
    for piece in refs[:-1]:
        total = total + piece[...].astype(f32)
    refs[-1][...] = total


def adamw_into(outs, weight, gradient, mean, square):
    for out, value in zip(outs, adamw_update(weight, gradient, mean, square)):
        out[...] = value


def conv_step_kernel(count, own, *refs):
    came, (weight, mean, square, first, second, new) = refs[:count], refs[count:]
    channels = weight.shape[2]
    total = own[...]
    for piece in came:
        total = total + piece[...].astype(f32)
    for k in range(2):
        adamw_into(
            (first.at[k], second.at[k], new.at[k]),
            weight[k],
            total[:, k * channels : (k + 1) * channels],
            mean[k],
            square[k],
        )


def lateral_step_kernel(count, own, *refs):
    came, inputs, outs, loss = refs[:count], refs[count : count + 9], refs[count + 9 : -1], refs[-1]
    total = own[...]
    for piece in came:
        total = total + piece[...].astype(f32)
    lines = inputs[0].shape[0]
    deltas, rows = inputs[6].shape
    square = parted(total[total.shape[0] - 8 :])
    gradients = (total[:lines], total[lines : total.shape[0] - 8], square[:deltas, :rows])
    for k, gradient in enumerate(gradients):
        weight, mean, second = (ref[...] for ref in inputs[3 * k : 3 * k + 3])
        adamw_into(outs[3 * k : 3 * k + 3], weight, gradient, mean, second)
    line = lax.broadcasted_iota(jnp.int32, square.shape, 0)
    loss[0, 0] = jnp.sum(jnp.where(line >= deltas, square, 0.0))


def on_device(
    section_four,
    section_five,
    target_four,
    target_five,
    target_six,
    anchor_four,
    anchor_five,
    anchor_six,
    lateral_four,
    lateral_five,
    output_conv,
    delta_head,
    mean_four,
    mean_five,
    mean_conv,
    mean_head,
    square_four,
    square_five,
    square_conv,
    square_head,
):
    n_rows, n_batch = lax.axis_size("rows"), lax.axis_size("batch")
    _, low_group, high_group = row_groups()
    crops, height, width, depth = section_four.shape
    low_height, low_width, low_depth = section_five.shape[1:]
    four_n, five_n, conv_n = lateral_four.shape[0], lateral_five.shape[0], output_conv.shape[1]
    channels, deltas = delta_head.shape[0] * n_rows * n_batch // 9, delta_head.shape[1]
    shape = jax.ShapeDtypeStruct

    flat = [jnp.transpose(a, (0, 3, 1, 2)) for a in (anchor_four, anchor_five, anchor_six)]
    sources = [lateral_four, lateral_five, delta_head.T, *flat]
    (lateral,) = call(
        pack_kernel,
        "pack",
        sources,
        [shape((four_n + five_n + 8, channels), bf16)],
        [pltpu.VMEM((DELTA_ROWS, LANES), f32)]
        + [pltpu.VMEM(v.shape, v.dtype) for v in sources]
        + [pltpu.SemaphoreType.DMA((len(sources),))],
        apart=len(sources),
    )
    parts = gathered_batch(lateral)
    lateral = jnp.concatenate(
        [p[:four_n] for p in parts]
        + [p[four_n : four_n + five_n] for p in parts]
        + [p[four_n + five_n :] for p in parts]
    )
    laterals = gathered_high(lateral)

    conv = jnp.concatenate([output_conv[0], output_conv[1]], axis=1).astype(bf16)
    conv = jnp.concatenate(gathered_batch(conv))

    lines = height + low_height + low_height // 2
    flat, _ = lax.optimization_barrier(
        (
            [
                jnp.transpose(t, (0, 3, 1, 2))
                for t in (
                    target_four,
                    target_five,
                    target_six,
                    anchor_four,
                    anchor_five,
                    anchor_six,
                )
            ],
            lateral,
        )
    )
    target, mask = call(
        planes_kernel,
        "planes",
        [*flat, section_four, section_five],
        [shape((crops, DELTA_ROWS, lines * LANES), f32)] * 2,
    )
    laterals, target, mask = lax.optimization_barrier((laterals, target, mask))
    laterals = gathered_low(laterals)
    convs = gathered_high(conv)

    edge = width + low_width
    full_edge = edge + DELTA_ROWS
    input_rims = [pltpu.VMEM((crops, full_edge, channels), bf16)] * 2
    grad_rims = [pltpu.VMEM((crops, edge, channels), bf16)] * 2
    head_rims = [pltpu.VMEM((crops, 2 * deltas, 2 * width), f32)] * 2
    input_four, input_five, pair, other = call(
        functools.partial(lateral_kernel, n_rows),
        "laterals",
        [section_four, section_five, *laterals, mask],
        [
            shape((crops, height, width, channels), bf16),
            shape((crops, low_height, low_width, channels), bf16),
            shape((crops, full_edge, channels), bf16),
            shape((crops, full_edge, channels), bf16),
        ],
        [
            pltpu.VMEM((depth, channels), bf16),
            pltpu.VMEM((low_depth, channels), bf16),
            pltpu.VMEM((channels // LANES, width, LANES), f32),
        ]
        + input_rims,
        flops=2 * crops * channels * (height * width * depth + low_height * low_width * low_depth),
    )
    pair_in, other_in = from_neighbours(pair, other)
    head, count = call(
        functools.partial(head_weights_kernel, n_rows, n_batch, deltas, conv_n),
        "head_weights",
        laterals,
        [shape((9 * DELTA_ROWS, channels), bf16), shape((1, 1), f32)],
        [pltpu.VMEM((DELTA_ROWS, 9 * channels + 2 * LANES), f32)],
        scalar_outs=1,
    )
    pair_in, other_in, head = lax.optimization_barrier((pair_in, other_in, head))
    early = (0, high_group - 1)
    early_convs = [
        lax.optimization_barrier((convs[j], pair_in, other_in))[0] for j in early
    ]
    early_low = gathered_low(early_convs)
    late = [j for j in range(high_group) if j not in early]
    late_convs, early_low = lax.optimization_barrier(([convs[j] for j in late], early_low))
    late_low = gathered_low(late_convs)
    convs = [None] * n_rows
    for group, lows in ((early, early_low), (late, late_low)):
        for i, j in enumerate(group):
            convs[j * low_group : (j + 1) * low_group] = lows[i * low_group : (i + 1) * low_group]

    conv_flops = 18 * crops * channels * channels * (height * width + low_height * low_width)
    levels, values, pair, other, kernel_four, kernel_five = call(
        functools.partial(output_kernel, n_rows, deltas),
        "outputs",
        [input_four, input_five, pair_in, other_in, head, target, mask, *convs],
        [
            shape((crops, lines, width, channels), bf16),
            shape((crops, DELTA_ROWS, (lines + 6) * width), f32),
            shape((crops, 2 * deltas, 2 * width), f32),
            shape((crops, 2 * deltas, 2 * width), f32),
            shape((9 * channels, channels), bf16),
            shape((9 * channels, channels), bf16),
        ],
        [
            pltpu.VMEM((crops, height + 2, width, channels), bf16),
            pltpu.VMEM((crops, low_height + 2, low_width, channels), bf16),
            pltpu.VMEM((low_height * low_width, LANES), f32),
        ]
        + input_rims
        + head_rims,
        flops=conv_flops,
    )
    pair, other = from_neighbours(pair, other)

    head_flops = 18 * DELTA_ROWS * crops * lines * width * channels
    head_grad, grad_four, grad_five, pair, other, loss = call(
        functools.partial(head_kernel, height, deltas),
        "heads",
        [levels, pair, other, pair_in, other_in, head, values, mask, count],
        [
            shape((9 * DELTA_ROWS, channels), f32),
            shape((crops, height, width, channels), bf16),
            shape((crops, low_height, low_width, channels), bf16),
            shape((crops, edge, channels), bf16),
            shape((crops, edge, channels), bf16),
            shape((1, 1), f32),
        ],
        [
            pltpu.VMEM((9 * DELTA_ROWS, lines * width), bf16),
            pltpu.VMEM((channels // LANES, low_width, LANES), f32),
        ]
        + head_rims
        + grad_rims
        + input_rims,
        flops=3 * head_flops,
        scalars=1,
        scalar_outs=1,
    )
    pair, other = from_neighbours(pair, other)

    conv_width = 2 * channels
    conv_blocks = call(
        functools.partial(conv_grad_kernel, n_rows),
        "conv_grads",
        [input_four, input_five, pair_in, other_in, grad_four, grad_five],
        [shape((high_group, n_batch * conv_n, conv_width), bf16)] * low_group,
        [
            pltpu.VMEM((channels, crops * (height + 2) * width), bf16),
            pltpu.VMEM((9 * channels, channels), bf16),
            pltpu.VMEM((9 * channels, channels), bf16),
        ]
        + input_rims,
        flops=conv_flops,
    )

    positions, low_positions = crops * height * width, crops * low_height * low_width
    conv_partial = summed_low(conv_blocks)
    pair, other, _ = lax.optimization_barrier((pair, other, conv_partial))
    lat_four, lat_five = call(
        merged_grad_kernel,
        "merged_grads",
        [grad_four, grad_five, pair, other, kernel_four, kernel_five],
        [shape((positions, channels), bf16), shape((low_positions, channels), bf16)],
        [
            pltpu.VMEM((crops, height + 2, width, channels), bf16),
            pltpu.VMEM((crops, low_height + 2, low_width, channels), bf16),
            pltpu.VMEM((4 * width, LANES), f32),
        ]
        + grad_rims,
        flops=conv_flops,
    )
    (conv_sum,) = call(
        total_kernel,
        "conv_total",
        [conv_partial[0], *sent_high(conv_partial)],
        [shape(conv_partial[0].shape, f32)],
        flops=20_000_000_000,
    )

    lateral_n = four_n + five_n + 8
    lateral_kept, *lateral_moved = call(
        functools.partial(section_grad_kernel, n_rows, n_batch, deltas, conv_n),
        "lateral_grads",
        [section_four, section_five, lat_four, lat_five, head_grad, loss],
        [shape((high_group, n_batch * lateral_n, channels), bf16)] * low_group,
        [
            pltpu.VMEM((depth, channels), bf16),
            pltpu.VMEM((low_depth, channels), bf16),
            pltpu.VMEM((DELTA_ROWS, 9 * channels + 2 * LANES), f32),
        ],
        flops=1,
        scalars=1,
    )
    lateral_partial = summed_low([lateral_kept, *lateral_moved])
    lateral_partial, conv_sum = lax.optimization_barrier((lateral_partial, conv_sum))
    lateral_sum = sum((v.astype(f32) for v in sent_high(lateral_partial)), lateral_partial[0])
    conv_shares = shared_batch(conv_sum.reshape(n_batch, conv_n, conv_width))
    conv_shares, lateral_sum = lax.optimization_barrier((conv_shares, lateral_sum))
    first_conv, second_conv, weight_conv = call(
        functools.partial(conv_step_kernel, n_batch - 1),
        "conv_step",
        [*conv_shares, output_conv, mean_conv, square_conv],
        [shape(output_conv.shape, f32)] * 3,
    )
    ends = (n_batch * four_n, n_batch * (four_n + five_n))
    lateral_sum = jnp.concatenate(
        [
            part.reshape(n_batch, -1, channels)
            for part in (
                lateral_sum[: ends[0]],
                lateral_sum[ends[0] : ends[1]],
                lateral_sum[ends[1] :],
            )
        ],
        axis=1,
    )
    turned_head = [v.T for v in (delta_head, mean_head, square_head)]
    outs = call(
        functools.partial(lateral_step_kernel, n_batch - 1),
        "lateral_step",
        [
            *shared_batch(lateral_sum),
            lateral_four,
            mean_four,
            square_four,
            lateral_five,
            mean_five,
            square_five,
            *turned_head,
        ],
        [shape(lateral_four.shape, f32)] * 3
        + [shape(lateral_five.shape, f32)] * 3
        + [shape(turned_head[0].shape, f32)] * 3
        + [shape((1, 1), f32)],
        scalar_outs=1,
    )
    first_four, second_four, weight_four, first_five, second_five, weight_five = outs[:6]
    first_head, second_head, weight_head = (v.T for v in outs[6:9])
    loss_sum = outs[9]
    return (
        loss_sum[0, 0],
        count[0, 0],
        first_four,
        first_five,
        first_conv,
        first_head,
        second_four,
        second_five,
        second_conv,
        second_head,
        weight_four,
        weight_five,
        weight_conv,
        weight_head,
    )


def solution(mesh):
    split = P("batch", "rows", None, None)
    whole, pair = P(("rows", "batch"), None), P(None, ("rows", "batch"), None)
    weights = (whole, whole, pair, whole)
    return jax.shard_map(
        on_device,
        mesh=mesh,
        in_specs=(split,) * 8 + weights * 3,
        out_specs=(P(), P()) + weights * 3,
        check_vma=False,
    )
```
